128 devices in a mesh: lon: 32 (over y, x, z_lo), lat: 4 (over z_hi, core).
Axes of the slice: x: 4, y: 4, z: 4 (z_hi: 2, z_lo: 2; z = z_hi * 2 + z_lo), core: 2. Of those that a mesh axis runs over, the one named last changes fastest.
Arguments:
- first_features: bfloat16 [32, 8192, 128], P(None, ('lon', 'lat')), may hold values from -6 to 6
- second_features: bfloat16 [32, 8192, 128], P(None, ('lon', 'lat')), may hold values from -6 to 6
- hidden_state: bfloat16 [32, 8192, 128], P('lat', 'lon'), may hold values from -1 to 1
- encoder_weight: bfloat16 [289, 128], replicated, may hold values from -0.375 to 0.375
- gates_weight: bfloat16 [3, 3, 256, 256], replicated, may hold values from -0.125 to 0.125
- candidate_weight: bfloat16 [3, 3, 256, 128], replicated, may hold values from -0.125 to 0.125
- row_metric: float32 [32], replicated, may hold values from 1 to 3
Outputs:
- new_state: bfloat16 [32, 8192, 128], P('lat', 'lon')
The draws below stay inside these ranges and needn't reach their ends.
All inputs are finite; a program needn't handle non-finite values.
Results may differ from the reference program's by a relative error of at most 0.0058.
Values may be sent and summed in bfloat16 or wider, within the bound.
No kernel may reach another device: no remote copies, remote signals or barrier semaphores. Data moves between devices by JAX's collectives and lax.ppermute only.
A program may use at most 64 MiB of HBM per device.

```python
import math
import jax
import jax.numpy as jnp
from jax import lax

FEAT = 128
HID = 128
MOT = 128
RADIUS = 8
WIN = 17
ROWS = 32
WIDTH = 8192


def levels(key, dims, cuts, smallest, high):
    def one(axis_at, blocks):
        steps = jax.random.uniform(jax.random.fold_in(jax.random.fold_in(key, 6), axis_at), (blocks,), jnp.float32, smallest / len(cuts), high / len(cuts))
        return jnp.repeat(jnp.exp(steps), dims[axis_at] // blocks).reshape((-1,) + (1,) * (len(dims) - axis_at - 1))

    factor_of = one(*cuts[0])
    for cut in cuts[1:]:
        factor_of = factor_of * one(*cut)
    return factor_of


def noise(rng, extent, width, limit, shards=(), kind=jnp.bfloat16):
    entries = jax.random.normal(rng, extent, jnp.float32) * width
    if len(shards) > 0:
        entries = levels(rng, extent, shards, -0.22, 0.18) * entries
    return jnp.clip(entries, min=-limit, max=limit).astype(kind)


def setup_inputs(seed: int = 0) -> dict:
    arg_keys = jax.random.split(jax.random.key(seed), 8)
    first_features = noise(arg_keys[0], (ROWS, WIDTH, FEAT), 1.0, 6.0, ((1, 128),))
    second_features = noise(arg_keys[1], (ROWS, WIDTH, FEAT), 1.0, 6.0, ((1, 128),))
    hidden_state = jnp.clip(jax.random.uniform(arg_keys[2], (ROWS, WIDTH, HID), jnp.float32, -1.0, 1.0) * levels(arg_keys[2], (ROWS, WIDTH, HID), ((0, 4), (1, 32)), -0.4, 0.0), -1.0, 1.0).astype(jnp.bfloat16)
    encoder_weight = noise(arg_keys[3], (WIN * WIN, MOT), (WIN * WIN) ** -0.5, 0.375)
    gates_weight = noise(arg_keys[4], (3, 3, HID + MOT, 2 * HID), (9 * (HID + MOT)) ** -0.5, 0.125)
    candidate_weight = noise(arg_keys[5], (3, 3, HID + MOT, HID), (9 * (HID + MOT)) ** -0.5, 0.125)
    row_metric = jnp.clip(jnp.exp(jax.random.uniform(arg_keys[6], (ROWS,), jnp.float32, math.log(1.0), math.log(3.0))), 1.0, 3.0)
    return {"first_features": first_features, "second_features": second_features, "hidden_state": hidden_state, "encoder_weight": encoder_weight, "gates_weight": gates_weight, "candidate_weight": candidate_weight, "row_metric": row_metric}


def correlate_all(first_map, second_map):
    height = first_map.shape[0]
    columns = first_map.shape[1]
    padded = jnp.pad(second_map, ((RADIUS, RADIUS), (0, 0), (0, 0)))
    padded = jnp.concatenate([padded[:, -RADIUS:], padded, padded[:, :RADIUS]], axis=1)

    def one_row(row_index):
        first_row = lax.dynamic_index_in_dim(first_map, row_index, 0, keepdims=False).astype(jnp.float32)
        strip = lax.dynamic_slice_in_dim(padded, row_index, WIN, 0).astype(jnp.float32)
        planes = []
        for shift_x in range(WIN):
            window = strip[:, shift_x:shift_x + columns]
            planes.append(jnp.einsum("wf,awf->wa", first_row, window, precision=lax.Precision.HIGHEST))
        stacked = jnp.stack(planes, axis=-1)
        return stacked.reshape(columns, WIN * WIN) * (FEAT ** -0.5)

    return lax.map(one_row, jnp.arange(height, dtype=jnp.int32))


def metric_conv(source_map, weights, metric):
    height = source_map.shape[0]
    columns = source_map.shape[1]
    padded = jnp.pad(source_map, ((1, 1), (0, 0), (0, 0)))
    padded = jnp.concatenate([padded[:, -1:], padded, padded[:, :1]], axis=1)
    summed = jnp.zeros((height, columns, weights.shape[-1]), jnp.float32)
    for tap_row in range(3):
        for tap_col in range(3):
            window = padded[tap_row:tap_row + height, tap_col:tap_col + columns].reshape(height * columns, -1)
            contribution = jnp.dot(window, weights[tap_row, tap_col], preferred_element_type=jnp.float32)
            contribution = contribution.reshape(height, columns, -1)
            if tap_col != 1:
                contribution = contribution * metric[:, None, None]
            summed = summed + contribution
    return summed


def reference(first_features, second_features, hidden_state, encoder_weight, gates_weight, candidate_weight, row_metric):
    correlation = correlate_all(first_features, second_features).astype(jnp.bfloat16)
    height = correlation.shape[0]
    columns = correlation.shape[1]
    motion = jax.nn.relu(jnp.dot(correlation.reshape(height * columns, -1), encoder_weight, preferred_element_type=jnp.float32))
    motion = motion.astype(jnp.bfloat16).reshape(height, columns, -1)
    joined = jnp.concatenate([hidden_state, motion], axis=-1)
    gate_values = jax.nn.sigmoid(metric_conv(joined, gates_weight, row_metric))
    update_gate = gate_values[..., :HID]
    reset_gate = gate_values[..., HID:]
    state_float = hidden_state.astype(jnp.float32)
    reset_state = (reset_gate * state_float).astype(jnp.bfloat16)
    candidate = jnp.tanh(metric_conv(jnp.concatenate([reset_state, motion], axis=-1), candidate_weight, row_metric))
    return ((1.0 - update_gate) * state_float + update_gate * candidate).astype(jnp.bfloat16)
```

```python
import jax
import jax.numpy as jnp
from jax import lax
from jax.experimental import pallas as pl
from jax.experimental.pallas import tpu as pltpu
from jax.sharding import PartitionSpec as P

RADIUS, WIN = 8, 17
G, S = 16, 5
BF, F32 = jnp.bfloat16, jnp.float32
NT = (((1,), (1,)), ((), ()))
BOTH = ("lon", "lat")
VM = pl.BlockSpec(memory_space=pltpu.VMEM)
SM = pl.BlockSpec(memory_space=pltpu.SMEM)


def widen(encoder_weight):
    w = encoder_weight.reshape(WIN, WIN, -1)[:, ::-1]
    w = jnp.pad(w, ((7, 7), (15, 0), (0, 0)))
    return w.reshape(31 * 32, -1)


def mirror(x):
    n = x.shape[0] // 8
    ids = 7 - lax.broadcasted_iota(jnp.int32, (8, 128), 0)
    tiles = [
        jnp.take_along_axis(x[8 * k : 8 * k + 8], ids, axis=0, mode="promise_in_bounds")
        for k in reversed(range(n))
    ]
    return jnp.concatenate(tiles, axis=0)


def correlate_kernel(t_ref, f_ref, s_ref, left_ref, right_ref, w_ref, o0, o1, o2, o3, fe, se, hal, band, acc):
    rows = f_ref.shape[0]
    blocks = rows // 8
    scale = 128**-0.5
    pad = jnp.zeros((16, 128), F32)
    for n, ref in enumerate((left_ref, right_ref)):
        hal[n, 0:16] = pad
        hal[n, 16:400] = ref[...].astype(F32)
    fpad = jnp.zeros((8, 128), F32)
    for r in range(rows):
        fe[r, 0:8] = fpad
        fe[r, 72:80] = fpad
        fe[r, 8:72] = f_ref[r].astype(F32)
        fe[r, 6:8] = hal[0, 336 + 2 * r : 338 + 2 * r]
        fe[r, 72:74] = hal[1, 336 + 2 * r : 338 + 2 * r]
        se[r, 16:80] = mirror(s_ref[r].astype(F32)).astype(BF)
        se[r, 80:96] = mirror(hal[0, 10 + 10 * r : 26 + 10 * r]).astype(BF)
        se[r, 0:16] = mirror(hal[1, 16 + 10 * r : 32 + 10 * r]).astype(BF)
    for g in range(S):
        for b in range(blocks):
            lo, hi = max(0, 8 * b - 8), min(rows, 8 * b + 16)
            keys = se[8 * b : 8 * b + 8, 64 - G * g : 96 - G * g, :].reshape(256, 128)
            query = fe[lo:hi, G * g : G * g + G, :].reshape((hi - lo) * G, 128).astype(BF)
            c = lax.dot_general(query, keys, NT, preferred_element_type=F32)
            c = (c * scale).reshape(hi - lo, G, 256)
            for h in range(2):
                part = pltpu.roll(c[:, :, 128 * h : 128 * h + 128], 0, 2, stride=1, stride_axis=1)
                band[b, lo - 8 * b + 8 : hi - 8 * b + 8, G * g : G * g + G, 128 * h : 128 * h + 128] = part.astype(BF)
    done = set()
    for d in range(-8, 16):
        bs = [b for b in range(blocks) if 0 <= 8 * b + d < rows]
        b0, b1 = bs[0], bs[-1] + 1
        lhs = band[b0:b1, d + 8].reshape((b1 - b0) * S * G, 256)
        o = 15 - d
        part = jnp.dot(lhs, w_ref[32 * o : 32 * o + 256, :], preferred_element_type=F32)
        part = part.reshape(b1 - b0, S * G, 128)
        for n, b in enumerate(bs):
            i = 8 * b + d
            if i in done:
                acc[i + 2] += part[n]
            else:
                acc[i + 2] = part[n]
                done.add(i)
    zero = jnp.zeros((2, S * G, 128), F32)
    acc[0:2] = zero
    acc[rows + 2 : rows + 4] = zero
    t = t_ref[0]
    for k, out in enumerate((o0, o1, o2, o3)):
        base = 8 * (t ^ k)
        edges = []
        for r in range(12):
            m = jnp.maximum(acc[base + r], 0.0)
            out[64 * r : 64 * r + 64, :] = m[8:72].astype(BF)
            edges.append(jnp.where(t == 0, m[6:8], m[72:74]))
        edges.append(jnp.zeros((8, 128), F32))
        out[768:800, :] = jnp.concatenate(edges, axis=0).astype(BF)


def correlate(t, f, s, left, right, w_wide):
    piece = jax.ShapeDtypeStruct((800, 128), BF)
    return pl.pallas_call(
        correlate_kernel,
        out_shape=(piece,) * 4,
        in_specs=[SM] + [VM] * 5,
        out_specs=(VM,) * 4,
        scratch_shapes=[
            pltpu.VMEM((32, 80, 128), F32),
            pltpu.VMEM((32, 96, 128), BF),
            pltpu.VMEM((2, 400, 128), F32),
            pltpu.VMEM((4, 24, S * G, 256), BF),
            pltpu.VMEM((36, S * G, 128), F32),
        ],
        compiler_params=pltpu.CompilerParams(vmem_limit_bytes=40 << 20),
        name="correlate",
    )(t, f, s, left, right, w_wide)


def gru_kernel(t_ref, metric_ref, h_ref, hl_ref, hr_ref, top_ref, bot_ref, m0, m1, m2, m3, gw_ref, cw_ref, out_ref, hf, mf, x, m3s, rf, r, ug):
    t = t_ref[0]
    for n, ref in ((0, top_ref), (10, bot_ref)):
        for i in range(2):
            hf[n + i, 0:272] = ref[272 * i : 272 * i + 272].astype(F32)
    hl, hr = hl_ref[...].astype(F32), hr_ref[...].astype(F32)
    for i in range(8):
        hf[2 + i, 2:258] = h_ref[i].astype(F32)
        hf[2 + i, 0:2] = hl[2 * i : 2 * i + 2]
        hf[2 + i, 258:260] = hr[2 * i : 2 * i + 2]
    for k, m in enumerate((m0, m1, m2, m3)):
        s = t ^ k
        for i in range(12):
            mf[i, pl.ds(2 + 64 * s, 64)] = m[64 * i : 64 * i + 64].astype(F32)
    for k, m in enumerate((m0, m1, m2, m3)):
        s = t ^ k

        @pl.when((s == 0) | (s == 3))
        def _(m=m, s=s):
            e = m[768:800].astype(F32)
            at = jnp.where(s == 0, 0, 258)
            for i in range(12):
                mf[i, pl.ds(at, 2)] = e[2 * i : 2 * i + 2]

    for q in range(3):
        for i in range(12):
            x[q, i, :, 0:128] = hf[i, q : q + 272].astype(BF)
            x[q, i, :, 128:256] = mf[i, q : q + 272].astype(BF)
    for i in range(12):
        m3s[i] = mf[i, 3:259].astype(BF)
    sides_w = jnp.concatenate([gw_ref[p, q] for q in (0, 2) for p in range(3)], axis=0)
    center_w = jnp.concatenate([gw_ref[p, 1] for p in range(3)], axis=0)
    for i in range(10):
        lhs = jnp.concatenate([x[q, i + p] for q in (0, 2) for p in range(3)], axis=1)
        sides = jnp.dot(lhs, sides_w, preferred_element_type=F32)
        lhs = jnp.concatenate([x[1, i + p] for p in range(3)], axis=1)
        center = jnp.dot(lhs, center_w, preferred_element_type=F32)
        gate = center + sides * metric_ref[8 * t + i]
        gate = 0.5 * jnp.tanh(0.5 * gate) + 0.5
        rf[i, 0:272] = gate[:, 128:] * hf[i + 1, 1:273]
        if 1 <= i < 9:
            ug[i - 1] = gate[:, 0:128]
    for q in range(3):
        for i in range(10):
            r[q, i] = rf[i, q : q + 256].astype(BF)
    zero = jnp.zeros((256, 128), BF)

    def pair(rr, q):
        first = cw_ref[rr, q] if rr < 3 else zero
        second = cw_ref[rr - 1, q] if rr > 0 else zero
        return jnp.concatenate([first, second], axis=1)

    sides_w = jnp.concatenate([pair(rr, q) for q in (0, 2) for rr in range(4)], axis=0)
    center_w = jnp.concatenate([pair(rr, 1) for rr in range(4)], axis=0)

    def taps(q, row):
        mm = m3s[row + 1] if q == 2 else x[q + 1, row + 1, 0:256, 128:256]
        return [r[q, row], mm]

    for i in range(0, 8, 2):
        lhs = jnp.concatenate(sum([taps(q, i + rr) for q in (0, 2) for rr in range(4)], []), axis=1)
        sides = jnp.dot(lhs, sides_w, preferred_element_type=F32)
        lhs = jnp.concatenate(sum([taps(1, i + rr) for rr in range(4)], []), axis=1)
        center = jnp.dot(lhs, center_w, preferred_element_type=F32)
        for n in range(2):
            part = slice(128 * n, 128 * n + 128)
            cand = jnp.tanh(center[:, part] + sides[:, part] * metric_ref[8 * t + i + n + 1])
            u = ug[i + n, 1:257]
            h = hf[i + n + 2, 2:258]
            out_ref[i + n] = ((1.0 - u) * h + u * cand).astype(BF)


def gru(t, metric, h, hl, hr, top, bot, ms, gw, cw):
    return pl.pallas_call(
        gru_kernel,
        out_shape=jax.ShapeDtypeStruct((8, 256, 128), BF),
        in_specs=[SM, SM] + [VM] * 11,
        out_specs=VM,
        scratch_shapes=[
            pltpu.VMEM((12, 280, 128), F32),
            pltpu.VMEM((12, 280, 128), F32),
            pltpu.VMEM((3, 12, 272, 256), BF),
            pltpu.VMEM((12, 256, 128), BF),
            pltpu.VMEM((10, 272, 128), F32),
            pltpu.VMEM((3, 10, 256, 128), BF),
            pltpu.VMEM((8, 272, 128), F32),
        ],
        compiler_params=pltpu.CompilerParams(vmem_limit_bytes=40 << 20),
        name="gru",
    )(t, metric, h, hl, hr, top, bot, *ms, gw, cw)


def body(first, second, hidden, encoder_weight, gates_weight, candidate_weight, row_metric):
    t = lax.axis_index("lat").astype(jnp.int32)[None]
    slabs = lax.axis_size("lon") * lax.axis_size("lat")
    up = [(i, (i + 1) % slabs) for i in range(slabs)]
    down = [((i + 1) % slabs, i) for i in range(slabs)]
    count = lax.axis_size("lon")
    east = [(i, (i + 1) % count) for i in range(count)]
    west = [((i + 1) % count, i) for i in range(count)]

    def rim(s, f):
        return jnp.concatenate([s.reshape(-1, 128), f.reshape(-1, 128)], axis=0)

    left = lax.ppermute(rim(second[:, 54:], first[:, 62:]), BOTH, up)
    right = lax.ppermute(rim(second[:, :10], first[:, :2]), BOTH, down)
    hl = lax.ppermute(hidden[:, 254:].reshape(16, 128), "lon", east)
    hr = lax.ppermute(hidden[:, :2].reshape(16, 128), "lon", west)
    pieces = correlate(t, first, second, left, right, widen(encoder_weight))

    def rows(a):
        wide = jnp.concatenate([hl.reshape(8, 2, 128)[a : a + 2], hidden[a : a + 2], hr.reshape(8, 2, 128)[a : a + 2]], axis=1)
        return jnp.pad(wide, ((0, 0), (0, 12), (0, 0))).reshape(544, 128)

    top = lax.ppermute(rows(6), "lat", [(0, 1), (1, 2), (2, 3)])
    bot = lax.ppermute(rows(0), "lat", [(1, 0), (2, 1), (3, 2)])
    ms = [pieces[0]] + [lax.ppermute(pieces[k], "lat", [(i, i ^ k) for i in range(4)]) for k in (1, 2, 3)]
    metric = jnp.pad(row_metric, (1, 1))
    return gru(t, metric, hidden, hl, hr, top, bot, ms, gates_weight, candidate_weight)


def solution(mesh):
    return jax.shard_map(
        body,
        mesh=mesh,
        in_specs=(
            P(None, BOTH, None),
            P(None, BOTH, None),
            P("lat", "lon", None),
            P(),
            P(),
            P(),
            P(),
        ),
        out_specs=P("lat", "lon", None),
        check_vma=False,
    )
```

```python
import functools

import jax
import jax.numpy as jnp
from jax import lax
from jax.experimental import pallas as pl
from jax.experimental.pallas import tpu as pltpu
from jax.sharding import PartitionSpec as P

RADIUS, WIN = 8, 17
G, S = 16, 5
BF, F32 = jnp.bfloat16, jnp.float32
NT = (((1,), (1,)), ((), ()))
BOTH = ("lon", "lat")
VM = pl.BlockSpec(memory_space=pltpu.VMEM)
SM = pl.BlockSpec(memory_space=pltpu.SMEM)


def widen(encoder_weight):
    w = encoder_weight.reshape(WIN, WIN, -1)[:, ::-1]
    w = jnp.pad(w, ((7, 7), (15, 0), (0, 0)))
    return w.reshape(31 * 32, -1)


def mirror(x):
    n = x.shape[0] // 8
    ids = 7 - lax.broadcasted_iota(jnp.int32, (8, 128), 0)
    tiles = [
        jnp.take_along_axis(x[8 * k : 8 * k + 8], ids, axis=0, mode="promise_in_bounds")
        for k in reversed(range(n))
    ]
    return jnp.concatenate(tiles, axis=0)


def pack_kernel(t_ref, f_ref, s_ref, h_ref, a_ref, b_ref, up, down, sb, fb, hb, sem):
    rows = f_ref.shape[0]
    moves = []
    for n, col in enumerate((48, 0)):
        moves.append((s_ref.at[:, col : col + 16], sb.at[n]))
        moves.append((f_ref.at[:, col : col + 16], fb.at[n]))
        moves.append((h_ref.at[6 - 6 * n : 8 - 6 * n], hb.at[n]))
    copies = [pltpu.make_async_copy(a, b, sem.at[k]) for k, (a, b) in enumerate(moves)]
    for c in copies:
        c.start()
    for c in copies:
        c.wait()
    for r in range(rows):
        up[10 * r : 10 * r + 10] = sb[0, r].astype(F32)[6:16]
        down[10 * r : 10 * r + 10] = sb[1, r].astype(F32)[0:10]
        up[320 + 2 * r : 322 + 2 * r] = fb[0, r].astype(F32)[14:16]
        down[320 + 2 * r : 322 + 2 * r] = fb[1, r].astype(F32)[0:2]
    even = lax.rem(t_ref[0], 2) == 0

    def put(n_ref, p_ref):
        n_ref[0:384] = up[...].astype(BF)
        p_ref[0:384] = down[...].astype(BF)
        for i in range(2):
            n_ref[384 + 256 * i : 640 + 256 * i] = hb[0, i]
            p_ref[384 + 256 * i : 640 + 256 * i] = hb[1, i]

    @pl.when(even)
    def _():
        put(a_ref, b_ref)

    @pl.when(jnp.logical_not(even))
    def _():
        put(b_ref, a_ref)


def pack(t, f, s, h):
    hbm = pl.BlockSpec(memory_space=pl.ANY)
    return pl.pallas_call(
        pack_kernel,
        out_shape=(jax.ShapeDtypeStruct((896, 128), BF),) * 2,
        in_specs=[SM, hbm, hbm, hbm],
        out_specs=(VM, VM),
        scratch_shapes=[
            pltpu.VMEM((384, 128), F32),
            pltpu.VMEM((384, 128), F32),
            pltpu.VMEM((2, 32, 16, 128), BF),
            pltpu.VMEM((2, 32, 16, 128), BF),
            pltpu.VMEM((2, 2, 256, 128), BF),
            pltpu.SemaphoreType.DMA((6,)),
        ],
        name="pack",
    )(t, f, s, h)


def correlate_groups(fe, se, w_ref, band, acc, groups):
    rows = fe.shape[0]
    blocks = rows // 8
    width = G * len(groups)
    scale = 128**-0.5
    for n, (fcol, scol) in enumerate(groups):
        for b in range(blocks):
            lo, hi = max(0, 8 * b - 8), min(rows, 8 * b + 16)
            keys = se[8 * b : 8 * b + 8, scol : scol + 32, :].reshape(256, 128)
            query = fe[lo:hi, fcol : fcol + G, :].reshape((hi - lo) * G, 128).astype(BF)
            c = lax.dot_general(query, keys, NT, preferred_element_type=F32)
            c = (c * scale).reshape(hi - lo, G, 256)
            for h in range(2):
                part = pltpu.roll(c[:, :, 128 * h : 128 * h + 128], 0, 2, stride=1, stride_axis=1)
                band[b, lo - 8 * b + 8 : hi - 8 * b + 8, G * n : G * n + G, 128 * h : 128 * h + 128] = part.astype(BF)
    done = set()
    for d in range(-8, 16):
        bs = [b for b in range(blocks) if 0 <= 8 * b + d < rows]
        b0, b1 = bs[0], bs[-1] + 1
        lhs = band[b0:b1, d + 8].reshape((b1 - b0) * width, 256)
        o = 15 - d
        part = jnp.dot(lhs, w_ref[32 * o : 32 * o + 256, :], preferred_element_type=F32)
        part = part.reshape(b1 - b0, width, 128)
        for n, b in enumerate(bs):
            i = 8 * b + d
            if i in done:
                acc[i + 2] += part[n]
            else:
                acc[i + 2] = part[n]
                done.add(i)
    zero = jnp.zeros((2, width, 128), F32)
    acc[0:2] = zero
    acc[rows + 2 : rows + 4] = zero


def inner_kernel(t_ref, f_ref, s_ref, w_ref, z_ref, o_ref, fe, se, band, acc):
    for r in range(f_ref.shape[0]):
        fe[r] = f_ref[r].astype(F32)
        se[r] = mirror(s_ref[r].astype(F32)).astype(BF)
    correlate_groups(fe, se, w_ref, band, acc, [(8 + G * g, 32 - G * g) for g in range(3)])
    high = t_ref[0] // 2
    for base, ref in ((14 * (1 - high) + 2, z_ref), (14 * high + 2, o_ref)):
        for r in range(18):
            ref[48 * r : 48 * r + 48] = jnp.maximum(acc[base + r], 0.0).astype(BF)


def inner(t, f, s, w_wide):
    return pl.pallas_call(
        inner_kernel,
        out_shape=(jax.ShapeDtypeStruct((864, 128), BF),) * 2,
        in_specs=[SM] + [VM] * 3,
        out_specs=(VM,) * 2,
        scratch_shapes=[
            pltpu.VMEM((32, 64, 128), F32),
            pltpu.VMEM((32, 64, 128), BF),
            pltpu.VMEM((4, 24, 48, 256), BF),
            pltpu.VMEM((36, 48, 128), F32),
        ],
        compiler_params=pltpu.CompilerParams(vmem_limit_bytes=24 << 20),
        name="inner",
    )(t, f, s, w_wide)


def edge_kernel(t_ref, l_ref, f_ref, s_ref, a_ref, b_ref, h_ref, w_ref, oi_ref, z_ref, o_ref, near_ref, far_ref, fe, se, hal, band, acc, top, bot):
    t = t_ref[0]
    odd = lax.rem(t, 2)
    for n, ref in ((1 - odd, a_ref), (odd, b_ref)):
        hal[n, 0:16] = jnp.zeros((16, 128), F32)
        hal[n, 16:400] = ref[0:384].astype(F32)
    fpad = jnp.zeros((8, 128), F32)
    for r in range(f_ref.shape[0]):
        fe[r, 0:8] = fpad
        fe[r, 24:32] = fpad
        fe[r, 8:16] = f_ref[r, 0:16].astype(F32)[0:8]
        fe[r, 16:24] = f_ref[r, 48:64].astype(F32)[8:16]
        fe[r, 6:8] = hal[0, 336 + 2 * r : 338 + 2 * r]
        fe[r, 24:26] = hal[1, 336 + 2 * r : 338 + 2 * r]
        se[r, 32:48] = mirror(s_ref[r, 0:16].astype(F32)).astype(BF)
        se[r, 48:64] = mirror(hal[0, 10 + 10 * r : 26 + 10 * r]).astype(BF)
        se[r, 0:16] = mirror(hal[1, 16 + 10 * r : 32 + 10 * r]).astype(BF)
        se[r, 16:32] = mirror(s_ref[r, 48:64].astype(F32)).astype(BF)
    correlate_groups(fe, se, w_ref, band, acc, [(0, 32), (16, 0)])

    def write(ref, base):
        rims = []
        for r in range(18):
            m = jnp.maximum(acc[base + r], 0.0)
            ref[16 * r : 16 * r + 16] = m[8:24].astype(BF)
            rims += [m[6:8], m[24:26]]
        rims.append(jnp.zeros((8, 128), F32))
        ref[288:368] = jnp.concatenate(rims, axis=0).astype(BF)

    write(z_ref, 14 * (1 - t // 2) + 2)
    o_ref[0:864] = oi_ref[...]
    write(o_ref.at[864:1232], 14 * (t // 2) + 2)
    side_rows(t, a_ref, b_ref, top, bot)

    def ends(col, out):
        parts = []
        for i in range(12):
            if i < 2:
                v = top[256 * i + col : 256 * i + col + 16]
            elif i < 10:
                v = h_ref[i - 2, col : col + 16].astype(F32)
            else:
                v = bot[256 * (i - 10) + col : 256 * (i - 10) + col + 16]
            parts.append(v[0:2] if col == 0 else v[14:16])
        parts.append(jnp.zeros((8, 128), F32))
        out[...] = jnp.concatenate(parts, axis=0).astype(BF)

    west_even = lax.rem(l_ref[0], 2) == 0

    @pl.when(west_even)
    def _():
        ends(240, near_ref)
        ends(0, far_ref)

    @pl.when(jnp.logical_not(west_even))
    def _():
        ends(0, near_ref)
        ends(240, far_ref)


def side_rows(t, a_ref, b_ref, top, bot):
    even = lax.rem(t, 2) == 0

    @pl.when(even)
    def _():
        bot[...] = a_ref[384:896].astype(F32)
        top[...] = jnp.where(t == 2, b_ref[384:896].astype(F32), 0.0)

    @pl.when(jnp.logical_not(even))
    def _():
        top[...] = a_ref[384:896].astype(F32)
        bot[...] = jnp.where(t == 1, b_ref[384:896].astype(F32), 0.0)


def edge(t, l, f, s, a, b, h, w_wide, oi):
    def sds(n):
        return jax.ShapeDtypeStruct((n, 128), BF)

    return pl.pallas_call(
        edge_kernel,
        out_shape=(sds(368), sds(1232), sds(32), sds(32)),
        in_specs=[SM, SM] + [VM] * 7,
        out_specs=(VM,) * 4,
        scratch_shapes=[
            pltpu.VMEM((32, 32, 128), F32),
            pltpu.VMEM((32, 64, 128), BF),
            pltpu.VMEM((2, 400, 128), F32),
            pltpu.VMEM((4, 24, 32, 256), BF),
            pltpu.VMEM((36, 32, 128), F32),
            pltpu.VMEM((512, 128), F32),
            pltpu.VMEM((512, 128), F32),
        ],
        compiler_params=pltpu.CompilerParams(vmem_limit_bytes=24 << 20),
        name="edge",
    )(t, l, f, s, a, b, h, w_wide, oi)


def join_kernel(i_ref, e_ref, near_ref, far_ref, o_ref):
    o_ref[0:864] = i_ref[...]
    o_ref[864:1232] = e_ref[...]


def join(zi, ze, near, far):
    return pl.pallas_call(
        join_kernel,
        out_shape=jax.ShapeDtypeStruct((1232, 128), BF),
        in_specs=[VM] * 4,
        out_specs=VM,
        compiler_params=pltpu.CompilerParams(vmem_limit_bytes=8 << 20),
        name="join",
    )(zi, ze, near, far)


def half_kernel(*refs, last):
    if last:
        t_ref, l_ref, metric_ref, h_ref, a_ref, b_ref, near_ref, far_ref, p_ref, q_ref, gw_ref, cw_ref, other_ref, out_ref = refs[:14]
        hf, mf, x, m3s, rf, r, ug, top, bot = refs[14:]
    else:
        t_ref, l_ref, metric_ref, h_ref, a_ref, b_ref, near_ref, far_ref, p_ref, q_ref, gw_ref, cw_ref, out_ref = refs[:13]
        hf, mf, x, m3s, rf, r, ug, top, bot = refs[13:]
    t = t_ref[0]
    high = t // 2
    part = 1 - high if last else high
    c0 = pl.multiple_of(128 * part, 128)
    left_half = part == 0
    side_rows(t, a_ref, b_ref, top, bot)
    west_even = lax.rem(l_ref[0], 2) == 0
    near, far = near_ref[...].astype(F32), far_ref[...].astype(F32)
    hr = jnp.where(west_even, near, far)
    hl = jnp.where(west_even, far, near)
    for i in range(12):
        if i < 2:
            mid = top[pl.ds(256 * i + c0, 128)]
            lo, hi = top[256 * i + 120 : 256 * i + 128], top[256 * i + 128 : 256 * i + 136]
        elif i < 10:
            mid = h_ref[i - 2, pl.ds(c0, 128)].astype(F32)
            lo, hi = h_ref[i - 2, 112:128].astype(F32)[8:16], h_ref[i - 2, 128:144].astype(F32)[0:8]
        else:
            mid = bot[pl.ds(256 * (i - 10) + c0, 128)]
            lo, hi = bot[256 * (i - 10) + 120 : 256 * (i - 10) + 128], bot[256 * (i - 10) + 128 : 256 * (i - 10) + 136]
        hf[i, 2:130] = mid
        hf[i, 0:2] = jnp.where(left_half, hl[2 * i : 2 * i + 2], lo[6:8])
        hf[i, 130:132] = jnp.where(left_half, hi[0:2], hr[2 * i : 2 * i + 2])
    start = 8 * t - 2 - 14 * high
    odd = lax.rem(t, 2)
    for i in range(12):
        row = start + i
        inside = (row >= 0) & (row < 18)
        row = jnp.clip(row, 0, 17)
        for s, ref in ((odd, p_ref), (1 - odd, q_ref)):
            mid = ref[pl.ds(pl.multiple_of(48 * row, 16), 48)].astype(F32)
            ends = ref[pl.ds(pl.multiple_of(864 + 16 * row, 16), 16)].astype(F32)
            mf[i, pl.ds(10 + 64 * s, 48)] = jnp.where(inside, mid, 0.0)
            ends = jnp.where(inside, ends, 0.0)
            mf[i, pl.ds(2 + 64 * s, 8)] = ends[0:8]
            mf[i, pl.ds(58 + 64 * s, 8)] = ends[8:16]
    rims = bot
    for s, ref in ((odd, p_ref), (1 - odd, q_ref)):
        rims[8:88] = ref[1152:1232].astype(F32)
        for i in range(12):
            row = start + i
            inside = (row >= 0) & (row < 18)
            row = jnp.clip(row, 0, 17)
            v = rims[pl.ds(8 + 4 * row + 2 * s, 2)]
            mf[i, pl.ds(130 * s, 2)] = jnp.where(inside, v, 0.0)
    for q in range(3):
        for i in range(12):
            x[q, i, :, 0:128] = hf[i, q : q + 144].astype(BF)
            x[q, i, :, 128:256] = mf[i, q : q + 144].astype(BF)
    for i in range(12):
        m3s[i] = mf[i, 3:131].astype(BF)
    sides_w = jnp.concatenate([gw_ref[p, q] for q in (0, 2) for p in range(3)], axis=0)
    center_w = jnp.concatenate([gw_ref[p, 1] for p in range(3)], axis=0)
    for i in range(0, 10, 2):
        lhs = jnp.concatenate([x[q, i + p : i + p + 2].reshape(288, 256) for q in (0, 2) for p in range(3)], axis=1)
        sides = jnp.dot(lhs, sides_w, preferred_element_type=F32)
        lhs = jnp.concatenate([x[1, i + p : i + p + 2].reshape(288, 256) for p in range(3)], axis=1)
        center = jnp.dot(lhs, center_w, preferred_element_type=F32)
        for n in range(2):
            cut = slice(144 * n, 144 * n + 144)
            gate = center[cut] + sides[cut] * metric_ref[8 * t + i + n]
            gate = 0.5 * jnp.tanh(0.5 * gate) + 0.5
            rf[i + n, 0:144] = gate[:, 128:] * hf[i + n + 1, 1:145]
            if 1 <= i + n < 9:
                ug[i + n - 1] = gate[:, 0:128]
    for q in range(3):
        for i in range(10):
            r[q, i] = rf[i, q : q + 128].astype(BF)
    zero = jnp.zeros((256, 128), BF)

    def pair(rr, q):
        first = cw_ref[rr, q] if rr < 3 else zero
        second = cw_ref[rr - 1, q] if rr > 0 else zero
        return jnp.concatenate([first, second], axis=1)

    sides_w = jnp.concatenate([pair(rr, q) for q in (0, 2) for rr in range(4)], axis=0)
    center_w = jnp.concatenate([pair(rr, 1) for rr in range(4)], axis=0)

    def taps(q, row):
        mm = m3s[row + 1] if q == 2 else x[q + 1, row + 1, 0:128, 128:256]
        return [r[q, row], mm]

    def stack(qs, i):
        one = [jnp.concatenate(sum([taps(q, i + k + rr) for q in qs for rr in range(4)], []), axis=1) for k in (0, 2)]
        return jnp.concatenate(one, axis=0)

    for i in range(0, 8, 4):
        sides = jnp.dot(stack((0, 2), i), sides_w, preferred_element_type=F32)
        center = jnp.dot(stack((1,), i), center_w, preferred_element_type=F32)
        for n in range(4):
            cut = (slice(128 * (n // 2), 128 * (n // 2) + 128), slice(128 * (n % 2), 128 * (n % 2) + 128))
            cand = jnp.tanh(center[cut] + sides[cut] * metric_ref[8 * t + i + n + 1])
            u = ug[i + n, 1:129]
            h = hf[i + n + 2, 2:130]
            new = ((1.0 - u) * h + u * cand).astype(BF)
            if last:
                out_ref[i + n, pl.ds(c0, 128)] = new
                out_ref[i + n, pl.ds(pl.multiple_of(128 - c0, 128), 128)] = other_ref[i + n]
            else:
                out_ref[i + n] = new


def half(t, l, metric, h, a, b, near, far, p, q, gw, cw, other=None):
    last = other is not None
    return pl.pallas_call(
        functools.partial(half_kernel, last=last),
        out_shape=jax.ShapeDtypeStruct((8, 256 if last else 128, 128), BF),
        in_specs=[SM, SM, SM] + [VM] * (10 if last else 9),
        out_specs=VM,
        scratch_shapes=[
            pltpu.VMEM((12, 152, 128), F32),
            pltpu.VMEM((12, 152, 128), F32),
            pltpu.VMEM((3, 12, 144, 256), BF),
            pltpu.VMEM((12, 128, 128), BF),
            pltpu.VMEM((10, 144, 128), F32),
            pltpu.VMEM((3, 10, 128, 128), BF),
            pltpu.VMEM((8, 144, 128), F32),
            pltpu.VMEM((512, 128), F32),
            pltpu.VMEM((512, 128), F32),
        ],
        compiler_params=pltpu.CompilerParams(vmem_limit_bytes=24 << 20),
        name="second_half" if last else "first_half",
    )(t, l, metric, h, a, b, near, far, p, q, gw, cw, *((other,) if last else ()))


def swaps(n, first):
    pairs = [(i % n, (i + 1) % n) for i in range(first, n, 2)]
    return pairs + [(j, i) for i, j in pairs]


def body(first, second, hidden, encoder_weight, gates_weight, candidate_weight, row_metric):
    t = lax.axis_index("lat").astype(jnp.int32)[None]
    l = lax.axis_index("lon").astype(jnp.int32)[None]
    count = lax.axis_size("lon")
    slabs = count * lax.axis_size("lat")
    w_wide = widen(encoder_weight)
    metric = jnp.pad(row_metric, (1, 1))
    core = [(i, i ^ 1) for i in range(4)]
    chip = [(i, i ^ 2) for i in range(4)]

    a_send, b_send = pack(t, first, second, hidden)
    with jax.named_scope("rim_far"):
        b = lax.ppermute(b_send, BOTH, swaps(slabs, 1))
    with jax.named_scope("rim_near"):
        a = lax.ppermute(a_send, BOTH, swaps(slabs, 0))
    z_send, oi = inner(t, first, second, w_wide)
    with jax.named_scope("inner_chip"):
        zi = lax.ppermute(z_send, "lat", chip)
    ze_send, own, near_send, far_send = edge(t, l, first, second, a, b, hidden, w_wide, oi)
    with jax.named_scope("edge_chip"):
        ze = lax.ppermute(ze_send, "lat", chip)
    with jax.named_scope("state_near"):
        near = lax.ppermute(near_send, "lon", swaps(count, 0))
    with jax.named_scope("state_far"):
        far = lax.ppermute(far_send, "lon", swaps(count, 1))
    with jax.named_scope("own_core"):
        mate = lax.ppermute(own, "lat", core)
    z = join(zi, ze, near, far)
    with jax.named_scope("chip_core"):
        k = lax.ppermute(z, "lat", core)
    shared = (t, l, metric, hidden, a, b, near, far)
    one = half(*shared, own, mate, gates_weight, candidate_weight)
    return half(*shared, z, k, gates_weight, candidate_weight, one)


def solution(mesh):
    return jax.shard_map(
        body,
        mesh=mesh,
        in_specs=(
            P(None, BOTH, None),
            P(None, BOTH, None),
            P("lat", "lon", None),
            P(),
            P(),
            P(),
            P(),
        ),
        out_specs=P("lat", "lon", None),
        check_vma=False,
    )
```

```python
import functools

import jax
import jax.numpy as jnp
from jax import lax
from jax.experimental import pallas as pl
from jax.experimental.pallas import tpu as pltpu
from jax.sharding import PartitionSpec as P

RADIUS, WIN = 8, 17
G, S = 16, 5
BF, F32 = jnp.bfloat16, jnp.float32
NT = (((1,), (1,)), ((), ()))
BOTH = ("lon", "lat")
VM = pl.BlockSpec(memory_space=pltpu.VMEM)
SM = pl.BlockSpec(memory_space=pltpu.SMEM)


def mirror(x):
    n = x.shape[0] // 8
    ids = 7 - lax.broadcasted_iota(jnp.int32, (8, 128), 0)
    tiles = [
        jnp.take_along_axis(x[8 * k : 8 * k + 8], ids, axis=0, mode="promise_in_bounds")
        for k in reversed(range(n))
    ]
    return jnp.concatenate(tiles, axis=0)


def pack_kernel(t_ref, l_ref, f_ref, s_ref, h_ref, a_ref, b_ref, near_ref, far_ref, up, down, sb, fb, hb, cb, sem):
    rows = f_ref.shape[0]
    moves = []
    for n, col in enumerate((48, 0)):
        moves.append((s_ref.at[:, col : col + 16], sb.at[n]))
        moves.append((f_ref.at[:, col : col + 16], fb.at[n]))
        moves.append((h_ref.at[6 - 6 * n : 8 - 6 * n], hb.at[n]))
        moves.append((h_ref.at[:, 240 - 240 * n : 256 - 240 * n], cb.at[n]))
    copies = [pltpu.make_async_copy(a, b, sem.at[k]) for k, (a, b) in enumerate(moves)]
    for c in copies:
        c.start()
    for c in copies:
        c.wait()
    for r in range(rows):
        up[10 * r : 10 * r + 10] = sb[0, r].astype(F32)[6:16]
        down[10 * r : 10 * r + 10] = sb[1, r].astype(F32)[0:10]
        up[320 + 2 * r : 322 + 2 * r] = fb[0, r].astype(F32)[14:16]
        down[320 + 2 * r : 322 + 2 * r] = fb[1, r].astype(F32)[0:2]
    east = jnp.concatenate([cb[0, i].astype(F32)[14:16] for i in range(8)], axis=0)
    west = jnp.concatenate([cb[1, i].astype(F32)[0:2] for i in range(8)], axis=0)
    even = lax.rem(l_ref[0], 2) == 0
    near_ref[...] = jnp.where(even, east, west).astype(BF)
    far_ref[...] = jnp.where(even, west, east).astype(BF)
    even = lax.rem(t_ref[0], 2) == 0

    def put(n_ref, p_ref):
        n_ref[0:384] = up[...].astype(BF)
        p_ref[0:384] = down[...].astype(BF)
        for i in range(2):
            n_ref[384 + 256 * i : 640 + 256 * i] = hb[0, i]
            p_ref[384 + 256 * i : 640 + 256 * i] = hb[1, i]

    @pl.when(even)
    def _():
        put(a_ref, b_ref)

    @pl.when(jnp.logical_not(even))
    def _():
        put(b_ref, a_ref)


def pack(t, l, f, s, h):
    hbm = pl.BlockSpec(memory_space=pl.ANY)
    return pl.pallas_call(
        pack_kernel,
        out_shape=(jax.ShapeDtypeStruct((896, 128), BF),) * 2 + (jax.ShapeDtypeStruct((16, 128), BF),) * 2,
        in_specs=[SM, SM, hbm, hbm, hbm],
        out_specs=(VM,) * 4,
        scratch_shapes=[
            pltpu.VMEM((384, 128), F32),
            pltpu.VMEM((384, 128), F32),
            pltpu.VMEM((2, 32, 16, 128), BF),
            pltpu.VMEM((2, 32, 16, 128), BF),
            pltpu.VMEM((2, 2, 256, 128), BF),
            pltpu.VMEM((2, 8, 16, 128), BF),
            pltpu.SemaphoreType.DMA((8,)),
        ],
        name="pack",
    )(t, l, f, s, h)


def correlate_groups(fe, se, w_ref, band, acc, groups):
    rows = fe.shape[0]
    blocks = rows // 8
    width = G * len(groups)
    scale = 128**-0.5
    for n, (fcol, scol) in enumerate(groups):
        for b in range(blocks):
            lo, hi = max(0, 8 * b - 8), min(rows, 8 * b + 16)
            keys = se[8 * b : 8 * b + 8, scol : scol + 32, :].reshape(256, 128)
            query = fe[lo:hi, fcol : fcol + G, :].reshape((hi - lo) * G, 128).astype(BF)
            c = lax.dot_general(query, keys, NT, preferred_element_type=F32)
            c = (c * scale).reshape(hi - lo, G, 256)
            for h in range(2):
                part = pltpu.roll(c[:, :, 128 * h : 128 * h + 128], 0, 2, stride=1, stride_axis=1)
                band[b, lo - 8 * b + 8 : hi - 8 * b + 8, G * n : G * n + G, 128 * h : 128 * h + 128] = part.astype(BF)
    done = set()
    for d in range(-8, 16):
        bs = [b for b in range(blocks) if 0 <= 8 * b + d < rows]
        b0, b1 = bs[0], bs[-1] + 1
        lhs = band[b0:b1, d + 8].reshape((b1 - b0) * width, 256)
        o = 15 - d
        part = jnp.dot(lhs, w_ref[32 * o : 32 * o + 256, :], preferred_element_type=F32)
        part = part.reshape(b1 - b0, width, 128)
        for n, b in enumerate(bs):
            i = 8 * b + d
            if i in done:
                acc[i + 2] += part[n]
            else:
                acc[i + 2] = part[n]
                done.add(i)
    zero = jnp.zeros((2, width, 128), F32)
    acc[0:2] = zero
    acc[rows + 2 : rows + 4] = zero


def widen(enc_ref, wide_ref, enc, wide):
    wide[...] = jnp.zeros(wide.shape, F32)
    enc[0:8] = jnp.zeros((8, 128), F32)
    enc[8:297] = enc_ref[...].astype(F32)
    for a in range(WIN):
        at = 32 * (a + 7) + 15
        wide[at : at + 17] = mirror(enc[17 * a + 1 : 17 * a + 25])[0:17]
    wide_ref[...] = wide[...].astype(BF)


def inner_kernel(t_ref, f_ref, s_ref, enc_ref, z_ref, o_ref, c_ref, w_ref, fe, se, band, acc, enc, wide):
    widen(enc_ref, w_ref, enc, wide)
    for r in range(f_ref.shape[0]):
        fe[r] = f_ref[r].astype(F32)
        se[r] = mirror(s_ref[r].astype(F32)).astype(BF)
    correlate_groups(fe, se, w_ref, band, acc, [(8 + G * g, 32 - G * g) for g in range(3)])
    high = t_ref[0] // 2
    for base, ref in ((14 * (1 - high) + 2, z_ref), (14 * high + 2, o_ref)):
        for r in range(18):
            ref[48 * r : 48 * r + 48] = jnp.maximum(acc[base + r], 0.0).astype(BF)
    base = 8 * (t_ref[0] ^ 1)
    for r in range(12):
        c_ref[48 * r : 48 * r + 48] = jnp.maximum(acc[base + r], 0.0).astype(BF)


def inner(t, f, s, enc):
    return pl.pallas_call(
        inner_kernel,
        out_shape=(jax.ShapeDtypeStruct((864, 128), BF),) * 2 + (jax.ShapeDtypeStruct((576, 128), BF), jax.ShapeDtypeStruct((992, 128), BF)),
        in_specs=[SM] + [VM] * 3,
        out_specs=(VM,) * 4,
        scratch_shapes=[
            pltpu.VMEM((32, 64, 128), F32),
            pltpu.VMEM((32, 64, 128), BF),
            pltpu.VMEM((4, 24, 48, 256), BF),
            pltpu.VMEM((36, 48, 128), F32),
            pltpu.VMEM((304, 128), F32),
            pltpu.VMEM((992, 128), F32),
        ],
        compiler_params=pltpu.CompilerParams(vmem_limit_bytes=24 << 20),
        cost_estimate=pl.CostEstimate(flops=1000000000, bytes_accessed=1000000, transcendentals=0),
        name="inner",
    )(t, f, s, enc)


def edge_kernel(t_ref, f_ref, s_ref, a_ref, b_ref, near_ref, far_ref, w_ref, oi_ref, ci_ref, z_ref, o_ref, c_ref, fe, se, hal, band, acc):
    t = t_ref[0]
    odd = lax.rem(t, 2)
    for n, ref in ((1 - odd, a_ref), (odd, b_ref)):
        hal[n, 0:16] = jnp.zeros((16, 128), F32)
        hal[n, 16:400] = ref[0:384].astype(F32)
    fpad = jnp.zeros((8, 128), F32)
    for r in range(f_ref.shape[0]):
        fe[r, 0:8] = fpad
        fe[r, 24:32] = fpad
        fe[r, 8:16] = f_ref[r, 0:16].astype(F32)[0:8]
        fe[r, 16:24] = f_ref[r, 48:64].astype(F32)[8:16]
        fe[r, 6:8] = hal[0, 336 + 2 * r : 338 + 2 * r]
        fe[r, 24:26] = hal[1, 336 + 2 * r : 338 + 2 * r]
        se[r, 32:48] = mirror(s_ref[r, 0:16].astype(F32)).astype(BF)
        se[r, 48:64] = mirror(hal[0, 10 + 10 * r : 26 + 10 * r]).astype(BF)
        se[r, 0:16] = mirror(hal[1, 16 + 10 * r : 32 + 10 * r]).astype(BF)
        se[r, 16:32] = mirror(s_ref[r, 48:64].astype(F32)).astype(BF)
    correlate_groups(fe, se, w_ref, band, acc, [(0, 32), (16, 0)])

    def write(ref, base, count=18):
        rims = []
        for r in range(count):
            m = jnp.maximum(acc[base + r], 0.0)
            ref[16 * r : 16 * r + 16] = m[8:24].astype(BF)
            rims += [m[6:8], m[24:26]]
        if count % 4:
            rims.append(jnp.zeros((8, 128), F32))
        at, n = 16 * count, -(-count // 4) * 16
        ref[at : at + n] = jnp.concatenate(rims, axis=0).astype(BF)

    write(z_ref, 14 * (1 - t // 2) + 2)
    o_ref[0:864] = oi_ref[...]
    write(o_ref.at[864:1232], 14 * (t // 2) + 2)
    c_ref[0:576] = ci_ref[...]
    write(c_ref.at[576:816], 8 * (t ^ 1), 12)
    for ref, at in ((z_ref, 368), (c_ref, 816)):
        ref[at : at + 16] = near_ref[...]
        ref[at + 16 : at + 32] = far_ref[...]


def side_rows(t, a_ref, b_ref, top, bot):
    even = lax.rem(t, 2) == 0

    @pl.when(even)
    def _():
        bot[...] = a_ref[384:896].astype(F32)
        top[...] = jnp.where(t == 2, b_ref[384:896].astype(F32), 0.0)

    @pl.when(jnp.logical_not(even))
    def _():
        top[...] = a_ref[384:896].astype(F32)
        bot[...] = jnp.where(t == 1, b_ref[384:896].astype(F32), 0.0)


def edge(t, f, s, a, b, near, far, w_wide, oi, ci):
    return pl.pallas_call(
        edge_kernel,
        out_shape=(jax.ShapeDtypeStruct((400, 128), BF), jax.ShapeDtypeStruct((1232, 128), BF), jax.ShapeDtypeStruct((848, 128), BF)),
        in_specs=[SM] + [VM] * 9,
        out_specs=(VM,) * 3,
        scratch_shapes=[
            pltpu.VMEM((32, 32, 128), F32),
            pltpu.VMEM((32, 64, 128), BF),
            pltpu.VMEM((2, 400, 128), F32),
            pltpu.VMEM((4, 24, 32, 256), BF),
            pltpu.VMEM((36, 32, 128), F32),
        ],
        compiler_params=pltpu.CompilerParams(vmem_limit_bytes=24 << 20),
        cost_estimate=pl.CostEstimate(flops=1000000000, bytes_accessed=1000000, transcendentals=0),
        name="edge",
    )(t, f, s, a, b, near, far, w_wide, oi, ci)


def join_kernel(i_ref, e_ref, one_ref, o_ref):
    o_ref[0:864] = i_ref[...]
    o_ref[864:1264] = e_ref[...]


def join(zi, ze, one):
    return pl.pallas_call(
        join_kernel,
        out_shape=jax.ShapeDtypeStruct((1264, 128), BF),
        in_specs=[VM] * 3,
        out_specs=VM,
        compiler_params=pltpu.CompilerParams(vmem_limit_bytes=8 << 20),
        name="join",
    )(zi, ze, one)


def state_rows(t, a_ref, b_ref, h_ref, hs, top, bot):
    side_rows(t, a_ref, b_ref, top, bot)
    hs[0:512] = top[...]
    hs[2560:3072] = bot[...]
    for i in range(8):
        hs[512 + 256 * i : 768 + 256 * i] = h_ref[i].astype(F32)


def gates(metric_ref, t, x, gw_ref, width, put):
    sides_w = jnp.concatenate([gw_ref[p, q] for q in (0, 2) for p in range(3)], axis=0)
    center_w = jnp.concatenate([gw_ref[p, 1] for p in range(3)], axis=0)
    for i in range(0, 10, 2):
        lhs = jnp.concatenate([x[q, i + p : i + p + 2].reshape(2 * width, 256) for q in (0, 2) for p in range(3)], axis=1)
        sides = jnp.dot(lhs, sides_w, preferred_element_type=F32)
        lhs = jnp.concatenate([x[1, i + p : i + p + 2].reshape(2 * width, 256) for p in range(3)], axis=1)
        center = jnp.dot(lhs, center_w, preferred_element_type=F32)
        for n in range(2):
            cut = slice(width * n, width * n + width)
            gate = center[cut] + sides[cut] * metric_ref[jnp.clip(8 * t + i + n - 1, 0, 31)]
            put(i + n, 0.5 * jnp.tanh(0.5 * gate) + 0.5)


def candidates(metric_ref, t, x, m3s, r, cw_ref, width, put):
    zero = jnp.zeros((256, 128), BF)

    def pair(rr, q):
        first = cw_ref[rr, q] if rr < 3 else zero
        second = cw_ref[rr - 1, q] if rr > 0 else zero
        return jnp.concatenate([first, second], axis=1)

    sides_w = jnp.concatenate([pair(rr, q) for q in (0, 2) for rr in range(4)], axis=0)
    center_w = jnp.concatenate([pair(rr, 1) for rr in range(4)], axis=0)

    def taps(q, row):
        mm = m3s[row + 1] if q == 2 else x[q + 1, row + 1, 0:width, 128:256]
        return [r[q, row], mm]

    def stack(qs, i):
        one = [jnp.concatenate(sum([taps(q, i + k + rr) for q in qs for rr in range(4)], []), axis=1) for k in (0, 2)]
        return jnp.concatenate(one, axis=0)

    for i in range(0, 8, 4):
        sides = jnp.dot(stack((0, 2), i), sides_w, preferred_element_type=F32)
        center = jnp.dot(stack((1,), i), center_w, preferred_element_type=F32)
        for n in range(4):
            cut = (slice(width * (n // 2), width * (n // 2) + width), slice(128 * (n % 2), 128 * (n % 2) + 128))
            put(i + n, jnp.tanh(center[cut] + sides[cut] * metric_ref[8 * t + i + n]))


def piece_row(ref, row, inside, count):
    mid = ref[pl.ds(pl.multiple_of(48 * row, 16), 48)].astype(F32)
    ends = ref[pl.ds(pl.multiple_of(48 * count + 16 * row, 16), 16)].astype(F32)
    if inside is not None:
        mid, ends = jnp.where(inside, mid, 0.0), jnp.where(inside, ends, 0.0)
    return mid, ends


def first_kernel(t_ref, metric_ref, h_ref, a_ref, b_ref, own_ref, mate_ref, zi_ref, gw_ref, cw_ref, out_ref, hs, mf, x, m3s, rf, r, ug, top, bot, rims):
    t = t_ref[0]
    high = t // 2
    base = 112 * high
    state_rows(t, a_ref, b_ref, h_ref, hs, top, bot)
    start = 8 * t - 2 - 14 * high
    odd = lax.rem(t, 2)
    for s, ref, count in ((odd, own_ref, 18), (1 - odd, mate_ref, 12)):
        rims[0:80] = ref[1152:1232].astype(F32) if count == 18 else jnp.pad(ref[768:816].astype(F32), ((0, 32), (0, 0)))
        for i in range(12):
            row, inside = i, None
            if count == 18:
                row = start + i
                inside = (row >= 0) & (row < 18)
                row = jnp.clip(row, 0, 17)
            mid, ends = piece_row(ref, row, inside, count)
            at = 64 * s + 16 * high
            mf[i, pl.ds(at + 8, 48)] = mid
            mf[i, pl.ds(at, 8)] = ends[0:8]
            mf[i, pl.ds(at + 56, 8)] = ends[8:16]

            @pl.when(s != high)
            def _(i=i, row=row, s=s, inside=inside):
                v = rims[pl.ds(4 * row + 2 * s, 2)]
                mf[i, pl.ds(128 - 114 * high, 2)] = v if inside is None else jnp.where(inside, v, 0.0)

    for q in range(3):
        for i in range(12):
            x[q, i, :, 0:128] = hs[pl.ds(256 * i + base + 14 + q, 128)].astype(BF)
            x[q, i, :, 128:256] = mf[i, 14 + q : 142 + q].astype(BF)
    for i in range(12):
        m3s[i] = mf[i, 17:129].astype(BF)

    def put_gate(i, gate):
        rf[i, 0:128] = gate[:, 128:] * hs[pl.ds(256 * (i + 1) + base + 15, 128)]
        if 1 <= i < 9:
            ug[i - 1] = gate[:, 0:128]

    gates(metric_ref, t, x, gw_ref, 128, put_gate)
    for q in range(3):
        for i in range(10):
            r[q, i] = rf[i, q : q + 112].astype(BF)

    def put_new(i, cand):
        u = ug[i, 1:113]
        h = hs[pl.ds(256 * (i + 2) + base + 16, 112)]
        out_ref[i] = ((1.0 - u) * h + u * cand).astype(BF)

    candidates(metric_ref, t, x, m3s, r, cw_ref, 112, put_new)


def first_part(t, metric, h, a, b, own, mate, zi, gw, cw):
    return pl.pallas_call(
        first_kernel,
        out_shape=jax.ShapeDtypeStruct((8, 112, 128), BF),
        in_specs=[SM, SM] + [VM] * 8,
        out_specs=VM,
        scratch_shapes=[
            pltpu.VMEM((3072, 128), F32),
            pltpu.VMEM((12, 152, 128), F32),
            pltpu.VMEM((3, 12, 128, 256), BF),
            pltpu.VMEM((12, 112, 128), BF),
            pltpu.VMEM((10, 136, 128), F32),
            pltpu.VMEM((3, 10, 112, 128), BF),
            pltpu.VMEM((8, 128, 128), F32),
            pltpu.VMEM((512, 128), F32),
            pltpu.VMEM((512, 128), F32),
            pltpu.VMEM((80, 128), F32),
        ],
        compiler_params=pltpu.CompilerParams(vmem_limit_bytes=24 << 20),
        cost_estimate=pl.CostEstimate(flops=4000000000, bytes_accessed=4000000, transcendentals=0),
        name="first_part",
    )(t, metric, h, a, b, own, mate, zi, gw, cw)


def second_kernel(
    t_ref, l_ref, metric_ref, h_ref, a_ref, b_ref, near_ref, far_ref, own_ref, mate_ref, z_ref, k_ref, gw_ref, cw_ref, one_ref, out_ref,
    hs, hf, mf, x, m3s, rf, r, ug, top, bot, rims,
):
    t = t_ref[0]
    high = t // 2
    c0 = pl.multiple_of(128 - 128 * high, 128)
    state_rows(t, a_ref, b_ref, h_ref, hs, top, bot)
    west_even = lax.rem(l_ref[0], 2) == 0
    odd = lax.rem(t, 2)
    low = high == 0

    def twelve(own, at):
        mates, others = mate_ref[816 + at : 832 + at].astype(F32), k_ref[1232 + at : 1248 + at].astype(F32)
        others = jnp.where((t == 1) | (t == 2), others, 0.0)
        above = jnp.where(odd == 1, mates, others)[12:16]
        below = jnp.where(odd == 1, others, mates)[0:4]
        return jnp.concatenate([above, own[...].astype(F32), below], axis=0)

    near, far = twelve(near_ref, 0), twelve(far_ref, 16)
    hr = jnp.where(west_even, near, far)
    hl = jnp.where(west_even, far, near)
    for i in range(12):
        hf[i, 2:130] = hs[pl.ds(256 * i + c0, 128)]
        side_w, side_e = hl[2 * i : 2 * i + 2], hr[2 * i : 2 * i + 2]
        hf[i, 0:2] = jnp.where(low, hs[256 * i + 126 : 256 * i + 128], side_w)
        hf[i, 130:132] = jnp.where(low, side_e, hs[256 * i + 128 : 256 * i + 130])
        hf[i, pl.ds(146 - 2 * high, 18)] = hs[pl.ds(256 * i + 238 * high, 18)]
        hf[i, pl.ds(144 + 18 * high, 2)] = jnp.where(low, side_w, side_e)
    start = 8 * t - 2 - 14 * high
    for s, ref in ((odd, z_ref), (1 - odd, k_ref)):
        rims[0:80] = ref[1152:1232].astype(F32)
        for i in range(12):
            row = start + i
            inside = (row >= 0) & (row < 18)
            row = jnp.clip(row, 0, 17)
            mid = ref[pl.ds(pl.multiple_of(48 * row, 16), 48)].astype(F32)
            ends = ref[pl.ds(pl.multiple_of(864 + 16 * row, 16), 16)].astype(F32)
            mf[i, pl.ds(10 + 64 * s, 48)] = jnp.where(inside, mid, 0.0)
            ends = jnp.where(inside, ends, 0.0)
            mf[i, pl.ds(2 + 64 * s, 8)] = ends[0:8]
            mf[i, pl.ds(58 + 64 * s, 8)] = ends[8:16]
            v = rims[pl.ds(4 * row + 2 * s, 2)]
            mf[i, pl.ds(130 * s, 2)] = jnp.where(inside, v, 0.0)
    mine = odd == high
    mates = jnp.pad(mate_ref[768:816].astype(F32), ((0, 32), (0, 0)))
    rims[0:80] = jnp.where(mine, own_ref[1152:1232].astype(F32), mates)
    for i in range(12):
        row = start + i
        inside = (row >= 0) & (row < 18)
        row = jnp.clip(row, 0, 17)
        at = pl.multiple_of(48 * row + 32 * high, 16)
        mid = jnp.where(inside, own_ref[pl.ds(at, 16)].astype(F32), 0.0)
        at = pl.multiple_of(864 + 16 * row, 16)
        ends = jnp.where(inside, own_ref[pl.ds(at, 16)].astype(F32), 0.0)
        at = pl.multiple_of(48 * i + 32 * high, 16)
        mid = jnp.where(mine, mid, mate_ref[pl.ds(at, 16)].astype(F32))
        ends = jnp.where(mine, ends, mate_ref[576 + 16 * i : 592 + 16 * i].astype(F32))
        mf[i, pl.ds(154 - 10 * high, 10)] = jnp.where(low, mid[0:10], mid[6:16])
        mf[i, pl.ds(146 + 8 * high, 8)] = jnp.where(low, ends[0:8], ends[8:16])
        row = jnp.where(mine, row, i)
        inside = inside | jnp.logical_not(mine)
        v = rims[pl.ds(4 * row + 2 * high, 2)]
        mf[i, pl.ds(144 + 18 * high, 2)] = jnp.where(inside, v, 0.0)
    for q in range(3):
        for i in range(12):
            x[q, i, :, 0:128] = hf[i, q : q + 176].astype(BF)
            x[q, i, :, 128:256] = mf[i, q : q + 176].astype(BF)
    for i in range(12):
        m3s[i] = mf[i, 3:163].astype(BF)

    def put_gate(i, gate):
        rf[i, 0:176] = gate[:, 128:] * hf[i + 1, 1:177]
        if 1 <= i < 9:
            ug[i - 1] = gate[:, 0:128]

    gates(metric_ref, t, x, gw_ref, 176, put_gate)
    for q in range(3):
        for i in range(10):
            r[q, i] = rf[i, q : q + 160].astype(BF)

    def put_new(i, cand):
        u = ug[i, 1:161]
        h = hf[i + 2, 2:162]
        new = ((1.0 - u) * h + u * cand).astype(BF)
        out_ref[i, pl.ds(c0, 128)] = new[0:128]
        out_ref[i, pl.ds(pl.multiple_of(240 * high, 16), 16)] = new[144:160]
        out_ref[i, pl.ds(pl.multiple_of(16 + 112 * high, 16), 112)] = one_ref[i]

    candidates(metric_ref, t, x, m3s, r, cw_ref, 160, put_new)


def second_part(t, l, metric, h, a, b, near, far, own, mate, z, k, gw, cw, one):
    return pl.pallas_call(
        second_kernel,
        out_shape=jax.ShapeDtypeStruct((8, 256, 128), BF),
        in_specs=[SM, SM, SM] + [VM] * 12,
        out_specs=VM,
        scratch_shapes=[
            pltpu.VMEM((3072, 128), F32),
            pltpu.VMEM((12, 184, 128), F32),
            pltpu.VMEM((12, 184, 128), F32),
            pltpu.VMEM((3, 12, 176, 256), BF),
            pltpu.VMEM((12, 160, 128), BF),
            pltpu.VMEM((10, 184, 128), F32),
            pltpu.VMEM((3, 10, 160, 128), BF),
            pltpu.VMEM((8, 176, 128), F32),
            pltpu.VMEM((512, 128), F32),
            pltpu.VMEM((512, 128), F32),
            pltpu.VMEM((80, 128), F32),
        ],
        compiler_params=pltpu.CompilerParams(vmem_limit_bytes=24 << 20),
        cost_estimate=pl.CostEstimate(flops=5000000000, bytes_accessed=4000000, transcendentals=0),
        name="second_part",
    )(t, l, metric, h, a, b, near, far, own, mate, z, k, gw, cw, one)


def swaps(n, first):
    pairs = [(i % n, (i + 1) % n) for i in range(first, n, 2)]
    return pairs + [(j, i) for i, j in pairs]


def body(first, second, hidden, encoder_weight, gates_weight, candidate_weight, row_metric):
    t = lax.axis_index("lat").astype(jnp.int32)[None]
    l = lax.axis_index("lon").astype(jnp.int32)[None]
    count = lax.axis_size("lon")
    slabs = count * lax.axis_size("lat")
    core = [(i, i ^ 1) for i in range(4)]
    chip = [(i, i ^ 2) for i in range(4)]

    a_send, b_send, near_send, far_send = pack(t, l, first, second, hidden)
    with jax.named_scope("rim_far"):
        b = lax.ppermute(b_send, BOTH, swaps(slabs, 1))
    with jax.named_scope("rim_near"):
        a = lax.ppermute(a_send, BOTH, swaps(slabs, 0))
    with jax.named_scope("state_near"):
        near = lax.ppermute(near_send, "lon", swaps(count, 0))
    with jax.named_scope("state_far"):
        far = lax.ppermute(far_send, "lon", swaps(count, 1))
    zi_send, oi, ci, w_wide = inner(t, first, second, encoder_weight)
    with jax.named_scope("inner_chip"):
        zi = lax.ppermute(zi_send, "lat", chip)
    ze_send, own, own_send = edge(t, first, second, a, b, near, far, w_wide, oi, ci)
    with jax.named_scope("edge_chip"):
        ze = lax.ppermute(ze_send, "lat", chip)
    with jax.named_scope("own_core"):
        mate = lax.ppermute(own_send, "lat", core)
    one = first_part(t, row_metric, hidden, a, b, own, mate, zi, gates_weight, candidate_weight)
    z = join(zi, ze, one)
    with jax.named_scope("chip_core"):
        k = lax.ppermute(z, "lat", core)
    return second_part(t, l, row_metric, hidden, a, b, near, far, own, mate, z, k, gates_weight, candidate_weight, one)


def solution(mesh):
    return jax.shard_map(
        body,
        mesh=mesh,
        in_specs=(
            P(None, BOTH, None),
            P(None, BOTH, None),
            P("lat", "lon", None),
            P(),
            P(),
            P(),
            P(),
        ),
        out_specs=P("lat", "lon", None),
        check_vma=False,
    )
```

```python
import functools

import jax
import jax.numpy as jnp
from jax import lax
from jax.experimental import pallas as pl
from jax.experimental.pallas import tpu as pltpu
from jax.sharding import PartitionSpec as P

RADIUS, WIN = 8, 17
G, S = 16, 5
BF, F32 = jnp.bfloat16, jnp.float32
NT = (((1,), (1,)), ((), ()))
BOTH = ("lon", "lat")
VM = pl.BlockSpec(memory_space=pltpu.VMEM)
SM = pl.BlockSpec(memory_space=pltpu.SMEM)


def mirror(x):
    n = x.shape[0] // 8
    ids = 7 - lax.broadcasted_iota(jnp.int32, (8, 128), 0)
    tiles = [
        jnp.take_along_axis(x[8 * k : 8 * k + 8], ids, axis=0, mode="promise_in_bounds")
        for k in reversed(range(n))
    ]
    return jnp.concatenate(tiles, axis=0)


def pack_kernel(t_ref, l_ref, f_ref, s_ref, h_ref, a_ref, b_ref, near_ref, far_ref, up, down, sb, fb, hb, cb, sem):
    rows = f_ref.shape[0]
    moves = []
    for n, col in enumerate((48, 0)):
        moves.append((s_ref.at[:, col : col + 16], sb.at[n]))
        moves.append((f_ref.at[:, col : col + 16], fb.at[n]))
        moves.append((h_ref.at[6 - 6 * n : 8 - 6 * n], hb.at[n]))
        moves.append((h_ref.at[:, 240 - 240 * n : 256 - 240 * n], cb.at[n]))
    copies = [pltpu.make_async_copy(a, b, sem.at[k]) for k, (a, b) in enumerate(moves)]
    for c in copies:
        c.start()
    for c in copies:
        c.wait()
    for r in range(rows):
        up[10 * r : 10 * r + 10] = sb[0, r].astype(F32)[6:16]
        down[10 * r : 10 * r + 10] = sb[1, r].astype(F32)[0:10]
        up[320 + 2 * r : 322 + 2 * r] = fb[0, r].astype(F32)[14:16]
        down[320 + 2 * r : 322 + 2 * r] = fb[1, r].astype(F32)[0:2]
    east = jnp.concatenate([cb[0, i].astype(F32)[14:16] for i in range(8)], axis=0)
    west = jnp.concatenate([cb[1, i].astype(F32)[0:2] for i in range(8)], axis=0)
    even = lax.rem(l_ref[0], 2) == 0
    near_ref[...] = jnp.where(even, east, west).astype(BF)
    far_ref[...] = jnp.where(even, west, east).astype(BF)
    even = lax.rem(t_ref[0], 2) == 0

    def put(n_ref, p_ref):
        n_ref[0:384] = up[...].astype(BF)
        p_ref[0:384] = down[...].astype(BF)
        for i in range(2):
            n_ref[384 + 256 * i : 640 + 256 * i] = hb[0, i]
            p_ref[384 + 256 * i : 640 + 256 * i] = hb[1, i]

    @pl.when(even)
    def _():
        put(a_ref, b_ref)

    @pl.when(jnp.logical_not(even))
    def _():
        put(b_ref, a_ref)


def pack(t, l, f, s, h):
    hbm = pl.BlockSpec(memory_space=pl.ANY)
    return pl.pallas_call(
        pack_kernel,
        out_shape=(pltpu.VMEM((896, 128), BF),) * 2 + (pltpu.VMEM((16, 128), BF),) * 2,
        in_specs=[SM, SM, hbm, hbm, hbm],
        out_specs=(VM,) * 4,
        scratch_shapes=[
            pltpu.VMEM((384, 128), F32),
            pltpu.VMEM((384, 128), F32),
            pltpu.VMEM((2, 32, 16, 128), BF),
            pltpu.VMEM((2, 32, 16, 128), BF),
            pltpu.VMEM((2, 2, 256, 128), BF),
            pltpu.VMEM((2, 8, 16, 128), BF),
            pltpu.SemaphoreType.DMA((8,)),
        ],
        name="pack",
    )(t, l, f, s, h)


def correlate_groups(fe, se, w_ref, band, acc, groups):
    rows = fe.shape[0]
    blocks = rows // 8
    width = G * len(groups)
    scale = 128**-0.5
    for n, (fcol, scol) in enumerate(groups):
        for b in range(blocks):
            lo, hi = max(0, 8 * b - 8), min(rows, 8 * b + 16)
            keys = se[8 * b : 8 * b + 8, scol : scol + 32, :].reshape(256, 128)
            query = fe[lo:hi, fcol : fcol + G, :].reshape((hi - lo) * G, 128).astype(BF)
            c = lax.dot_general(query, keys, NT, preferred_element_type=F32)
            c = (c * scale).reshape(hi - lo, G, 256)
            for h in range(2):
                part = pltpu.roll(c[:, :, 128 * h : 128 * h + 128], 0, 2, stride=1, stride_axis=1)
                band[b, lo - 8 * b + 8 : hi - 8 * b + 8, G * n : G * n + G, 128 * h : 128 * h + 128] = part.astype(BF)
    done = set()
    for d in range(-8, 16):
        bs = [b for b in range(blocks) if 0 <= 8 * b + d < rows]
        b0, b1 = bs[0], bs[-1] + 1
        lhs = band[b0:b1, d + 8].reshape((b1 - b0) * width, 256)
        o = 15 - d
        part = jnp.dot(lhs, w_ref[32 * o : 32 * o + 256, :], preferred_element_type=F32)
        part = part.reshape(b1 - b0, width, 128)
        for n, b in enumerate(bs):
            i = 8 * b + d
            if i in done:
                acc[i + 2] += part[n]
            else:
                acc[i + 2] = part[n]
                done.add(i)
    zero = jnp.zeros((2, width, 128), F32)
    acc[0:2] = zero
    acc[rows + 2 : rows + 4] = zero


def widen(enc_ref, wide_ref, enc, wide):
    wide[...] = jnp.zeros(wide.shape, F32)
    enc[0:8] = jnp.zeros((8, 128), F32)
    enc[8:297] = enc_ref[...].astype(F32)
    for a in range(WIN):
        at = 32 * (a + 7) + 15
        wide[at : at + 17] = mirror(enc[17 * a + 1 : 17 * a + 25])[0:17]
    wide_ref[...] = wide[...].astype(BF)


def inner_kernel(t_ref, f_ref, s_ref, enc_ref, z_ref, o_ref, c_ref, w_ref, fe, se, band, acc, enc, wide):
    widen(enc_ref, w_ref, enc, wide)
    for r in range(f_ref.shape[0]):
        fe[r] = f_ref[r].astype(F32)
        se[r] = mirror(s_ref[r].astype(F32)).astype(BF)
    correlate_groups(fe, se, w_ref, band, acc, [(8 + G * g, 32 - G * g) for g in range(3)])
    high = t_ref[0] // 2
    for base, ref in ((14 * (1 - high) + 2, z_ref), (14 * high + 2, o_ref)):
        for r in range(18):
            ref[48 * r : 48 * r + 48] = jnp.maximum(acc[base + r], 0.0).astype(BF)
    base = 8 * (t_ref[0] ^ 1)
    for r in range(12):
        c_ref[48 * r : 48 * r + 48] = jnp.maximum(acc[base + r], 0.0).astype(BF)


def inner(t, f, s, enc):
    return pl.pallas_call(
        inner_kernel,
        out_shape=(jax.ShapeDtypeStruct((864, 128), BF),) * 2 + (jax.ShapeDtypeStruct((576, 128), BF), jax.ShapeDtypeStruct((992, 128), BF)),
        in_specs=[SM] + [VM] * 3,
        out_specs=(VM,) * 4,
        scratch_shapes=[
            pltpu.VMEM((32, 64, 128), F32),
            pltpu.VMEM((32, 64, 128), BF),
            pltpu.VMEM((4, 24, 48, 256), BF),
            pltpu.VMEM((36, 48, 128), F32),
            pltpu.VMEM((304, 128), F32),
            pltpu.VMEM((992, 128), F32),
        ],
        compiler_params=pltpu.CompilerParams(vmem_limit_bytes=24 << 20),
        cost_estimate=pl.CostEstimate(flops=1000000000, bytes_accessed=1000000, transcendentals=0),
        name="inner",
    )(t, f, s, enc)


def edge_kernel(t_ref, f_ref, s_ref, a_ref, b_ref, near_ref, far_ref, w_ref, oi_ref, ci_ref, z_ref, o_ref, c_ref, fe, se, hal, band, acc):
    t = t_ref[0]
    odd = lax.rem(t, 2)
    for n, ref in ((1 - odd, a_ref), (odd, b_ref)):
        hal[n, 0:16] = jnp.zeros((16, 128), F32)
        hal[n, 16:400] = ref[0:384].astype(F32)
    fpad = jnp.zeros((8, 128), F32)
    for r in range(f_ref.shape[0]):
        fe[r, 0:8] = fpad
        fe[r, 24:32] = fpad
        fe[r, 8:16] = f_ref[r, 0:16].astype(F32)[0:8]
        fe[r, 16:24] = f_ref[r, 48:64].astype(F32)[8:16]
        fe[r, 6:8] = hal[0, 336 + 2 * r : 338 + 2 * r]
        fe[r, 24:26] = hal[1, 336 + 2 * r : 338 + 2 * r]
        se[r, 32:48] = mirror(s_ref[r, 0:16].astype(F32)).astype(BF)
        se[r, 48:64] = mirror(hal[0, 10 + 10 * r : 26 + 10 * r]).astype(BF)
        se[r, 0:16] = mirror(hal[1, 16 + 10 * r : 32 + 10 * r]).astype(BF)
        se[r, 16:32] = mirror(s_ref[r, 48:64].astype(F32)).astype(BF)
    correlate_groups(fe, se, w_ref, band, acc, [(0, 32), (16, 0)])

    def write(ref, base, count=18):
        rims = []
        for r in range(count):
            m = jnp.maximum(acc[base + r], 0.0)
            ref[16 * r : 16 * r + 16] = m[8:24].astype(BF)
            rims += [m[6:8], m[24:26]]
        if count % 4:
            rims.append(jnp.zeros((8, 128), F32))
        at, n = 16 * count, -(-count // 4) * 16
        ref[at : at + n] = jnp.concatenate(rims, axis=0).astype(BF)

    write(z_ref, 14 * (1 - t // 2) + 2)
    o_ref[0:864] = oi_ref[...]
    write(o_ref.at[864:1232], 14 * (t // 2) + 2)
    c_ref[0:576] = ci_ref[...]
    write(c_ref.at[576:816], 8 * (t ^ 1), 12)
    for ref, at in ((z_ref, 368), (c_ref, 816)):
        ref[at : at + 16] = near_ref[...]
        ref[at + 16 : at + 32] = far_ref[...]


def side_rows(t, a_ref, b_ref, top, bot):
    even = lax.rem(t, 2) == 0

    @pl.when(even)
    def _():
        bot[...] = a_ref[384:896].astype(F32)
        top[...] = jnp.where(t == 2, b_ref[384:896].astype(F32), 0.0)

    @pl.when(jnp.logical_not(even))
    def _():
        top[...] = a_ref[384:896].astype(F32)
        bot[...] = jnp.where(t == 1, b_ref[384:896].astype(F32), 0.0)


def edge(t, f, s, a, b, near, far, w_wide, oi, ci):
    return pl.pallas_call(
        edge_kernel,
        out_shape=(jax.ShapeDtypeStruct((400, 128), BF), jax.ShapeDtypeStruct((1232, 128), BF), jax.ShapeDtypeStruct((848, 128), BF)),
        in_specs=[SM] + [VM] * 9,
        out_specs=(VM,) * 3,
        scratch_shapes=[
            pltpu.VMEM((32, 32, 128), F32),
            pltpu.VMEM((32, 64, 128), BF),
            pltpu.VMEM((2, 400, 128), F32),
            pltpu.VMEM((4, 24, 32, 256), BF),
            pltpu.VMEM((36, 32, 128), F32),
        ],
        compiler_params=pltpu.CompilerParams(vmem_limit_bytes=24 << 20),
        cost_estimate=pl.CostEstimate(flops=1000000000, bytes_accessed=1000000, transcendentals=0),
        name="edge",
    )(t, f, s, a, b, near, far, w_wide, oi, ci)


def join_kernel(i_ref, e_ref, one_ref, o_ref):
    o_ref[0:864] = i_ref[...]
    o_ref[864:1264] = e_ref[...]


def join(zi, ze, one):
    return pl.pallas_call(
        join_kernel,
        out_shape=jax.ShapeDtypeStruct((1264, 128), BF),
        in_specs=[VM] * 3,
        out_specs=VM,
        compiler_params=pltpu.CompilerParams(vmem_limit_bytes=8 << 20),
        name="join",
    )(zi, ze, one)


def state_rows(t, a_ref, b_ref, h_ref, hs, top, bot):
    side_rows(t, a_ref, b_ref, top, bot)
    hs[0:512] = top[...]
    hs[2560:3072] = bot[...]
    for i in range(8):
        hs[512 + 256 * i : 768 + 256 * i] = h_ref[i].astype(F32)


def gates(metric_ref, t, x, gw_ref, width, put):
    sides_w = jnp.concatenate([gw_ref[p, q] for q in (0, 2) for p in range(3)], axis=0)
    center_w = jnp.concatenate([gw_ref[p, 1] for p in range(3)], axis=0)
    for i in range(0, 10, 2):
        lhs = jnp.concatenate([x[q, i + p : i + p + 2].reshape(2 * width, 256) for q in (0, 2) for p in range(3)], axis=1)
        sides = jnp.dot(lhs, sides_w, preferred_element_type=F32)
        lhs = jnp.concatenate([x[1, i + p : i + p + 2].reshape(2 * width, 256) for p in range(3)], axis=1)
        center = jnp.dot(lhs, center_w, preferred_element_type=F32)
        for n in range(2):
            cut = slice(width * n, width * n + width)
            gate = center[cut] + sides[cut] * metric_ref[jnp.clip(8 * t + i + n - 1, 0, 31)]
            put(i + n, 0.5 * jnp.tanh(0.5 * gate) + 0.5)


def candidates(metric_ref, t, x, m3s, r, cw_ref, width, put):
    zero = jnp.zeros((256, 128), BF)

    def pair(rr, q):
        first = cw_ref[rr, q] if rr < 3 else zero
        second = cw_ref[rr - 1, q] if rr > 0 else zero
        return jnp.concatenate([first, second], axis=1)

    sides_w = jnp.concatenate([pair(rr, q) for q in (0, 2) for rr in range(4)], axis=0)
    center_w = jnp.concatenate([pair(rr, 1) for rr in range(4)], axis=0)

    def taps(q, row):
        mm = m3s[row + 1] if q == 2 else x[q + 1, row + 1, 0:width, 128:256]
        return [r[q, row], mm]

    def stack(qs, i):
        one = [jnp.concatenate(sum([taps(q, i + k + rr) for q in qs for rr in range(4)], []), axis=1) for k in (0, 2)]
        return jnp.concatenate(one, axis=0)

    for i in range(0, 8, 4):
        sides = jnp.dot(stack((0, 2), i), sides_w, preferred_element_type=F32)
        center = jnp.dot(stack((1,), i), center_w, preferred_element_type=F32)
        for n in range(4):
            cut = (slice(width * (n // 2), width * (n // 2) + width), slice(128 * (n % 2), 128 * (n % 2) + 128))
            put(i + n, jnp.tanh(center[cut] + sides[cut] * metric_ref[8 * t + i + n]))


def piece_row(ref, row, inside, count):
    mid = ref[pl.ds(pl.multiple_of(48 * row, 16), 48)].astype(F32)
    ends = ref[pl.ds(pl.multiple_of(48 * count + 16 * row, 16), 16)].astype(F32)
    if inside is not None:
        mid, ends = jnp.where(inside, mid, 0.0), jnp.where(inside, ends, 0.0)
    return mid, ends


def first_kernel(t_ref, metric_ref, h_ref, a_ref, b_ref, own_ref, mate_ref, zi_ref, gw_ref, cw_ref, out_ref, hs, mf, x, m3s, rf, r, ug, top, bot, rims):
    t = t_ref[0]
    high = t // 2
    base = 112 * high
    state_rows(t, a_ref, b_ref, h_ref, hs, top, bot)
    start = 8 * t - 2 - 14 * high
    odd = lax.rem(t, 2)
    for s, ref, count in ((odd, own_ref, 18), (1 - odd, mate_ref, 12)):
        rims[0:80] = ref[1152:1232].astype(F32) if count == 18 else jnp.pad(ref[768:816].astype(F32), ((0, 32), (0, 0)))
        for i in range(12):
            row, inside = i, None
            if count == 18:
                row = start + i
                inside = (row >= 0) & (row < 18)
                row = jnp.clip(row, 0, 17)
            mid, ends = piece_row(ref, row, inside, count)
            at = 64 * s + 16 * high
            mf[i, pl.ds(at + 8, 48)] = mid
            mf[i, pl.ds(at, 8)] = ends[0:8]
            mf[i, pl.ds(at + 56, 8)] = ends[8:16]

            @pl.when(s != high)
            def _(i=i, row=row, s=s, inside=inside):
                v = rims[pl.ds(4 * row + 2 * s, 2)]
                mf[i, pl.ds(128 - 114 * high, 2)] = v if inside is None else jnp.where(inside, v, 0.0)

    for q in range(3):
        for i in range(12):
            x[q, i, :, 0:128] = hs[pl.ds(256 * i + base + 14 + q, 128)].astype(BF)
            x[q, i, :, 128:256] = mf[i, 14 + q : 142 + q].astype(BF)
    for i in range(12):
        m3s[i] = mf[i, 17:129].astype(BF)

    def put_gate(i, gate):
        rf[i, 0:128] = gate[:, 128:] * hs[pl.ds(256 * (i + 1) + base + 15, 128)]
        if 1 <= i < 9:
            ug[i - 1] = gate[:, 0:128]

    gates(metric_ref, t, x, gw_ref, 128, put_gate)
    for q in range(3):
        for i in range(10):
            r[q, i] = rf[i, q : q + 112].astype(BF)

    def put_new(i, cand):
        u = ug[i, 1:113]
        h = hs[pl.ds(256 * (i + 2) + base + 16, 112)]
        out_ref[i] = ((1.0 - u) * h + u * cand).astype(BF)

    candidates(metric_ref, t, x, m3s, r, cw_ref, 112, put_new)


def first_part(t, metric, h, a, b, own, mate, zi, gw, cw):
    return pl.pallas_call(
        first_kernel,
        out_shape=jax.ShapeDtypeStruct((8, 112, 128), BF),
        in_specs=[SM, SM] + [VM] * 8,
        out_specs=VM,
        scratch_shapes=[
            pltpu.VMEM((3072, 128), F32),
            pltpu.VMEM((12, 152, 128), F32),
            pltpu.VMEM((3, 12, 128, 256), BF),
            pltpu.VMEM((12, 112, 128), BF),
            pltpu.VMEM((10, 136, 128), F32),
            pltpu.VMEM((3, 10, 112, 128), BF),
            pltpu.VMEM((8, 128, 128), F32),
            pltpu.VMEM((512, 128), F32),
            pltpu.VMEM((512, 128), F32),
            pltpu.VMEM((80, 128), F32),
        ],
        compiler_params=pltpu.CompilerParams(vmem_limit_bytes=24 << 20),
        cost_estimate=pl.CostEstimate(flops=4000000000, bytes_accessed=4000000, transcendentals=0),
        name="first_part",
    )(t, metric, h, a, b, own, mate, zi, gw, cw)


def second_kernel(
    t_ref, l_ref, metric_ref, h_ref, a_ref, b_ref, near_ref, far_ref, own_ref, mate_ref, z_ref, k_ref, gw_ref, cw_ref, one_ref, out_ref,
    ob, sem, hs, hf, mf, x, m3s, rf, r, ug, top, bot, rims,
):
    t = t_ref[0]
    high = t // 2
    c0 = pl.multiple_of(128 - 128 * high, 128)
    state_rows(t, a_ref, b_ref, h_ref, hs, top, bot)
    west_even = lax.rem(l_ref[0], 2) == 0
    odd = lax.rem(t, 2)
    low = high == 0

    def twelve(own, at):
        mates, others = mate_ref[816 + at : 832 + at].astype(F32), k_ref[1232 + at : 1248 + at].astype(F32)
        others = jnp.where((t == 1) | (t == 2), others, 0.0)
        above = jnp.where(odd == 1, mates, others)[12:16]
        below = jnp.where(odd == 1, others, mates)[0:4]
        return jnp.concatenate([above, own[...].astype(F32), below], axis=0)

    near, far = twelve(near_ref, 0), twelve(far_ref, 16)
    hr = jnp.where(west_even, near, far)
    hl = jnp.where(west_even, far, near)
    for i in range(12):
        hf[i, 2:130] = hs[pl.ds(256 * i + c0, 128)]
        side_w, side_e = hl[2 * i : 2 * i + 2], hr[2 * i : 2 * i + 2]
        hf[i, 0:2] = jnp.where(low, hs[256 * i + 126 : 256 * i + 128], side_w)
        hf[i, 130:132] = jnp.where(low, side_e, hs[256 * i + 128 : 256 * i + 130])
        hf[i, pl.ds(146 - 2 * high, 18)] = hs[pl.ds(256 * i + 238 * high, 18)]
        hf[i, pl.ds(144 + 18 * high, 2)] = jnp.where(low, side_w, side_e)
    start = 8 * t - 2 - 14 * high
    for s, ref in ((odd, z_ref), (1 - odd, k_ref)):
        rims[0:80] = ref[1152:1232].astype(F32)
        for i in range(12):
            row = start + i
            inside = (row >= 0) & (row < 18)
            row = jnp.clip(row, 0, 17)
            mid = ref[pl.ds(pl.multiple_of(48 * row, 16), 48)].astype(F32)
            ends = ref[pl.ds(pl.multiple_of(864 + 16 * row, 16), 16)].astype(F32)
            mf[i, pl.ds(10 + 64 * s, 48)] = jnp.where(inside, mid, 0.0)
            ends = jnp.where(inside, ends, 0.0)
            mf[i, pl.ds(2 + 64 * s, 8)] = ends[0:8]
            mf[i, pl.ds(58 + 64 * s, 8)] = ends[8:16]
            v = rims[pl.ds(4 * row + 2 * s, 2)]
            mf[i, pl.ds(130 * s, 2)] = jnp.where(inside, v, 0.0)
    mine = odd == high
    mates = jnp.pad(mate_ref[768:816].astype(F32), ((0, 32), (0, 0)))
    rims[0:80] = jnp.where(mine, own_ref[1152:1232].astype(F32), mates)
    for i in range(12):
        row = start + i
        inside = (row >= 0) & (row < 18)
        row = jnp.clip(row, 0, 17)
        at = pl.multiple_of(48 * row + 32 * high, 16)
        mid = jnp.where(inside, own_ref[pl.ds(at, 16)].astype(F32), 0.0)
        at = pl.multiple_of(864 + 16 * row, 16)
        ends = jnp.where(inside, own_ref[pl.ds(at, 16)].astype(F32), 0.0)
        at = pl.multiple_of(48 * i + 32 * high, 16)
        mid = jnp.where(mine, mid, mate_ref[pl.ds(at, 16)].astype(F32))
        ends = jnp.where(mine, ends, mate_ref[576 + 16 * i : 592 + 16 * i].astype(F32))
        mf[i, pl.ds(154 - 10 * high, 10)] = jnp.where(low, mid[0:10], mid[6:16])
        mf[i, pl.ds(146 + 8 * high, 8)] = jnp.where(low, ends[0:8], ends[8:16])
        row = jnp.where(mine, row, i)
        inside = inside | jnp.logical_not(mine)
        v = rims[pl.ds(4 * row + 2 * high, 2)]
        mf[i, pl.ds(144 + 18 * high, 2)] = jnp.where(inside, v, 0.0)
    for q in range(3):
        for i in range(12):
            x[q, i, :, 0:128] = hf[i, q : q + 176].astype(BF)
            x[q, i, :, 128:256] = mf[i, q : q + 176].astype(BF)
    for i in range(12):
        m3s[i] = mf[i, 3:163].astype(BF)

    def put_gate(i, gate):
        rf[i, 0:176] = gate[:, 128:] * hf[i + 1, 1:177]
        if 1 <= i < 9:
            ug[i - 1] = gate[:, 0:128]

    gates(metric_ref, t, x, gw_ref, 176, put_gate)
    for q in range(3):
        for i in range(10):
            r[q, i] = rf[i, q : q + 160].astype(BF)

    def put_new(i, cand):
        u = ug[i, 1:161]
        h = hf[i + 2, 2:162]
        new = ((1.0 - u) * h + u * cand).astype(BF)
        ob[i, pl.ds(c0, 128)] = new[0:128]
        ob[i, pl.ds(pl.multiple_of(240 * high, 16), 16)] = new[144:160]
        ob[i, pl.ds(pl.multiple_of(16 + 112 * high, 16), 112)] = one_ref[i]
        pltpu.make_async_copy(ob.at[i], out_ref.at[i], sem.at[i]).start()

    candidates(metric_ref, t, x, m3s, r, cw_ref, 160, put_new)
    for i in range(8):
        pltpu.make_async_copy(ob.at[i], out_ref.at[i], sem.at[i]).wait()


def second_part(t, l, metric, h, a, b, near, far, own, mate, z, k, gw, cw, one):
    return pl.pallas_call(
        second_kernel,
        out_shape=jax.ShapeDtypeStruct((8, 256, 128), BF),
        in_specs=[SM, SM, SM] + [VM] * 12,
        out_specs=pl.BlockSpec(memory_space=pl.ANY),
        scratch_shapes=[
            pltpu.VMEM((8, 256, 128), BF),
            pltpu.SemaphoreType.DMA((8,)),
            pltpu.VMEM((3072, 128), F32),
            pltpu.VMEM((12, 184, 128), F32),
            pltpu.VMEM((12, 184, 128), F32),
            pltpu.VMEM((3, 12, 176, 256), BF),
            pltpu.VMEM((12, 160, 128), BF),
            pltpu.VMEM((10, 184, 128), F32),
            pltpu.VMEM((3, 10, 160, 128), BF),
            pltpu.VMEM((8, 176, 128), F32),
            pltpu.VMEM((512, 128), F32),
            pltpu.VMEM((512, 128), F32),
            pltpu.VMEM((80, 128), F32),
        ],
        compiler_params=pltpu.CompilerParams(vmem_limit_bytes=24 << 20),
        cost_estimate=pl.CostEstimate(flops=5000000000, bytes_accessed=4000000, transcendentals=0),
        name="second_part",
    )(t, l, metric, h, a, b, near, far, own, mate, z, k, gw, cw, one)


def swaps(n, first):
    pairs = [(i % n, (i + 1) % n) for i in range(first, n, 2)]
    return pairs + [(j, i) for i, j in pairs]


def body(first, second, hidden, encoder_weight, gates_weight, candidate_weight, row_metric):
    t = lax.axis_index("lat").astype(jnp.int32)[None]
    l = lax.axis_index("lon").astype(jnp.int32)[None]
    count = lax.axis_size("lon")
    slabs = count * lax.axis_size("lat")
    core = [(i, i ^ 1) for i in range(4)]
    chip = [(i, i ^ 2) for i in range(4)]

    a_send, b_send, near_send, far_send = pack(t, l, first, second, hidden)
    with jax.named_scope("rim_far"):
        b = lax.ppermute(b_send, BOTH, swaps(slabs, 1))
    with jax.named_scope("rim_near"):
        a = lax.ppermute(a_send, BOTH, swaps(slabs, 0))
    with jax.named_scope("state_near"):
        near = lax.ppermute(near_send, "lon", swaps(count, 0))
    with jax.named_scope("state_far"):
        far = lax.ppermute(far_send, "lon", swaps(count, 1))
    zi_send, oi, ci, w_wide = inner(t, first, second, encoder_weight)
    with jax.named_scope("inner_chip"):
        zi = lax.ppermute(zi_send, "lat", chip)
    ze_send, own, own_send = edge(t, first, second, a, b, near, far, w_wide, oi, ci)
    with jax.named_scope("edge_chip"):
        ze = lax.ppermute(ze_send, "lat", chip)
    with jax.named_scope("own_core"):
        mate = lax.ppermute(own_send, "lat", core)
    one = first_part(t, row_metric, hidden, a, b, own, mate, zi, gates_weight, candidate_weight)
    z = join(zi, ze, one)
    with jax.named_scope("chip_core"):
        k = lax.ppermute(z, "lat", core)
    return second_part(t, l, row_metric, hidden, a, b, near, far, own, mate, z, k, gates_weight, candidate_weight, one)


def solution(mesh):
    return jax.shard_map(
        body,
        mesh=mesh,
        in_specs=(
            P(None, BOTH, None),
            P(None, BOTH, None),
            P("lat", "lon", None),
            P(),
            P(),
            P(),
            P(),
        ),
        out_specs=P("lat", "lon", None),
        check_vma=False,
    )
```

```python
import functools

import jax
import jax.numpy as jnp
from jax import lax
from jax.experimental import pallas as pl
from jax.experimental.pallas import tpu as pltpu
from jax.sharding import PartitionSpec as P

RADIUS, WIN = 8, 17
G, S = 16, 5
BF, F32 = jnp.bfloat16, jnp.float32
NT = (((1,), (1,)), ((), ()))
BOTH = ("lon", "lat")
VM = pl.BlockSpec(memory_space=pltpu.VMEM)
SM = pl.BlockSpec(memory_space=pltpu.SMEM)


def mirror(x):
    n = x.shape[0] // 8
    ids = 7 - lax.broadcasted_iota(jnp.int32, (8, 128), 0)
    tiles = [
        jnp.take_along_axis(x[8 * k : 8 * k + 8], ids, axis=0, mode="promise_in_bounds")
        for k in reversed(range(n))
    ]
    return jnp.concatenate(tiles, axis=0)


def pack_kernel(t_ref, l_ref, f_ref, s_ref, h_ref, a_ref, b_ref, near_ref, far_ref, up, down, sb, fb, hb, cb, sem):
    rows = f_ref.shape[0]
    moves = []
    for n, col in enumerate((48, 0)):
        moves.append((s_ref.at[:, col : col + 16], sb.at[n]))
        moves.append((f_ref.at[:, col : col + 16], fb.at[n]))
        moves.append((h_ref.at[6 - 6 * n : 8 - 6 * n], hb.at[n]))
        moves.append((h_ref.at[:, 240 - 240 * n : 256 - 240 * n], cb.at[n]))
    copies = [pltpu.make_async_copy(a, b, sem.at[k]) for k, (a, b) in enumerate(moves)]
    for c in copies:
        c.start()
    for c in copies:
        c.wait()
    for r in range(rows):
        up[10 * r : 10 * r + 10] = sb[0, r].astype(F32)[6:16]
        down[10 * r : 10 * r + 10] = sb[1, r].astype(F32)[0:10]
        up[320 + 2 * r : 322 + 2 * r] = fb[0, r].astype(F32)[14:16]
        down[320 + 2 * r : 322 + 2 * r] = fb[1, r].astype(F32)[0:2]
    east = jnp.concatenate([cb[0, i].astype(F32)[14:16] for i in range(8)], axis=0)
    west = jnp.concatenate([cb[1, i].astype(F32)[0:2] for i in range(8)], axis=0)
    even = lax.rem(l_ref[0], 2) == 0
    near_ref[...] = jnp.where(even, east, west).astype(BF)
    far_ref[...] = jnp.where(even, west, east).astype(BF)
    even = lax.rem(t_ref[0], 2) == 0

    b_ref[896:912] = jnp.zeros((16, 128), BF)

    def put(n_ref, p_ref):
        n_ref[0:384] = up[...].astype(BF)
        p_ref[0:384] = down[...].astype(BF)
        for i in range(2):
            n_ref[384 + 256 * i : 640 + 256 * i] = hb[0, i]
            p_ref[384 + 256 * i : 640 + 256 * i] = hb[1, i]

    @pl.when(even)
    def _():
        put(a_ref, b_ref)

    @pl.when(jnp.logical_not(even))
    def _():
        put(b_ref, a_ref)


def pack(t, l, f, s, h):
    hbm = pl.BlockSpec(memory_space=pl.ANY)
    return pl.pallas_call(
        pack_kernel,
        out_shape=(pltpu.VMEM((896, 128), BF), pltpu.VMEM((912, 128), BF)) + (pltpu.VMEM((16, 128), BF),) * 2,
        in_specs=[SM, SM, hbm, hbm, hbm],
        out_specs=(VM,) * 4,
        scratch_shapes=[
            pltpu.VMEM((384, 128), F32),
            pltpu.VMEM((384, 128), F32),
            pltpu.VMEM((2, 32, 16, 128), BF),
            pltpu.VMEM((2, 32, 16, 128), BF),
            pltpu.VMEM((2, 2, 256, 128), BF),
            pltpu.VMEM((2, 8, 16, 128), BF),
            pltpu.SemaphoreType.DMA((8,)),
        ],
        name="pack",
    )(t, l, f, s, h)


def correlate_groups(fe, se, w_ref, band, acc, groups):
    rows = fe.shape[0]
    blocks = rows // 8
    width = G * len(groups)
    scale = 128**-0.5
    for n, (fcol, scol) in enumerate(groups):
        for b in range(blocks):
            lo, hi = max(0, 8 * b - 8), min(rows, 8 * b + 16)
            keys = se[8 * b : 8 * b + 8, scol : scol + 32, :].reshape(256, 128)
            query = fe[lo:hi, fcol : fcol + G, :].reshape((hi - lo) * G, 128).astype(BF)
            c = lax.dot_general(query, keys, NT, preferred_element_type=F32)
            c = (c * scale).reshape(hi - lo, G, 256)
            for h in range(2):
                part = pltpu.roll(c[:, :, 128 * h : 128 * h + 128], 0, 2, stride=1, stride_axis=1)
                band[b, lo - 8 * b + 8 : hi - 8 * b + 8, G * n : G * n + G, 128 * h : 128 * h + 128] = part.astype(BF)
    done = set()
    for d in range(-8, 16):
        bs = [b for b in range(blocks) if 0 <= 8 * b + d < rows]
        b0, b1 = bs[0], bs[-1] + 1
        lhs = band[b0:b1, d + 8].reshape((b1 - b0) * width, 256)
        o = 15 - d
        part = jnp.dot(lhs, w_ref[32 * o : 32 * o + 256, :], preferred_element_type=F32)
        part = part.reshape(b1 - b0, width, 128)
        for n, b in enumerate(bs):
            i = 8 * b + d
            if i in done:
                acc[i + 2] += part[n]
            else:
                acc[i + 2] = part[n]
                done.add(i)
    zero = jnp.zeros((2, width, 128), F32)
    acc[0:2] = zero
    acc[rows + 2 : rows + 4] = zero


def widen(enc_ref, wide_ref, enc, wide):
    wide[...] = jnp.zeros(wide.shape, F32)
    enc[0:8] = jnp.zeros((8, 128), F32)
    enc[8:297] = enc_ref[...].astype(F32)
    for a in range(WIN):
        at = 32 * (a + 7) + 15
        wide[at : at + 17] = mirror(enc[17 * a + 1 : 17 * a + 25])[0:17]
    wide_ref[...] = wide[...].astype(BF)


def inner_kernel(t_ref, f_ref, s_ref, enc_ref, z_ref, o_ref, c_ref, w_ref, fe, se, band, acc, enc, wide):
    widen(enc_ref, w_ref, enc, wide)
    for r in range(f_ref.shape[0]):
        fe[r] = f_ref[r].astype(F32)
        se[r] = mirror(s_ref[r].astype(F32)).astype(BF)
    correlate_groups(fe, se, w_ref, band, acc, [(8 + G * g, 32 - G * g) for g in range(3)])
    high = t_ref[0] // 2
    for base, ref in ((14 * (1 - high) + 2, z_ref), (14 * high + 2, o_ref)):
        for r in range(18):
            ref[48 * r : 48 * r + 48] = jnp.maximum(acc[base + r], 0.0).astype(BF)
    base = 8 * (t_ref[0] ^ 1)
    for r in range(12):
        c_ref[48 * r : 48 * r + 48] = jnp.maximum(acc[base + r], 0.0).astype(BF)


def inner(t, f, s, enc):
    return pl.pallas_call(
        inner_kernel,
        out_shape=(jax.ShapeDtypeStruct((864, 128), BF),) * 2 + (jax.ShapeDtypeStruct((576, 128), BF), jax.ShapeDtypeStruct((992, 128), BF)),
        in_specs=[SM] + [VM] * 3,
        out_specs=(VM,) * 4,
        scratch_shapes=[
            pltpu.VMEM((32, 64, 128), F32),
            pltpu.VMEM((32, 64, 128), BF),
            pltpu.VMEM((4, 24, 48, 256), BF),
            pltpu.VMEM((36, 48, 128), F32),
            pltpu.VMEM((304, 128), F32),
            pltpu.VMEM((992, 128), F32),
        ],
        compiler_params=pltpu.CompilerParams(vmem_limit_bytes=24 << 20),
        cost_estimate=pl.CostEstimate(flops=1000000000, bytes_accessed=1000000, transcendentals=0),
        name="inner",
    )(t, f, s, enc)


def edge_kernel(t_ref, f_ref, s_ref, a_ref, b_ref, near_ref, far_ref, w_ref, oi_ref, ci_ref, state_ref, z_ref, o_ref, c_ref, fe, se, hal, band, acc):
    t = t_ref[0]
    odd = lax.rem(t, 2)
    for n, ref in ((1 - odd, a_ref), (odd, b_ref)):
        hal[n, 0:16] = jnp.zeros((16, 128), F32)
        hal[n, 16:400] = ref[0:384].astype(F32)
    fpad = jnp.zeros((8, 128), F32)
    for r in range(f_ref.shape[0]):
        fe[r, 0:8] = fpad
        fe[r, 24:32] = fpad
        fe[r, 8:16] = f_ref[r, 0:16].astype(F32)[0:8]
        fe[r, 16:24] = f_ref[r, 48:64].astype(F32)[8:16]
        fe[r, 6:8] = hal[0, 336 + 2 * r : 338 + 2 * r]
        fe[r, 24:26] = hal[1, 336 + 2 * r : 338 + 2 * r]
        se[r, 32:48] = mirror(s_ref[r, 0:16].astype(F32)).astype(BF)
        se[r, 48:64] = mirror(hal[0, 10 + 10 * r : 26 + 10 * r]).astype(BF)
        se[r, 0:16] = mirror(hal[1, 16 + 10 * r : 32 + 10 * r]).astype(BF)
        se[r, 16:32] = mirror(s_ref[r, 48:64].astype(F32)).astype(BF)
    correlate_groups(fe, se, w_ref, band, acc, [(0, 32), (16, 0)])

    def write(ref, base, count=18):
        rims = []
        for r in range(count):
            m = jnp.maximum(acc[base + r], 0.0)
            ref[16 * r : 16 * r + 16] = m[8:24].astype(BF)
            rims += [m[6:8], m[24:26]]
        if count % 4:
            rims.append(jnp.zeros((8, 128), F32))
        at, n = 16 * count, -(-count // 4) * 16
        ref[at : at + n] = jnp.concatenate(rims, axis=0).astype(BF)

    write(z_ref, 14 * (1 - t // 2) + 2)
    o_ref[0:864] = oi_ref[...]
    write(o_ref.at[864:1232], 14 * (t // 2) + 2)
    c_ref[0:576] = ci_ref[...]
    write(c_ref.at[576:816], 8 * (t ^ 1), 12)
    for ref, at in ((z_ref, 368), (c_ref, 816)):
        ref[at : at + 16] = near_ref[...]
        ref[at + 16 : at + 32] = far_ref[...]


def side_rows(t, a_ref, b_ref, top, bot):
    even = lax.rem(t, 2) == 0

    @pl.when(even)
    def _():
        bot[...] = a_ref[384:896].astype(F32)
        top[...] = jnp.where(t == 2, b_ref[384:896].astype(F32), 0.0)

    @pl.when(jnp.logical_not(even))
    def _():
        top[...] = a_ref[384:896].astype(F32)
        bot[...] = jnp.where(t == 1, b_ref[384:896].astype(F32), 0.0)


def edge(t, f, s, a, b, near, far, w_wide, oi, ci, state):
    return pl.pallas_call(
        edge_kernel,
        out_shape=(jax.ShapeDtypeStruct((400, 128), BF), jax.ShapeDtypeStruct((1232, 128), BF), jax.ShapeDtypeStruct((848, 128), BF)),
        in_specs=[SM] + [VM] * 10,
        out_specs=(VM,) * 3,
        scratch_shapes=[
            pltpu.VMEM((32, 32, 128), F32),
            pltpu.VMEM((32, 64, 128), BF),
            pltpu.VMEM((2, 400, 128), F32),
            pltpu.VMEM((4, 24, 32, 256), BF),
            pltpu.VMEM((36, 32, 128), F32),
        ],
        compiler_params=pltpu.CompilerParams(vmem_limit_bytes=24 << 20),
        cost_estimate=pl.CostEstimate(flops=1000000000, bytes_accessed=1000000, transcendentals=0),
        name="edge",
    )(t, f, s, a, b, near, far, w_wide, oi, ci, state)


def join_kernel(i_ref, e_ref, one_ref, o_ref):
    o_ref[0:864] = i_ref[...]
    o_ref[864:1264] = e_ref[...]


def join(zi, ze, one):
    return pl.pallas_call(
        join_kernel,
        out_shape=jax.ShapeDtypeStruct((1264, 128), BF),
        in_specs=[VM] * 3,
        out_specs=VM,
        compiler_params=pltpu.CompilerParams(vmem_limit_bytes=8 << 20),
        name="join",
    )(zi, ze, one)


def state_rows(t, a_ref, b_ref, h_ref, hs, top, bot):
    side_rows(t, a_ref, b_ref, top, bot)
    hs[0:512] = top[...]
    hs[2560:3072] = bot[...]
    for i in range(8):
        hs[512 + 256 * i : 768 + 256 * i] = h_ref[i].astype(F32)


def gate_products(x, gw_ref, width, i, lanes):
    def part(qs):
        lhs = jnp.concatenate([x[q, i + p : i + p + 2, :, lanes[0]].reshape(2 * width, -1) for q in qs for p in range(3)], axis=1)
        rhs = jnp.concatenate([gw_ref[p, q, lanes[1]] for q in qs for p in range(3)], axis=0)
        return jnp.dot(lhs, rhs, preferred_element_type=F32)

    return part((0, 2)), part((1,))


def gates(metric_ref, t, x, gw_ref, state_ref, width, put):
    for i in range(0, 10, 2):
        known = 2 <= i < 8
        half = slice(128, 256)
        sides, center = gate_products(x, gw_ref, width, i, (half, half) if known else (slice(0, 256), slice(0, 256)))
        for n in range(2):
            cut = slice(width * n, width * n + width)
            gate = center[cut] + sides[cut] * metric_ref[jnp.clip(8 * t + i + n - 1, 0, 31)]
            if known:
                gate = gate + state_ref[i + n - 2]
            put(i + n, 0.5 * jnp.tanh(0.5 * gate) + 0.5)


def state_products(metric_ref, t, x, gw_ref, width, out):
    for i in range(0, 6, 2):
        sides, center = gate_products(x, gw_ref, width, i, (slice(0, 128), slice(0, 128)))
        for n in range(2):
            cut = slice(width * n, width * n + width)
            out[i + n] = center[cut] + sides[cut] * metric_ref[8 * t + i + n + 1]


def state_first_kernel(t_ref, metric_ref, h_ref, gw_ref, out_ref, hs, x):
    t = t_ref[0]
    for i in range(8):
        hs[256 * i : 256 * i + 256] = h_ref[i].astype(F32)
    for q in range(3):
        for i in range(8):
            x[q, i] = hs[pl.ds(256 * i + 112 * (t // 2) + 14 + q, 128)].astype(BF)
    state_products(metric_ref, t, x, gw_ref, 128, out_ref)


def state_second_kernel(t_ref, l_ref, metric_ref, h_ref, near_ref, far_ref, gw_ref, out_ref, hs, hf, x):
    t = t_ref[0]
    high = t // 2
    c0 = pl.multiple_of(128 - 128 * high, 128)
    west_even = lax.rem(l_ref[0], 2) == 0
    near, far = near_ref[...].astype(F32), far_ref[...].astype(F32)
    hr = jnp.where(west_even, near, far)
    hl = jnp.where(west_even, far, near)
    for i in range(8):
        hs[256 * i : 256 * i + 256] = h_ref[i].astype(F32)
    for i in range(8):
        outer(hf, hs, i, c0, high, hl[2 * i : 2 * i + 2], hr[2 * i : 2 * i + 2])
    for q in range(3):
        for i in range(8):
            x[q, i] = hf[i, q : q + 176].astype(BF)
    state_products(metric_ref, t, x, gw_ref, 176, out_ref)


def outer(hf, hs, i, c0, high, side_w, side_e):
    low = high == 0
    hf[i, 2:130] = hs[pl.ds(256 * i + c0, 128)]
    hf[i, 0:2] = jnp.where(low, hs[256 * i + 126 : 256 * i + 128], side_w)
    hf[i, 130:132] = jnp.where(low, side_e, hs[256 * i + 128 : 256 * i + 130])
    hf[i, pl.ds(146 - 2 * high, 18)] = hs[pl.ds(256 * i + 238 * high, 18)]
    hf[i, pl.ds(144 + 18 * high, 2)] = jnp.where(low, side_w, side_e)


def state_first(t, metric, h, gw):
    return pl.pallas_call(
        state_first_kernel,
        out_shape=jax.ShapeDtypeStruct((6, 128, 256), F32),
        in_specs=[SM, SM] + [VM] * 2,
        out_specs=VM,
        scratch_shapes=[pltpu.VMEM((2048, 128), F32), pltpu.VMEM((3, 8, 128, 128), BF)],
        compiler_params=pltpu.CompilerParams(vmem_limit_bytes=24 << 20),
        cost_estimate=pl.CostEstimate(flops=10**9, bytes_accessed=2 << 20, transcendentals=0),
        name="state_first",
    )(t, metric, h, gw)


def state_second(t, l, metric, h, near, far, gw):
    return pl.pallas_call(
        state_second_kernel,
        out_shape=jax.ShapeDtypeStruct((6, 176, 256), F32),
        in_specs=[SM, SM, SM] + [VM] * 4,
        out_specs=VM,
        scratch_shapes=[pltpu.VMEM((2048, 128), F32), pltpu.VMEM((8, 184, 128), F32), pltpu.VMEM((3, 8, 176, 128), BF)],
        compiler_params=pltpu.CompilerParams(vmem_limit_bytes=24 << 20),
        cost_estimate=pl.CostEstimate(flops=10**9, bytes_accessed=2 << 20, transcendentals=0),
        name="state_second",
    )(t, l, metric, h, near, far, gw)


def candidates(metric_ref, t, x, m3s, r, cw_ref, width, put):
    zero = jnp.zeros((256, 128), BF)

    def pair(rr, q):
        first = cw_ref[rr, q] if rr < 3 else zero
        second = cw_ref[rr - 1, q] if rr > 0 else zero
        return jnp.concatenate([first, second], axis=1)

    sides_w = jnp.concatenate([pair(rr, q) for q in (0, 2) for rr in range(4)], axis=0)
    center_w = jnp.concatenate([pair(rr, 1) for rr in range(4)], axis=0)

    def taps(q, row):
        mm = m3s[row + 1] if q == 2 else x[q + 1, row + 1, 0:width, 128:256]
        return [r[q, row], mm]

    def stack(qs, i):
        one = [jnp.concatenate(sum([taps(q, i + k + rr) for q in qs for rr in range(4)], []), axis=1) for k in (0, 2)]
        return jnp.concatenate(one, axis=0)

    for i in range(0, 8, 4):
        sides = jnp.dot(stack((0, 2), i), sides_w, preferred_element_type=F32)
        center = jnp.dot(stack((1,), i), center_w, preferred_element_type=F32)
        for n in range(4):
            cut = (slice(width * (n // 2), width * (n // 2) + width), slice(128 * (n % 2), 128 * (n % 2) + 128))
            put(i + n, jnp.tanh(center[cut] + sides[cut] * metric_ref[8 * t + i + n]))


def piece_row(ref, row, inside, count):
    mid = ref[pl.ds(pl.multiple_of(48 * row, 16), 48)].astype(F32)
    ends = ref[pl.ds(pl.multiple_of(48 * count + 16 * row, 16), 16)].astype(F32)
    if inside is not None:
        mid, ends = jnp.where(inside, mid, 0.0), jnp.where(inside, ends, 0.0)
    return mid, ends


def first_kernel(t_ref, metric_ref, h_ref, a_ref, b_ref, own_ref, mate_ref, state_ref, gw_ref, cw_ref, out_ref, hs, mf, x, m3s, rf, r, ug, top, bot, rims):
    t = t_ref[0]
    high = t // 2
    base = 112 * high
    state_rows(t, a_ref, b_ref, h_ref, hs, top, bot)
    start = 8 * t - 2 - 14 * high
    odd = lax.rem(t, 2)
    for s, ref, count in ((odd, own_ref, 18), (1 - odd, mate_ref, 12)):
        rims[0:80] = ref[1152:1232].astype(F32) if count == 18 else jnp.pad(ref[768:816].astype(F32), ((0, 32), (0, 0)))
        for i in range(12):
            row, inside = i, None
            if count == 18:
                row = start + i
                inside = (row >= 0) & (row < 18)
                row = jnp.clip(row, 0, 17)
            mid, ends = piece_row(ref, row, inside, count)
            at = 64 * s + 16 * high
            mf[i, pl.ds(at + 8, 48)] = mid
            mf[i, pl.ds(at, 8)] = ends[0:8]
            mf[i, pl.ds(at + 56, 8)] = ends[8:16]

            @pl.when(s != high)
            def _(i=i, row=row, s=s, inside=inside):
                v = rims[pl.ds(4 * row + 2 * s, 2)]
                mf[i, pl.ds(128 - 114 * high, 2)] = v if inside is None else jnp.where(inside, v, 0.0)

    for q in range(3):
        for i in range(12):
            if not 4 <= i < 8:
                x[q, i, :, 0:128] = hs[pl.ds(256 * i + base + 14 + q, 128)].astype(BF)
            x[q, i, :, 128:256] = mf[i, 14 + q : 142 + q].astype(BF)
    for i in range(12):
        m3s[i] = mf[i, 17:129].astype(BF)

    def put_gate(i, gate):
        rf[i, 0:128] = gate[:, 128:] * hs[pl.ds(256 * (i + 1) + base + 15, 128)]
        if 1 <= i < 9:
            ug[i - 1] = gate[:, 0:128]

    gates(metric_ref, t, x, gw_ref, state_ref, 128, put_gate)
    for q in range(3):
        for i in range(10):
            r[q, i] = rf[i, q : q + 112].astype(BF)

    def put_new(i, cand):
        u = ug[i, 1:113]
        h = hs[pl.ds(256 * (i + 2) + base + 16, 112)]
        out_ref[i] = ((1.0 - u) * h + u * cand).astype(BF)

    candidates(metric_ref, t, x, m3s, r, cw_ref, 112, put_new)


def first_part(t, metric, h, a, b, own, mate, state, gw, cw):
    return pl.pallas_call(
        first_kernel,
        out_shape=jax.ShapeDtypeStruct((8, 112, 128), BF),
        in_specs=[SM, SM] + [VM] * 8,
        out_specs=VM,
        scratch_shapes=[
            pltpu.VMEM((3072, 128), F32),
            pltpu.VMEM((12, 152, 128), F32),
            pltpu.VMEM((3, 12, 128, 256), BF),
            pltpu.VMEM((12, 112, 128), BF),
            pltpu.VMEM((10, 136, 128), F32),
            pltpu.VMEM((3, 10, 112, 128), BF),
            pltpu.VMEM((8, 128, 128), F32),
            pltpu.VMEM((512, 128), F32),
            pltpu.VMEM((512, 128), F32),
            pltpu.VMEM((80, 128), F32),
        ],
        compiler_params=pltpu.CompilerParams(vmem_limit_bytes=24 << 20),
        cost_estimate=pl.CostEstimate(flops=10**7, bytes_accessed=10**5, transcendentals=0),
        name="first_part",
    )(t, metric, h, a, b, own, mate, state, gw, cw)


def second_kernel(
    t_ref, l_ref, metric_ref, h_ref, a_ref, b_ref, near_ref, far_ref, own_ref, mate_ref, z_ref, k_ref, state_ref, gw_ref, cw_ref, one_ref, out_ref,
    ob, sem, hs, hf, mf, x, m3s, rf, r, ug, top, bot, rims,
):
    t = t_ref[0]
    high = t // 2
    c0 = pl.multiple_of(128 - 128 * high, 128)
    state_rows(t, a_ref, b_ref, h_ref, hs, top, bot)
    west_even = lax.rem(l_ref[0], 2) == 0
    odd = lax.rem(t, 2)
    low = high == 0

    def twelve(own, at):
        mates, others = mate_ref[816 + at : 832 + at].astype(F32), k_ref[1232 + at : 1248 + at].astype(F32)
        others = jnp.where((t == 1) | (t == 2), others, 0.0)
        above = jnp.where(odd == 1, mates, others)[12:16]
        below = jnp.where(odd == 1, others, mates)[0:4]
        return jnp.concatenate([above, own[...].astype(F32), below], axis=0)

    near, far = twelve(near_ref, 0), twelve(far_ref, 16)
    hr = jnp.where(west_even, near, far)
    hl = jnp.where(west_even, far, near)
    for i in range(12):
        outer(hf, hs, i, c0, high, hl[2 * i : 2 * i + 2], hr[2 * i : 2 * i + 2])
    start = 8 * t - 2 - 14 * high
    for s, ref in ((odd, z_ref), (1 - odd, k_ref)):
        rims[0:80] = ref[1152:1232].astype(F32)
        for i in range(12):
            row = start + i
            inside = (row >= 0) & (row < 18)
            row = jnp.clip(row, 0, 17)
            mid = ref[pl.ds(pl.multiple_of(48 * row, 16), 48)].astype(F32)
            ends = ref[pl.ds(pl.multiple_of(864 + 16 * row, 16), 16)].astype(F32)
            mf[i, pl.ds(10 + 64 * s, 48)] = jnp.where(inside, mid, 0.0)
            ends = jnp.where(inside, ends, 0.0)
            mf[i, pl.ds(2 + 64 * s, 8)] = ends[0:8]
            mf[i, pl.ds(58 + 64 * s, 8)] = ends[8:16]
            v = rims[pl.ds(4 * row + 2 * s, 2)]
            mf[i, pl.ds(130 * s, 2)] = jnp.where(inside, v, 0.0)
    mine = odd == high
    mates = jnp.pad(mate_ref[768:816].astype(F32), ((0, 32), (0, 0)))
    rims[0:80] = jnp.where(mine, own_ref[1152:1232].astype(F32), mates)
    for i in range(12):
        row = start + i
        inside = (row >= 0) & (row < 18)
        row = jnp.clip(row, 0, 17)
        at = pl.multiple_of(48 * row + 32 * high, 16)
        mid = jnp.where(inside, own_ref[pl.ds(at, 16)].astype(F32), 0.0)
        at = pl.multiple_of(864 + 16 * row, 16)
        ends = jnp.where(inside, own_ref[pl.ds(at, 16)].astype(F32), 0.0)
        at = pl.multiple_of(48 * i + 32 * high, 16)
        mid = jnp.where(mine, mid, mate_ref[pl.ds(at, 16)].astype(F32))
        ends = jnp.where(mine, ends, mate_ref[576 + 16 * i : 592 + 16 * i].astype(F32))
        mf[i, pl.ds(154 - 10 * high, 10)] = jnp.where(low, mid[0:10], mid[6:16])
        mf[i, pl.ds(146 + 8 * high, 8)] = jnp.where(low, ends[0:8], ends[8:16])
        row = jnp.where(mine, row, i)
        inside = inside | jnp.logical_not(mine)
        v = rims[pl.ds(4 * row + 2 * high, 2)]
        mf[i, pl.ds(144 + 18 * high, 2)] = jnp.where(inside, v, 0.0)
    for q in range(3):
        for i in range(12):
            if not 4 <= i < 8:
                x[q, i, :, 0:128] = hf[i, q : q + 176].astype(BF)
            x[q, i, :, 128:256] = mf[i, q : q + 176].astype(BF)
    for i in range(12):
        m3s[i] = mf[i, 3:163].astype(BF)

    def put_gate(i, gate):
        rf[i, 0:176] = gate[:, 128:] * hf[i + 1, 1:177]
        if 1 <= i < 9:
            ug[i - 1] = gate[:, 0:128]

    gates(metric_ref, t, x, gw_ref, state_ref, 176, put_gate)
    for q in range(3):
        for i in range(10):
            r[q, i] = rf[i, q : q + 160].astype(BF)

    def put_new(i, cand):
        u = ug[i, 1:161]
        h = hf[i + 2, 2:162]
        new = ((1.0 - u) * h + u * cand).astype(BF)
        ob[i, pl.ds(c0, 128)] = new[0:128]
        ob[i, pl.ds(pl.multiple_of(240 * high, 16), 16)] = new[144:160]
        ob[i, pl.ds(pl.multiple_of(16 + 112 * high, 16), 112)] = one_ref[i]
        pltpu.make_async_copy(ob.at[i], out_ref.at[i], sem.at[i]).start()

    candidates(metric_ref, t, x, m3s, r, cw_ref, 160, put_new)
    for i in range(8):
        pltpu.make_async_copy(ob.at[i], out_ref.at[i], sem.at[i]).wait()


def second_part(t, l, metric, h, a, b, near, far, own, mate, z, k, state, gw, cw, one):
    return pl.pallas_call(
        second_kernel,
        out_shape=jax.ShapeDtypeStruct((8, 256, 128), BF),
        in_specs=[SM, SM, SM] + [VM] * 13,
        out_specs=pl.BlockSpec(memory_space=pl.ANY),
        scratch_shapes=[
            pltpu.VMEM((8, 256, 128), BF),
            pltpu.SemaphoreType.DMA((8,)),
            pltpu.VMEM((3072, 128), F32),
            pltpu.VMEM((12, 184, 128), F32),
            pltpu.VMEM((12, 184, 128), F32),
            pltpu.VMEM((3, 12, 176, 256), BF),
            pltpu.VMEM((12, 160, 128), BF),
            pltpu.VMEM((10, 184, 128), F32),
            pltpu.VMEM((3, 10, 160, 128), BF),
            pltpu.VMEM((8, 176, 128), F32),
            pltpu.VMEM((512, 128), F32),
            pltpu.VMEM((512, 128), F32),
            pltpu.VMEM((80, 128), F32),
        ],
        compiler_params=pltpu.CompilerParams(vmem_limit_bytes=24 << 20),
        cost_estimate=pl.CostEstimate(flops=5000000000, bytes_accessed=4000000, transcendentals=0),
        name="second_part",
    )(t, l, metric, h, a, b, near, far, own, mate, z, k, state, gw, cw, one)


def swaps(n, first):
    pairs = [(i % n, (i + 1) % n) for i in range(first, n, 2)]
    return pairs + [(j, i) for i, j in pairs]


def body(first, second, hidden, encoder_weight, gates_weight, candidate_weight, row_metric):
    t = lax.axis_index("lat").astype(jnp.int32)[None]
    l = lax.axis_index("lon").astype(jnp.int32)[None]
    count = lax.axis_size("lon")
    slabs = count * lax.axis_size("lat")
    core = [(i, i ^ 1) for i in range(4)]
    chip = [(i, i ^ 2) for i in range(4)]

    a_send, b_send, near_send, far_send = pack(t, l, first, second, hidden)
    with jax.named_scope("rim_far"):
        b = lax.ppermute(b_send, BOTH, swaps(slabs, 1))
    with jax.named_scope("rim_near"):
        a = lax.ppermute(a_send, BOTH, swaps(slabs, 0))
    with jax.named_scope("state_near"):
        near = lax.ppermute(near_send, "lon", swaps(count, 0))
    with jax.named_scope("state_far"):
        far = lax.ppermute(far_send, "lon", swaps(count, 1))
    zi_send, oi, ci, w_wide = inner(t, first, second, encoder_weight)
    with jax.named_scope("inner_chip"):
        zi = lax.ppermute(zi_send, "lat", chip)
    state_one = state_first(t, row_metric, hidden, gates_weight)
    state_two = state_second(t, l, row_metric, hidden, near, far, gates_weight)
    ze_send, own, own_send = edge(t, first, second, a, b, near, far, w_wide, oi, ci, state_one)
    with jax.named_scope("edge_chip"):
        ze = lax.ppermute(ze_send, "lat", chip)
    with jax.named_scope("own_core"):
        mate = lax.ppermute(own_send, "lat", core)
    one = first_part(t, row_metric, hidden, a, b, own, mate, state_one, gates_weight, candidate_weight)
    z = join(zi, ze, one)
    with jax.named_scope("chip_core"):
        k = lax.ppermute(z, "lat", core)
    return second_part(t, l, row_metric, hidden, a, b, near, far, own, mate, z, k, state_two, gates_weight, candidate_weight, one)


def solution(mesh):
    return jax.shard_map(
        body,
        mesh=mesh,
        in_specs=(
            P(None, BOTH, None),
            P(None, BOTH, None),
            P("lat", "lon", None),
            P(),
            P(),
            P(),
            P(),
        ),
        out_specs=P("lat", "lon", None),
        check_vma=False,
    )
```

```python
import functools

import jax
import jax.numpy as jnp
from jax import lax
from jax.experimental import pallas as pl
from jax.experimental.pallas import tpu as pltpu
from jax.sharding import PartitionSpec as P

RADIUS, WIN = 8, 17
G, S = 16, 5
BF, F32 = jnp.bfloat16, jnp.float32
NT = (((1,), (1,)), ((), ()))
BOTH = ("lon", "lat")
VM = pl.BlockSpec(memory_space=pltpu.VMEM)
SM = pl.BlockSpec(memory_space=pltpu.SMEM)


def mirror(x):
    n = x.shape[0] // 8
    ids = 7 - lax.broadcasted_iota(jnp.int32, (8, 128), 0)
    tiles = [
        jnp.take_along_axis(x[8 * k : 8 * k + 8], ids, axis=0, mode="promise_in_bounds")
        for k in reversed(range(n))
    ]
    return jnp.concatenate(tiles, axis=0)


def pack_kernel(t_ref, l_ref, f_ref, s_ref, h_ref, a_ref, b_ref, near_ref, far_ref, up, down, sb, fb, hb, cb, sem):
    rows = f_ref.shape[0]
    moves = []
    for n, col in enumerate((48, 0)):
        moves.append((s_ref.at[:, col : col + 16], sb.at[n]))
        moves.append((f_ref.at[:, col : col + 16], fb.at[n]))
        moves.append((h_ref.at[6 - 6 * n : 8 - 6 * n], hb.at[n]))
        moves.append((h_ref.at[:, 240 - 240 * n : 256 - 240 * n], cb.at[n]))
    copies = [pltpu.make_async_copy(a, b, sem.at[k]) for k, (a, b) in enumerate(moves)]
    for c in copies:
        c.start()
    for c in copies:
        c.wait()
    for r in range(rows):
        up[10 * r : 10 * r + 10] = sb[0, r].astype(F32)[6:16]
        down[10 * r : 10 * r + 10] = sb[1, r].astype(F32)[0:10]
        up[320 + 2 * r : 322 + 2 * r] = fb[0, r].astype(F32)[14:16]
        down[320 + 2 * r : 322 + 2 * r] = fb[1, r].astype(F32)[0:2]
    east = jnp.concatenate([cb[0, i].astype(F32)[14:16] for i in range(8)], axis=0)
    west = jnp.concatenate([cb[1, i].astype(F32)[0:2] for i in range(8)], axis=0)
    even = lax.rem(l_ref[0], 2) == 0
    near_ref[...] = jnp.where(even, east, west).astype(BF)
    far_ref[...] = jnp.where(even, west, east).astype(BF)
    even = lax.rem(t_ref[0], 2) == 0

    b_ref[896:912] = jnp.zeros((16, 128), BF)

    def put(n_ref, p_ref):
        n_ref[0:384] = up[...].astype(BF)
        p_ref[0:384] = down[...].astype(BF)
        for i in range(2):
            n_ref[384 + 256 * i : 640 + 256 * i] = hb[0, i]
            p_ref[384 + 256 * i : 640 + 256 * i] = hb[1, i]

    @pl.when(even)
    def _():
        put(a_ref, b_ref)

    @pl.when(jnp.logical_not(even))
    def _():
        put(b_ref, a_ref)


def pack(t, l, f, s, h):
    hbm = pl.BlockSpec(memory_space=pl.ANY)
    return pl.pallas_call(
        pack_kernel,
        out_shape=(pltpu.VMEM((896, 128), BF), pltpu.VMEM((912, 128), BF)) + (pltpu.VMEM((16, 128), BF),) * 2,
        in_specs=[SM, SM, hbm, hbm, hbm],
        out_specs=(VM,) * 4,
        scratch_shapes=[
            pltpu.VMEM((384, 128), F32),
            pltpu.VMEM((384, 128), F32),
            pltpu.VMEM((2, 32, 16, 128), BF),
            pltpu.VMEM((2, 32, 16, 128), BF),
            pltpu.VMEM((2, 2, 256, 128), BF),
            pltpu.VMEM((2, 8, 16, 128), BF),
            pltpu.SemaphoreType.DMA((8,)),
        ],
        name="pack",
    )(t, l, f, s, h)


def correlate_groups(fe, se, w_ref, band, acc, groups):
    rows = fe.shape[0]
    blocks = rows // 8
    width = G * len(groups)
    scale = 128**-0.5
    for n, (fcol, scol) in enumerate(groups):
        for b in range(blocks):
            lo, hi = max(0, 8 * b - 8), min(rows, 8 * b + 16)
            keys = se[8 * b : 8 * b + 8, scol : scol + 32, :].reshape(256, 128)
            query = fe[lo:hi, fcol : fcol + G, :].reshape((hi - lo) * G, 128).astype(BF)
            c = lax.dot_general(query, keys, NT, preferred_element_type=F32)
            c = (c * scale).reshape(hi - lo, G, 256)
            for h in range(2):
                part = pltpu.roll(c[:, :, 128 * h : 128 * h + 128], 0, 2, stride=1, stride_axis=1)
                band[b, lo - 8 * b + 8 : hi - 8 * b + 8, G * n : G * n + G, 128 * h : 128 * h + 128] = part.astype(BF)
    done = set()
    for d in range(-8, 16):
        bs = [b for b in range(blocks) if 0 <= 8 * b + d < rows]
        b0, b1 = bs[0], bs[-1] + 1
        lhs = band[b0:b1, d + 8].reshape((b1 - b0) * width, 256)
        o = 15 - d
        part = jnp.dot(lhs, w_ref[32 * o : 32 * o + 256, :], preferred_element_type=F32)
        part = part.reshape(b1 - b0, width, 128)
        for n, b in enumerate(bs):
            i = 8 * b + d
            if i in done:
                acc[i + 2] += part[n]
            else:
                acc[i + 2] = part[n]
                done.add(i)
    zero = jnp.zeros((2, width, 128), F32)
    acc[0:2] = zero
    acc[rows + 2 : rows + 4] = zero


def widen(enc_ref, wide_ref, enc, wide):
    wide[...] = jnp.zeros(wide.shape, F32)
    enc[0:8] = jnp.zeros((8, 128), F32)
    enc[8:297] = enc_ref[...].astype(F32)
    for a in range(WIN):
        at = 32 * (a + 7) + 15
        wide[at : at + 17] = mirror(enc[17 * a + 1 : 17 * a + 25])[0:17]
    wide_ref[...] = wide[...].astype(BF)


def inner_kernel(t_ref, f_ref, s_ref, enc_ref, z_ref, o_ref, c_ref, w_ref, fe, se, band, acc, enc, wide):
    widen(enc_ref, w_ref, enc, wide)
    for r in range(f_ref.shape[0]):
        fe[r] = f_ref[r].astype(F32)
        se[r] = mirror(s_ref[r].astype(F32)).astype(BF)
    correlate_groups(fe, se, w_ref, band, acc, [(8 + G * g, 32 - G * g) for g in range(3)])
    high = t_ref[0] // 2
    for base, ref in ((14 * (1 - high) + 2, z_ref), (14 * high + 2, o_ref)):
        for r in range(18):
            ref[48 * r : 48 * r + 48] = jnp.maximum(acc[base + r], 0.0).astype(BF)
    base = 8 * (t_ref[0] ^ 1)
    for r in range(12):
        c_ref[48 * r : 48 * r + 48] = jnp.maximum(acc[base + r], 0.0).astype(BF)


def inner(t, f, s, enc):
    return pl.pallas_call(
        inner_kernel,
        out_shape=(jax.ShapeDtypeStruct((864, 128), BF),) * 2 + (jax.ShapeDtypeStruct((576, 128), BF), jax.ShapeDtypeStruct((992, 128), BF)),
        in_specs=[SM] + [VM] * 3,
        out_specs=(VM,) * 4,
        scratch_shapes=[
            pltpu.VMEM((32, 64, 128), F32),
            pltpu.VMEM((32, 64, 128), BF),
            pltpu.VMEM((4, 24, 48, 256), BF),
            pltpu.VMEM((36, 48, 128), F32),
            pltpu.VMEM((304, 128), F32),
            pltpu.VMEM((992, 128), F32),
        ],
        compiler_params=pltpu.CompilerParams(vmem_limit_bytes=24 << 20),
        cost_estimate=pl.CostEstimate(flops=1000000000, bytes_accessed=1000000, transcendentals=0),
        name="inner",
    )(t, f, s, enc)


def edge_kernel(t_ref, f_ref, s_ref, a_ref, b_ref, near_ref, far_ref, w_ref, oi_ref, ci_ref, state_ref, z_ref, o_ref, c_ref, fe, se, hal, band, acc):
    t = t_ref[0]
    odd = lax.rem(t, 2)
    for n, ref in ((1 - odd, a_ref), (odd, b_ref)):
        hal[n, 0:16] = jnp.zeros((16, 128), F32)
        hal[n, 16:400] = ref[0:384].astype(F32)
    fpad = jnp.zeros((8, 128), F32)
    for r in range(f_ref.shape[0]):
        fe[r, 0:8] = fpad
        fe[r, 24:32] = fpad
        fe[r, 8:16] = f_ref[r, 0:16].astype(F32)[0:8]
        fe[r, 16:24] = f_ref[r, 48:64].astype(F32)[8:16]
        fe[r, 6:8] = hal[0, 336 + 2 * r : 338 + 2 * r]
        fe[r, 24:26] = hal[1, 336 + 2 * r : 338 + 2 * r]
        se[r, 32:48] = mirror(s_ref[r, 0:16].astype(F32)).astype(BF)
        se[r, 48:64] = mirror(hal[0, 10 + 10 * r : 26 + 10 * r]).astype(BF)
        se[r, 0:16] = mirror(hal[1, 16 + 10 * r : 32 + 10 * r]).astype(BF)
        se[r, 16:32] = mirror(s_ref[r, 48:64].astype(F32)).astype(BF)
    correlate_groups(fe, se, w_ref, band, acc, [(0, 32), (16, 0)])

    def write(ref, base, count=18):
        rims = []
        for r in range(count):
            m = jnp.maximum(acc[base + r], 0.0)
            ref[16 * r : 16 * r + 16] = m[8:24].astype(BF)
            rims += [m[6:8], m[24:26]]
        if count % 4:
            rims.append(jnp.zeros((8, 128), F32))
        at, n = 16 * count, -(-count // 4) * 16
        ref[at : at + n] = jnp.concatenate(rims, axis=0).astype(BF)

    write(z_ref, 14 * (1 - t // 2) + 2)
    o_ref[0:864] = oi_ref[...]
    write(o_ref.at[864:1232], 14 * (t // 2) + 2)
    c_ref[0:576] = ci_ref[...]
    write(c_ref.at[576:816], 8 * (t ^ 1), 12)
    for ref, at in ((z_ref, 368), (c_ref, 816)):
        ref[at : at + 16] = near_ref[...]
        ref[at + 16 : at + 32] = far_ref[...]


def side_rows(t, a_ref, b_ref, top, bot):
    even = lax.rem(t, 2) == 0

    @pl.when(even)
    def _():
        bot[...] = a_ref[384:896].astype(F32)
        top[...] = jnp.where(t == 2, b_ref[384:896].astype(F32), 0.0)

    @pl.when(jnp.logical_not(even))
    def _():
        top[...] = a_ref[384:896].astype(F32)
        bot[...] = jnp.where(t == 1, b_ref[384:896].astype(F32), 0.0)


def edge(t, f, s, a, b, near, far, w_wide, oi, ci, state):
    return pl.pallas_call(
        edge_kernel,
        out_shape=(jax.ShapeDtypeStruct((400, 128), BF), jax.ShapeDtypeStruct((1232, 128), BF), jax.ShapeDtypeStruct((848, 128), BF)),
        in_specs=[SM] + [VM] * 10,
        out_specs=(VM,) * 3,
        scratch_shapes=[
            pltpu.VMEM((32, 32, 128), F32),
            pltpu.VMEM((32, 64, 128), BF),
            pltpu.VMEM((2, 400, 128), F32),
            pltpu.VMEM((4, 24, 32, 256), BF),
            pltpu.VMEM((36, 32, 128), F32),
        ],
        compiler_params=pltpu.CompilerParams(vmem_limit_bytes=24 << 20),
        cost_estimate=pl.CostEstimate(flops=1000000000, bytes_accessed=1000000, transcendentals=0),
        name="edge",
    )(t, f, s, a, b, near, far, w_wide, oi, ci, state)


def join_kernel(i_ref, e_ref, one_ref, o_ref):
    o_ref[0:864] = i_ref[...]
    o_ref[864:1264] = e_ref[...]


def join(zi, ze, one):
    return pl.pallas_call(
        join_kernel,
        out_shape=jax.ShapeDtypeStruct((1264, 128), BF),
        in_specs=[VM] * 3,
        out_specs=VM,
        compiler_params=pltpu.CompilerParams(vmem_limit_bytes=8 << 20),
        name="join",
    )(zi, ze, one)


def state_rows(t, a_ref, b_ref, h_ref, hs, top, bot):
    side_rows(t, a_ref, b_ref, top, bot)
    hs[0:512] = top[...]
    hs[2560:3072] = bot[...]
    for i in range(8):
        hs[512 + 256 * i : 768 + 256 * i] = h_ref[i].astype(F32)


def gate_products(x, gw_ref, width, i, lanes):
    def part(qs):
        lhs = jnp.concatenate([x[q, i + p : i + p + 2, :, lanes[0]].reshape(2 * width, -1) for q in qs for p in range(3)], axis=1)
        rhs = jnp.concatenate([gw_ref[p, q, lanes[1]] for q in qs for p in range(3)], axis=0)
        return jnp.dot(lhs, rhs, preferred_element_type=F32)

    return part((0, 2)), part((1,))


def gates(metric_ref, t, x, gw_ref, state_ref, width, put):
    for i in range(0, 10, 2):
        known = 2 <= i < 8
        half = slice(128, 256)
        sides, center = gate_products(x, gw_ref, width, i, (half, half) if known else (slice(0, 256), slice(0, 256)))
        for n in range(2):
            cut = slice(width * n, width * n + width)
            gate = center[cut] + sides[cut] * metric_ref[jnp.clip(8 * t + i + n - 1, 0, 31)]
            if known:
                gate = gate + state_ref[i + n - 2]
            put(i + n, 0.5 * jnp.tanh(0.5 * gate) + 0.5)


def state_products(metric_ref, t, x, gw_ref, width, out):
    for i in range(0, 6, 2):
        sides, center = gate_products(x, gw_ref, width, i, (slice(0, 128), slice(0, 128)))
        for n in range(2):
            cut = slice(width * n, width * n + width)
            out[i + n] = center[cut] + sides[cut] * metric_ref[8 * t + i + n + 1]


def state_first_kernel(t_ref, metric_ref, h_ref, gw_ref, out_ref, hs, x):
    t = t_ref[0]
    for i in range(8):
        hs[256 * i : 256 * i + 256] = h_ref[i].astype(F32)
    for q in range(3):
        for i in range(8):
            x[q, i] = hs[pl.ds(256 * i + 126 * (t // 2) + q, 128)].astype(BF)
    state_products(metric_ref, t, x, gw_ref, 128, out_ref)


def state_second_kernel(t_ref, l_ref, metric_ref, h_ref, near_ref, far_ref, gw_ref, out_ref, hs, hf, x):
    t = t_ref[0]
    high = t // 2
    c0 = pl.multiple_of(128 - 128 * high, 128)
    west_even = lax.rem(l_ref[0], 2) == 0
    near, far = near_ref[...].astype(F32), far_ref[...].astype(F32)
    hr = jnp.where(west_even, near, far)
    hl = jnp.where(west_even, far, near)
    for i in range(8):
        hs[256 * i : 256 * i + 256] = h_ref[i].astype(F32)
    for i in range(8):
        outer(hf, hs, i, c0, high, hl[2 * i : 2 * i + 2], hr[2 * i : 2 * i + 2])
    for q in range(3):
        for i in range(8):
            x[q, i] = hf[i, q : q + 144].astype(BF)
    state_products(metric_ref, t, x, gw_ref, 144, out_ref)


def outer(hf, hs, i, c0, high, side_w, side_e):
    low = high == 0
    hf[i, 2:130] = hs[pl.ds(256 * i + c0, 128)]
    hf[i, 0:2] = jnp.where(low, hs[256 * i + 126 : 256 * i + 128], side_w)
    hf[i, 130:132] = jnp.where(low, side_e, hs[256 * i + 128 : 256 * i + 130])
    hf[i, pl.ds(134 - 2 * high, 4)] = hs[pl.ds(256 * i + 252 * high, 4)]
    hf[i, pl.ds(132 + 4 * high, 2)] = jnp.where(low, side_w, side_e)


def state_first(t, metric, h, gw):
    return pl.pallas_call(
        state_first_kernel,
        out_shape=jax.ShapeDtypeStruct((6, 128, 256), F32),
        in_specs=[SM, SM] + [VM] * 2,
        out_specs=VM,
        scratch_shapes=[pltpu.VMEM((2048, 128), F32), pltpu.VMEM((3, 8, 128, 128), BF)],
        compiler_params=pltpu.CompilerParams(vmem_limit_bytes=24 << 20),
        cost_estimate=pl.CostEstimate(flops=10**9, bytes_accessed=2 << 20, transcendentals=0),
        name="state_first",
    )(t, metric, h, gw)


def state_second(t, l, metric, h, near, far, gw):
    return pl.pallas_call(
        state_second_kernel,
        out_shape=jax.ShapeDtypeStruct((6, 144, 256), F32),
        in_specs=[SM, SM, SM] + [VM] * 4,
        out_specs=VM,
        scratch_shapes=[pltpu.VMEM((2048, 128), F32), pltpu.VMEM((8, 152, 128), F32), pltpu.VMEM((3, 8, 144, 128), BF)],
        compiler_params=pltpu.CompilerParams(vmem_limit_bytes=24 << 20),
        cost_estimate=pl.CostEstimate(flops=10**9, bytes_accessed=2 << 20, transcendentals=0),
        name="state_second",
    )(t, l, metric, h, near, far, gw)


def candidates(metric_ref, t, x, m3s, r, cw_ref, width, put):
    zero = jnp.zeros((256, 128), BF)

    def pair(rr, q):
        first = cw_ref[rr, q] if rr < 3 else zero
        second = cw_ref[rr - 1, q] if rr > 0 else zero
        return jnp.concatenate([first, second], axis=1)

    sides_w = jnp.concatenate([pair(rr, q) for q in (0, 2) for rr in range(4)], axis=0)
    center_w = jnp.concatenate([pair(rr, 1) for rr in range(4)], axis=0)

    def taps(q, row):
        mm = m3s[row + 1] if q == 2 else x[q + 1, row + 1, 0:width, 128:256]
        return [r[q, row], mm]

    def stack(qs, i):
        one = [jnp.concatenate(sum([taps(q, i + k + rr) for q in qs for rr in range(4)], []), axis=1) for k in (0, 2)]
        return jnp.concatenate(one, axis=0)

    for i in range(0, 8, 4):
        sides = jnp.dot(stack((0, 2), i), sides_w, preferred_element_type=F32)
        center = jnp.dot(stack((1,), i), center_w, preferred_element_type=F32)
        for n in range(4):
            cut = (slice(width * (n // 2), width * (n // 2) + width), slice(128 * (n % 2), 128 * (n % 2) + 128))
            put(i + n, jnp.tanh(center[cut] + sides[cut] * metric_ref[8 * t + i + n]))


def piece_row(ref, row, inside, count):
    mid = ref[pl.ds(pl.multiple_of(48 * row, 16), 48)].astype(F32)
    ends = ref[pl.ds(pl.multiple_of(48 * count + 16 * row, 16), 16)].astype(F32)
    if inside is not None:
        mid, ends = jnp.where(inside, mid, 0.0), jnp.where(inside, ends, 0.0)
    return mid, ends


def first_kernel(t_ref, metric_ref, h_ref, a_ref, b_ref, own_ref, mate_ref, state_ref, gw_ref, cw_ref, out_ref, hs, mf, x, m3s, rf, r, ug, top, bot, rims):
    t = t_ref[0]
    high = t // 2
    state_rows(t, a_ref, b_ref, h_ref, hs, top, bot)
    start = 8 * t - 2 - 14 * high
    odd = lax.rem(t, 2)
    for s, ref, count in ((odd, own_ref, 18), (1 - odd, mate_ref, 12)):
        rims[0:80] = ref[1152:1232].astype(F32) if count == 18 else jnp.pad(ref[768:816].astype(F32), ((0, 32), (0, 0)))
        for i in range(12):
            row, inside = i, None
            if count == 18:
                row = start + i
                inside = (row >= 0) & (row < 18)
                row = jnp.clip(row, 0, 17)
            mid, ends = piece_row(ref, row, inside, count)
            at = 64 * s + 16 * high
            mf[i, pl.ds(at + 8, 48)] = mid
            mf[i, pl.ds(at, 8)] = ends[0:8]
            mf[i, pl.ds(at + 56, 8)] = ends[8:16]

            @pl.when(s != high)
            def _(i=i, row=row, s=s, inside=inside):
                v = rims[pl.ds(4 * row + 2 * s, 2)]
                mf[i, pl.ds(128 - 114 * high, 2)] = v if inside is None else jnp.where(inside, v, 0.0)

    for q in range(3):
        for i in range(12):
            if not 4 <= i < 8:
                x[q, i, :, 0:128] = hs[pl.ds(256 * i + 126 * high + q, 128)].astype(BF)
            x[q, i, :, 128:256] = mf[i, pl.ds(14 * high + q, 128)].astype(BF)
    for i in range(12):
        m3s[i] = mf[i, pl.ds(14 * high + 3, 128)].astype(BF)

    def put_gate(i, gate):
        rf[i, 0:128] = gate[:, 128:] * hs[pl.ds(256 * (i + 1) + 126 * high + 1, 128)]
        if 1 <= i < 9:
            ug[i - 1, 0:128] = gate[:, 0:128]

    gates(metric_ref, t, x, gw_ref, state_ref, 128, put_gate)
    for q in range(3):
        for i in range(10):
            r[q, i] = rf[i, q : q + 128].astype(BF)

    def put_new(i, cand):
        u = ug[i, 1:129]
        h = hs[pl.ds(256 * (i + 2) + 126 * high + 2, 128)]
        out_ref[i] = ((1.0 - u) * h + u * cand).astype(BF)

    candidates(metric_ref, t, x, m3s, r, cw_ref, 128, put_new)


def first_part(t, metric, h, a, b, own, mate, state, gw, cw):
    return pl.pallas_call(
        first_kernel,
        out_shape=jax.ShapeDtypeStruct((8, 128, 128), BF),
        in_specs=[SM, SM] + [VM] * 8,
        out_specs=VM,
        scratch_shapes=[
            pltpu.VMEM((3072, 128), F32),
            pltpu.VMEM((12, 152, 128), F32),
            pltpu.VMEM((3, 12, 128, 256), BF),
            pltpu.VMEM((12, 128, 128), BF),
            pltpu.VMEM((10, 136, 128), F32),
            pltpu.VMEM((3, 10, 128, 128), BF),
            pltpu.VMEM((8, 136, 128), F32),
            pltpu.VMEM((512, 128), F32),
            pltpu.VMEM((512, 128), F32),
            pltpu.VMEM((80, 128), F32),
        ],
        compiler_params=pltpu.CompilerParams(vmem_limit_bytes=24 << 20),
        cost_estimate=pl.CostEstimate(flops=10**7, bytes_accessed=10**5, transcendentals=0),
        name="first_part",
    )(t, metric, h, a, b, own, mate, state, gw, cw)


def second_kernel(
    t_ref, l_ref, metric_ref, h_ref, a_ref, b_ref, near_ref, far_ref, own_ref, mate_ref, z_ref, k_ref, state_ref, gw_ref, cw_ref, one_ref, out_ref,
    ob, ow, sem, hs, hf, mf, x, m3s, rf, r, ug, top, bot, rims,
):
    t = t_ref[0]
    high = t // 2
    c0 = pl.multiple_of(128 - 128 * high, 128)
    state_rows(t, a_ref, b_ref, h_ref, hs, top, bot)
    west_even = lax.rem(l_ref[0], 2) == 0
    odd = lax.rem(t, 2)
    low = high == 0

    def twelve(own, at):
        mates, others = mate_ref[816 + at : 832 + at].astype(F32), k_ref[1232 + at : 1248 + at].astype(F32)
        others = jnp.where((t == 1) | (t == 2), others, 0.0)
        above = jnp.where(odd == 1, mates, others)[12:16]
        below = jnp.where(odd == 1, others, mates)[0:4]
        return jnp.concatenate([above, own[...].astype(F32), below], axis=0)

    near, far = twelve(near_ref, 0), twelve(far_ref, 16)
    hr = jnp.where(west_even, near, far)
    hl = jnp.where(west_even, far, near)
    for i in range(12):
        outer(hf, hs, i, c0, high, hl[2 * i : 2 * i + 2], hr[2 * i : 2 * i + 2])
    start = 8 * t - 2 - 14 * high
    for s, ref in ((odd, z_ref), (1 - odd, k_ref)):
        rims[0:80] = ref[1152:1232].astype(F32)
        for i in range(12):
            row = start + i
            inside = (row >= 0) & (row < 18)
            row = jnp.clip(row, 0, 17)
            mid = ref[pl.ds(pl.multiple_of(48 * row, 16), 48)].astype(F32)
            ends = ref[pl.ds(pl.multiple_of(864 + 16 * row, 16), 16)].astype(F32)
            mf[i, pl.ds(10 + 64 * s, 48)] = jnp.where(inside, mid, 0.0)
            ends = jnp.where(inside, ends, 0.0)
            mf[i, pl.ds(2 + 64 * s, 8)] = ends[0:8]
            mf[i, pl.ds(58 + 64 * s, 8)] = ends[8:16]
            v = rims[pl.ds(4 * row + 2 * s, 2)]
            mf[i, pl.ds(130 * s, 2)] = jnp.where(inside, v, 0.0)
    mine = odd == high
    mates = jnp.pad(mate_ref[768:816].astype(F32), ((0, 32), (0, 0)))
    rims[0:80] = jnp.where(mine, own_ref[1152:1232].astype(F32), mates)
    for i in range(12):
        row = start + i
        inside = (row >= 0) & (row < 18)
        row = jnp.clip(row, 0, 17)
        at = pl.multiple_of(864 + 16 * row, 16)
        ends = jnp.where(inside, own_ref[pl.ds(at, 16)].astype(F32), 0.0)
        ends = jnp.where(mine, ends, mate_ref[576 + 16 * i : 592 + 16 * i].astype(F32))
        mf[i, pl.ds(134 - 2 * high, 4)] = jnp.where(low, ends[0:4], ends[12:16])
        row = jnp.where(mine, row, i)
        inside = inside | jnp.logical_not(mine)
        v = rims[pl.ds(4 * row + 2 * high, 2)]
        mf[i, pl.ds(132 + 4 * high, 2)] = jnp.where(inside, v, 0.0)
    for q in range(3):
        for i in range(12):
            if not 4 <= i < 8:
                x[q, i, :, 0:128] = hf[i, q : q + 144].astype(BF)
            x[q, i, :, 128:256] = mf[i, q : q + 144].astype(BF)
    for i in range(12):
        m3s[i] = mf[i, 3:147].astype(BF)

    def put_gate(i, gate):
        rf[i, 0:144] = gate[:, 128:] * hf[i + 1, 1:145]
        if 1 <= i < 9:
            ug[i - 1, 0:144] = gate[:, 0:128]

    gates(metric_ref, t, x, gw_ref, state_ref, 144, put_gate)
    for q in range(3):
        for i in range(10):
            r[q, i] = rf[i, q : q + 144].astype(BF)

    def put_new(i, cand):
        u = ug[i, 1:145]
        h = hf[i + 2, 2:146]
        new = (1.0 - u) * h + u * cand
        ob[i, pl.ds(c0, 128)] = new[0:128].astype(BF)
        ow[i, pl.ds(2 - 2 * high, 126)] = one_ref[i].astype(F32)[0:126]
        ow[i, pl.ds(126 * high, 2)] = new[132:134]
        ob[i, pl.ds(pl.multiple_of(128 - c0, 128), 128)] = ow[i].astype(BF)
        pltpu.make_async_copy(ob.at[i], out_ref.at[i], sem.at[i]).start()

    candidates(metric_ref, t, x, m3s, r, cw_ref, 144, put_new)
    for i in range(8):
        pltpu.make_async_copy(ob.at[i], out_ref.at[i], sem.at[i]).wait()


def second_part(t, l, metric, h, a, b, near, far, own, mate, z, k, state, gw, cw, one):
    return pl.pallas_call(
        second_kernel,
        out_shape=jax.ShapeDtypeStruct((8, 256, 128), BF),
        in_specs=[SM, SM, SM] + [VM] * 13,
        out_specs=pl.BlockSpec(memory_space=pl.ANY),
        scratch_shapes=[
            pltpu.VMEM((8, 256, 128), BF),
            pltpu.VMEM((8, 128, 128), F32),
            pltpu.SemaphoreType.DMA((8,)),
            pltpu.VMEM((3072, 128), F32),
            pltpu.VMEM((12, 152, 128), F32),
            pltpu.VMEM((12, 152, 128), F32),
            pltpu.VMEM((3, 12, 144, 256), BF),
            pltpu.VMEM((12, 144, 128), BF),
            pltpu.VMEM((10, 152, 128), F32),
            pltpu.VMEM((3, 10, 144, 128), BF),
            pltpu.VMEM((8, 152, 128), F32),
            pltpu.VMEM((512, 128), F32),
            pltpu.VMEM((512, 128), F32),
            pltpu.VMEM((80, 128), F32),
        ],
        compiler_params=pltpu.CompilerParams(vmem_limit_bytes=24 << 20),
        cost_estimate=pl.CostEstimate(flops=5000000000, bytes_accessed=4000000, transcendentals=0),
        name="second_part",
    )(t, l, metric, h, a, b, near, far, own, mate, z, k, state, gw, cw, one)


def swaps(n, first):
    pairs = [(i % n, (i + 1) % n) for i in range(first, n, 2)]
    return pairs + [(j, i) for i, j in pairs]


def body(first, second, hidden, encoder_weight, gates_weight, candidate_weight, row_metric):
    t = lax.axis_index("lat").astype(jnp.int32)[None]
    l = lax.axis_index("lon").astype(jnp.int32)[None]
    count = lax.axis_size("lon")
    slabs = count * lax.axis_size("lat")
    core = [(i, i ^ 1) for i in range(4)]
    chip = [(i, i ^ 2) for i in range(4)]

    a_send, b_send, near_send, far_send = pack(t, l, first, second, hidden)
    with jax.named_scope("rim_far"):
        b = lax.ppermute(b_send, BOTH, swaps(slabs, 1))
    with jax.named_scope("rim_near"):
        a = lax.ppermute(a_send, BOTH, swaps(slabs, 0))
    with jax.named_scope("state_near"):
        near = lax.ppermute(near_send, "lon", swaps(count, 0))
    with jax.named_scope("state_far"):
        far = lax.ppermute(far_send, "lon", swaps(count, 1))
    zi_send, oi, ci, w_wide = inner(t, first, second, encoder_weight)
    with jax.named_scope("inner_chip"):
        zi = lax.ppermute(zi_send, "lat", chip)
    state_one = state_first(t, row_metric, hidden, gates_weight)
    state_two = state_second(t, l, row_metric, hidden, near, far, gates_weight)
    ze_send, own, own_send = edge(t, first, second, a, b, near, far, w_wide, oi, ci, state_one)
    with jax.named_scope("edge_chip"):
        ze = lax.ppermute(ze_send, "lat", chip)
    with jax.named_scope("own_core"):
        mate = lax.ppermute(own_send, "lat", core)
    one = first_part(t, row_metric, hidden, a, b, own, mate, state_one, gates_weight, candidate_weight)
    z = join(zi, ze, one)
    with jax.named_scope("chip_core"):
        k = lax.ppermute(z, "lat", core)
    return second_part(t, l, row_metric, hidden, a, b, near, far, own, mate, z, k, state_two, gates_weight, candidate_weight, one)


def solution(mesh):
    return jax.shard_map(
        body,
        mesh=mesh,
        in_specs=(
            P(None, BOTH, None),
            P(None, BOTH, None),
            P("lat", "lon", None),
            P(),
            P(),
            P(),
            P(),
        ),
        out_specs=P("lat", "lon", None),
        check_vma=False,
    )
```

```python
import functools

import jax
import jax.numpy as jnp
from jax import lax
from jax.experimental import pallas as pl
from jax.experimental.pallas import tpu as pltpu
from jax.sharding import PartitionSpec as P

RADIUS, WIN = 8, 17
G, S = 16, 5
BF, F32 = jnp.bfloat16, jnp.float32
NT = (((1,), (1,)), ((), ()))
BOTH = ("lon", "lat")
VM = pl.BlockSpec(memory_space=pltpu.VMEM)
SM = pl.BlockSpec(memory_space=pltpu.SMEM)


def mirror(x):
    n = x.shape[0] // 8
    ids = 7 - lax.broadcasted_iota(jnp.int32, (8, 128), 0)
    tiles = [
        jnp.take_along_axis(x[8 * k : 8 * k + 8], ids, axis=0, mode="promise_in_bounds")
        for k in reversed(range(n))
    ]
    return jnp.concatenate(tiles, axis=0)


def pack_kernel(t_ref, l_ref, f_ref, s_ref, h_ref, a_ref, b_ref, near_ref, far_ref, up, down, sb, fb, hb, cb, sem):
    rows = f_ref.shape[0]
    moves = []
    for n, col in enumerate((48, 0)):
        moves.append((s_ref.at[:, col : col + 16], sb.at[n]))
        moves.append((f_ref.at[:, col : col + 16], fb.at[n]))
        moves.append((h_ref.at[6 - 6 * n : 8 - 6 * n], hb.at[n]))
        moves.append((h_ref.at[:, 240 - 240 * n : 256 - 240 * n], cb.at[n]))
    copies = [pltpu.make_async_copy(a, b, sem.at[k]) for k, (a, b) in enumerate(moves)]
    for c in copies:
        c.start()
    for c in copies:
        c.wait()
    for r in range(rows):
        up[10 * r : 10 * r + 10] = sb[0, r].astype(F32)[6:16]
        down[10 * r : 10 * r + 10] = sb[1, r].astype(F32)[0:10]
        up[320 + 2 * r : 322 + 2 * r] = fb[0, r].astype(F32)[14:16]
        down[320 + 2 * r : 322 + 2 * r] = fb[1, r].astype(F32)[0:2]
    east = jnp.concatenate([cb[0, i].astype(F32)[14:16] for i in range(8)], axis=0)
    west = jnp.concatenate([cb[1, i].astype(F32)[0:2] for i in range(8)], axis=0)
    even = lax.rem(l_ref[0], 2) == 0
    near_ref[...] = jnp.where(even, east, west).astype(BF)
    far_ref[...] = jnp.where(even, west, east).astype(BF)
    even = lax.rem(t_ref[0], 2) == 0

    b_ref[896:912] = jnp.zeros((16, 128), BF)

    def put(n_ref, p_ref):
        n_ref[0:384] = up[...].astype(BF)
        p_ref[0:384] = down[...].astype(BF)
        for i in range(2):
            n_ref[384 + 256 * i : 640 + 256 * i] = hb[0, i]
            p_ref[384 + 256 * i : 640 + 256 * i] = hb[1, i]

    @pl.when(even)
    def _():
        put(a_ref, b_ref)

    @pl.when(jnp.logical_not(even))
    def _():
        put(b_ref, a_ref)


def pack(t, l, f, s, h):
    hbm = pl.BlockSpec(memory_space=pl.ANY)
    return pl.pallas_call(
        pack_kernel,
        out_shape=(pltpu.VMEM((896, 128), BF), pltpu.VMEM((912, 128), BF)) + (pltpu.VMEM((16, 128), BF),) * 2,
        in_specs=[SM, SM, hbm, hbm, hbm],
        out_specs=(VM,) * 4,
        scratch_shapes=[
            pltpu.VMEM((384, 128), F32),
            pltpu.VMEM((384, 128), F32),
            pltpu.VMEM((2, 32, 16, 128), BF),
            pltpu.VMEM((2, 32, 16, 128), BF),
            pltpu.VMEM((2, 2, 256, 128), BF),
            pltpu.VMEM((2, 8, 16, 128), BF),
            pltpu.SemaphoreType.DMA((8,)),
        ],
        name="pack",
    )(t, l, f, s, h)


def correlate_groups(fe, se, w_ref, band, acc, groups):
    rows = fe.shape[0]
    blocks = rows // 8
    width = G * len(groups)
    scale = 128**-0.5
    for n, (fcol, scol) in enumerate(groups):
        for b in range(blocks):
            lo, hi = max(0, 8 * b - 8), min(rows, 8 * b + 16)
            keys = se[8 * b : 8 * b + 8, scol : scol + 32, :].reshape(256, 128)
            query = fe[lo:hi, fcol : fcol + G, :].reshape((hi - lo) * G, 128).astype(BF)
            c = lax.dot_general(query, keys, NT, preferred_element_type=F32)
            c = (c * scale).reshape(hi - lo, G, 256)
            for h in range(2):
                part = pltpu.roll(c[:, :, 128 * h : 128 * h + 128], 0, 2, stride=1, stride_axis=1)
                band[b, lo - 8 * b + 8 : hi - 8 * b + 8, G * n : G * n + G, 128 * h : 128 * h + 128] = part.astype(BF)
    done = set()
    for d in range(-8, 16):
        bs = [b for b in range(blocks) if 0 <= 8 * b + d < rows]
        b0, b1 = bs[0], bs[-1] + 1
        lhs = band[b0:b1, d + 8].reshape((b1 - b0) * width, 256)
        o = 15 - d
        part = jnp.dot(lhs, w_ref[32 * o : 32 * o + 256, :], preferred_element_type=F32)
        part = part.reshape(b1 - b0, width, 128)
        for n, b in enumerate(bs):
            i = 8 * b + d
            if i in done:
                acc[i + 2] += part[n]
            else:
                acc[i + 2] = part[n]
                done.add(i)
    zero = jnp.zeros((2, width, 128), F32)
    acc[0:2] = zero
    acc[rows + 2 : rows + 4] = zero


def widen(enc_ref, wide_ref, enc, wide):
    wide[...] = jnp.zeros(wide.shape, F32)
    enc[0:8] = jnp.zeros((8, 128), F32)
    enc[8:297] = enc_ref[...].astype(F32)
    for a in range(WIN):
        at = 32 * (a + 7) + 15
        wide[at : at + 17] = mirror(enc[17 * a + 1 : 17 * a + 25])[0:17]
    wide_ref[...] = wide[...].astype(BF)


def inner_kernel(t_ref, f_ref, s_ref, enc_ref, z_ref, o_ref, c_ref, w_ref, fe, se, band, acc, enc, wide):
    widen(enc_ref, w_ref, enc, wide)
    for r in range(f_ref.shape[0]):
        fe[r] = f_ref[r].astype(F32)
        se[r] = mirror(s_ref[r].astype(F32)).astype(BF)
    correlate_groups(fe, se, w_ref, band, acc, [(8 + G * g, 32 - G * g) for g in range(3)])
    high = t_ref[0] // 2
    for base, ref in ((14 * (1 - high) + 2, z_ref), (14 * high + 2, o_ref)):
        for r in range(18):
            ref[48 * r : 48 * r + 48] = jnp.maximum(acc[base + r], 0.0).astype(BF)
    base = 8 * (t_ref[0] ^ 1)
    for r in range(12):
        c_ref[48 * r : 48 * r + 48] = jnp.maximum(acc[base + r], 0.0).astype(BF)


def inner(t, f, s, enc):
    return pl.pallas_call(
        inner_kernel,
        out_shape=(jax.ShapeDtypeStruct((864, 128), BF),) * 2 + (jax.ShapeDtypeStruct((576, 128), BF), jax.ShapeDtypeStruct((992, 128), BF)),
        in_specs=[SM] + [VM] * 3,
        out_specs=(VM,) * 4,
        scratch_shapes=[
            pltpu.VMEM((32, 64, 128), F32),
            pltpu.VMEM((32, 64, 128), BF),
            pltpu.VMEM((4, 24, 48, 256), BF),
            pltpu.VMEM((36, 48, 128), F32),
            pltpu.VMEM((304, 128), F32),
            pltpu.VMEM((992, 128), F32),
        ],
        compiler_params=pltpu.CompilerParams(vmem_limit_bytes=24 << 20),
        cost_estimate=pl.CostEstimate(flops=1000000000, bytes_accessed=1000000, transcendentals=0),
        name="inner",
    )(t, f, s, enc)


def edge_kernel(t_ref, f_ref, s_ref, a_ref, b_ref, near_ref, far_ref, w_ref, oi_ref, ci_ref, state_ref, z_ref, o_ref, c_ref, fe, se, hal, band, acc):
    t = t_ref[0]
    odd = lax.rem(t, 2)
    for n, ref in ((1 - odd, a_ref), (odd, b_ref)):
        hal[n, 0:16] = jnp.zeros((16, 128), F32)
        hal[n, 16:400] = ref[0:384].astype(F32)
    fpad = jnp.zeros((8, 128), F32)
    for r in range(f_ref.shape[0]):
        fe[r, 0:8] = fpad
        fe[r, 24:32] = fpad
        fe[r, 8:16] = f_ref[r, 0:16].astype(F32)[0:8]
        fe[r, 16:24] = f_ref[r, 48:64].astype(F32)[8:16]
        fe[r, 6:8] = hal[0, 336 + 2 * r : 338 + 2 * r]
        fe[r, 24:26] = hal[1, 336 + 2 * r : 338 + 2 * r]
        se[r, 32:48] = mirror(s_ref[r, 0:16].astype(F32)).astype(BF)
        se[r, 48:64] = mirror(hal[0, 10 + 10 * r : 26 + 10 * r]).astype(BF)
        se[r, 0:16] = mirror(hal[1, 16 + 10 * r : 32 + 10 * r]).astype(BF)
        se[r, 16:32] = mirror(s_ref[r, 48:64].astype(F32)).astype(BF)
    correlate_groups(fe, se, w_ref, band, acc, [(0, 32), (16, 0)])

    def write(ref, base, count=18):
        rims = []
        for r in range(count):
            m = jnp.maximum(acc[base + r], 0.0)
            ref[16 * r : 16 * r + 16] = m[8:24].astype(BF)
            rims += [m[6:8], m[24:26]]
        if count % 4:
            rims.append(jnp.zeros((8, 128), F32))
        at, n = 16 * count, -(-count // 4) * 16
        ref[at : at + n] = jnp.concatenate(rims, axis=0).astype(BF)

    write(z_ref, 14 * (1 - t // 2) + 2)
    o_ref[0:864] = oi_ref[...]
    write(o_ref.at[864:1232], 14 * (t // 2) + 2)
    c_ref[0:576] = ci_ref[...]
    write(c_ref.at[576:816], 8 * (t ^ 1), 12)
    for ref, at in ((z_ref, 368), (c_ref, 816)):
        ref[at : at + 16] = near_ref[...]
        ref[at + 16 : at + 32] = far_ref[...]


def side_rows(t, a_ref, b_ref, top, bot):
    even = lax.rem(t, 2) == 0

    @pl.when(even)
    def _():
        bot[...] = a_ref[384:896].astype(F32)
        top[...] = jnp.where(t == 2, b_ref[384:896].astype(F32), 0.0)

    @pl.when(jnp.logical_not(even))
    def _():
        top[...] = a_ref[384:896].astype(F32)
        bot[...] = jnp.where(t == 1, b_ref[384:896].astype(F32), 0.0)


def edge(t, f, s, a, b, near, far, w_wide, oi, ci, state):
    return pl.pallas_call(
        edge_kernel,
        out_shape=(jax.ShapeDtypeStruct((400, 128), BF), jax.ShapeDtypeStruct((1232, 128), BF), jax.ShapeDtypeStruct((848, 128), BF)),
        in_specs=[SM] + [VM] * 10,
        out_specs=(VM,) * 3,
        scratch_shapes=[
            pltpu.VMEM((32, 32, 128), F32),
            pltpu.VMEM((32, 64, 128), BF),
            pltpu.VMEM((2, 400, 128), F32),
            pltpu.VMEM((4, 24, 32, 256), BF),
            pltpu.VMEM((36, 32, 128), F32),
        ],
        compiler_params=pltpu.CompilerParams(vmem_limit_bytes=24 << 20),
        cost_estimate=pl.CostEstimate(flops=1000000000, bytes_accessed=1000000, transcendentals=0),
        name="edge",
    )(t, f, s, a, b, near, far, w_wide, oi, ci, state)


def join_kernel(i_ref, e_ref, one_ref, o_ref):
    o_ref[0:864] = i_ref[...]
    o_ref[864:1264] = e_ref[...]


def join(zi, ze, one):
    return pl.pallas_call(
        join_kernel,
        out_shape=jax.ShapeDtypeStruct((1264, 128), BF),
        in_specs=[VM] * 3,
        out_specs=VM,
        compiler_params=pltpu.CompilerParams(vmem_limit_bytes=8 << 20),
        name="join",
    )(zi, ze, one)


def state_rows(t, a_ref, b_ref, h_ref, hs, top, bot):
    side_rows(t, a_ref, b_ref, top, bot)
    hs[0:512] = top[...]
    hs[2560:3072] = bot[...]
    for i in range(8):
        hs[512 + 256 * i : 768 + 256 * i] = h_ref[i].astype(F32)


def gate_products(x, gw_ref, width, i, lanes):
    def part(qs):
        lhs = jnp.concatenate([x[q, i + p : i + p + 2, :, lanes[0]].reshape(2 * width, -1) for q in qs for p in range(3)], axis=1)
        rhs = jnp.concatenate([gw_ref[p, q, lanes[1]] for q in qs for p in range(3)], axis=0)
        return jnp.dot(lhs, rhs, preferred_element_type=F32)

    return part((0, 2)), part((1,))


def gates(metric_ref, t, x, gw_ref, state_ref, width, put):
    for i in range(0, 10, 2):
        known = 2 <= i < 8
        half = slice(128, 256)
        sides, center = gate_products(x, gw_ref, width, i, (half, half) if known else (slice(0, 256), slice(0, 256)))
        for n in range(2):
            cut = slice(width * n, width * n + width)
            gate = center[cut] + sides[cut] * metric_ref[jnp.clip(8 * t + i + n - 1, 0, 31)]
            if known:
                gate = gate + state_ref[i + n - 2]
            put(i + n, 0.5 * jnp.tanh(0.5 * gate) + 0.5)


def state_products(metric_ref, t, x, gw_ref, width, out):
    for i in range(0, 6, 2):
        sides, center = gate_products(x, gw_ref, width, i, (slice(0, 128), slice(0, 128)))
        for n in range(2):
            cut = slice(width * n, width * n + width)
            out[i + n] = center[cut] + sides[cut] * metric_ref[8 * t + i + n + 1]


def state_first_kernel(t_ref, metric_ref, h_ref, gw_ref, out_ref, hs, x):
    t = t_ref[0]
    for i in range(8):
        hs[256 * i : 256 * i + 256] = h_ref[i].astype(F32)
    for q in range(3):
        for i in range(8):
            x[q, i] = hs[pl.ds(256 * i + 126 * (t // 2) + q, 128)].astype(BF)
    state_products(metric_ref, t, x, gw_ref, 128, out_ref)


def state_second_kernel(t_ref, l_ref, metric_ref, h_ref, near_ref, far_ref, gw_ref, out_ref, hs, hf, x):
    t = t_ref[0]
    high = t // 2
    c0 = pl.multiple_of(128 - 128 * high, 128)
    west_even = lax.rem(l_ref[0], 2) == 0
    near, far = near_ref[...].astype(F32), far_ref[...].astype(F32)
    hr = jnp.where(west_even, near, far)
    hl = jnp.where(west_even, far, near)
    for i in range(8):
        hs[256 * i : 256 * i + 256] = h_ref[i].astype(F32)
    for i in range(8):
        outer(hf, hs, i, c0, high, hl[2 * i : 2 * i + 2], hr[2 * i : 2 * i + 2])
    for q in range(3):
        for i in range(8):
            x[q, i] = hf[i, q : q + 144].astype(BF)
    state_products(metric_ref, t, x, gw_ref, 144, out_ref)


def outer(hf, hs, i, c0, high, side_w, side_e):
    low = high == 0
    hf[i, 2:130] = hs[pl.ds(256 * i + c0, 128)]
    hf[i, 0:2] = jnp.where(low, hs[256 * i + 126 : 256 * i + 128], side_w)
    hf[i, 130:132] = jnp.where(low, side_e, hs[256 * i + 128 : 256 * i + 130])
    hf[i, pl.ds(134 - 2 * high, 4)] = hs[pl.ds(256 * i + 252 * high, 4)]
    hf[i, pl.ds(132 + 4 * high, 2)] = jnp.where(low, side_w, side_e)


def state_first(t, metric, h, gw):
    return pl.pallas_call(
        state_first_kernel,
        out_shape=jax.ShapeDtypeStruct((6, 128, 256), F32),
        in_specs=[SM, SM] + [VM] * 2,
        out_specs=VM,
        scratch_shapes=[pltpu.VMEM((2048, 128), F32), pltpu.VMEM((3, 8, 128, 128), BF)],
        compiler_params=pltpu.CompilerParams(vmem_limit_bytes=24 << 20),
        cost_estimate=pl.CostEstimate(flops=10**9, bytes_accessed=2 << 20, transcendentals=0),
        name="state_first",
    )(t, metric, h, gw)


def state_second(t, l, metric, h, near, far, gw):
    return pl.pallas_call(
        state_second_kernel,
        out_shape=jax.ShapeDtypeStruct((6, 144, 256), F32),
        in_specs=[SM, SM, SM] + [VM] * 4,
        out_specs=VM,
        scratch_shapes=[pltpu.VMEM((2048, 128), F32), pltpu.VMEM((8, 152, 128), F32), pltpu.VMEM((3, 8, 144, 128), BF)],
        compiler_params=pltpu.CompilerParams(vmem_limit_bytes=24 << 20),
        cost_estimate=pl.CostEstimate(flops=10**9, bytes_accessed=2 << 20, transcendentals=0),
        name="state_second",
    )(t, l, metric, h, near, far, gw)


def candidates(metric_ref, t, x, m3s, r, cw_ref, width, put):
    zero = jnp.zeros((256, 128), BF)

    def pair(rr, q):
        first = cw_ref[rr, q] if rr < 3 else zero
        second = cw_ref[rr - 1, q] if rr > 0 else zero
        return jnp.concatenate([first, second], axis=1)

    sides_w = jnp.concatenate([pair(rr, q) for q in (0, 2) for rr in range(4)], axis=0)
    center_w = jnp.concatenate([pair(rr, 1) for rr in range(4)], axis=0)

    def taps(q, row):
        mm = m3s[row + 1] if q == 2 else x[q + 1, row + 1, 0:width, 128:256]
        return [r[q, row], mm]

    def stack(qs, i):
        one = [jnp.concatenate(sum([taps(q, i + k + rr) for q in qs for rr in range(4)], []), axis=1) for k in (0, 2)]
        return jnp.concatenate(one, axis=0)

    for i in range(0, 8, 4):
        sides = jnp.dot(stack((0, 2), i), sides_w, preferred_element_type=F32)
        center = jnp.dot(stack((1,), i), center_w, preferred_element_type=F32)
        for n in range(4):
            cut = (slice(width * (n // 2), width * (n // 2) + width), slice(128 * (n % 2), 128 * (n % 2) + 128))
            put(i + n, jnp.tanh(center[cut] + sides[cut] * metric_ref[8 * t + i + n]))


def piece_row(ref, row, inside, count):
    mid = ref[pl.ds(pl.multiple_of(48 * row, 16), 48)].astype(F32)
    ends = ref[pl.ds(pl.multiple_of(48 * count + 16 * row, 16), 16)].astype(F32)
    if inside is not None:
        mid, ends = jnp.where(inside, mid, 0.0), jnp.where(inside, ends, 0.0)
    return mid, ends


def first_kernel(t_ref, metric_ref, h_ref, a_ref, b_ref, own_ref, mate_ref, state_ref, gw_ref, cw_ref, out_ref, hs, mf, x, m3s, rf, r, ug, top, bot, rims):
    t = t_ref[0]
    high = t // 2
    state_rows(t, a_ref, b_ref, h_ref, hs, top, bot)
    start = 8 * t - 2 - 14 * high
    odd = lax.rem(t, 2)
    for s, ref, count in ((odd, own_ref, 18), (1 - odd, mate_ref, 12)):
        rims[0:80] = ref[1152:1232].astype(F32) if count == 18 else jnp.pad(ref[768:816].astype(F32), ((0, 32), (0, 0)))
        for i in range(12):
            row, inside = i, None
            if count == 18:
                row = start + i
                inside = (row >= 0) & (row < 18)
                row = jnp.clip(row, 0, 17)
            mid, ends = piece_row(ref, row, inside, count)
            at = 64 * s + 16 * high
            mf[i, pl.ds(at + 8, 48)] = mid
            mf[i, pl.ds(at, 8)] = ends[0:8]
            mf[i, pl.ds(at + 56, 8)] = ends[8:16]

            @pl.when(s != high)
            def _(i=i, row=row, s=s, inside=inside):
                v = rims[pl.ds(4 * row + 2 * s, 2)]
                mf[i, pl.ds(128 - 114 * high, 2)] = v if inside is None else jnp.where(inside, v, 0.0)

    for q in range(3):
        for i in range(12):
            if not 4 <= i < 8:
                x[q, i, :, 0:128] = hs[pl.ds(256 * i + 126 * high + q, 128)].astype(BF)
            x[q, i, :, 128:256] = mf[i, pl.ds(14 * high + q, 128)].astype(BF)
    for i in range(12):
        m3s[i] = mf[i, pl.ds(14 * high + 3, 128)].astype(BF)

    def put_gate(i, gate):
        rf[i, 0:128] = gate[:, 128:] * hs[pl.ds(256 * (i + 1) + 126 * high + 1, 128)]
        if 1 <= i < 9:
            ug[i - 1, 0:128] = gate[:, 0:128]

    gates(metric_ref, t, x, gw_ref, state_ref, 128, put_gate)
    for q in range(3):
        for i in range(10):
            r[q, i] = rf[i, q : q + 128].astype(BF)

    def put_new(i, cand):
        u = ug[i, 1:129]
        h = hs[pl.ds(256 * (i + 2) + 126 * high + 2, 128)]
        out_ref[i] = ((1.0 - u) * h + u * cand).astype(BF)

    candidates(metric_ref, t, x, m3s, r, cw_ref, 128, put_new)


def first_part(t, metric, h, a, b, own, mate, state, gw, cw):
    return pl.pallas_call(
        first_kernel,
        out_shape=(jax.ShapeDtypeStruct((8, 128, 128), BF), pltpu.VMEM((3072, 128), F32)),
        in_specs=[SM, SM] + [VM] * 8,
        out_specs=(VM, VM),
        scratch_shapes=[
            pltpu.VMEM((12, 152, 128), F32),
            pltpu.VMEM((3, 12, 128, 256), BF),
            pltpu.VMEM((12, 128, 128), BF),
            pltpu.VMEM((10, 136, 128), F32),
            pltpu.VMEM((3, 10, 128, 128), BF),
            pltpu.VMEM((8, 136, 128), F32),
            pltpu.VMEM((512, 128), F32),
            pltpu.VMEM((512, 128), F32),
            pltpu.VMEM((80, 128), F32),
        ],
        compiler_params=pltpu.CompilerParams(vmem_limit_bytes=24 << 20),
        cost_estimate=pl.CostEstimate(flops=10**7, bytes_accessed=10**5, transcendentals=0),
        name="first_part",
    )(t, metric, h, a, b, own, mate, state, gw, cw)


def second_kernel(
    t_ref, l_ref, metric_ref, hs, near_ref, far_ref, own_ref, mate_ref, z_ref, k_ref, state_ref, gw_ref, cw_ref, one_ref, out_ref,
    ob, ow, sem, hf, mf, x, m3s, rf, r, ug, rims,
):
    t = t_ref[0]
    high = t // 2
    c0 = pl.multiple_of(128 - 128 * high, 128)
    west_even = lax.rem(l_ref[0], 2) == 0
    odd = lax.rem(t, 2)
    low = high == 0

    def twelve(own, at):
        mates, others = mate_ref[816 + at : 832 + at].astype(F32), k_ref[1232 + at : 1248 + at].astype(F32)
        others = jnp.where((t == 1) | (t == 2), others, 0.0)
        above = jnp.where(odd == 1, mates, others)[12:16]
        below = jnp.where(odd == 1, others, mates)[0:4]
        return jnp.concatenate([above, own[...].astype(F32), below], axis=0)

    near, far = twelve(near_ref, 0), twelve(far_ref, 16)
    hr = jnp.where(west_even, near, far)
    hl = jnp.where(west_even, far, near)
    for i in range(12):
        outer(hf, hs, i, c0, high, hl[2 * i : 2 * i + 2], hr[2 * i : 2 * i + 2])
    start = 8 * t - 2 - 14 * high
    for s, ref in ((odd, z_ref), (1 - odd, k_ref)):
        rims[0:80] = ref[1152:1232].astype(F32)
        for i in range(12):
            row = start + i
            inside = (row >= 0) & (row < 18)
            row = jnp.clip(row, 0, 17)
            mid = ref[pl.ds(pl.multiple_of(48 * row, 16), 48)].astype(F32)
            ends = ref[pl.ds(pl.multiple_of(864 + 16 * row, 16), 16)].astype(F32)
            mf[i, pl.ds(10 + 64 * s, 48)] = jnp.where(inside, mid, 0.0)
            ends = jnp.where(inside, ends, 0.0)
            mf[i, pl.ds(2 + 64 * s, 8)] = ends[0:8]
            mf[i, pl.ds(58 + 64 * s, 8)] = ends[8:16]
            v = rims[pl.ds(4 * row + 2 * s, 2)]
            mf[i, pl.ds(130 * s, 2)] = jnp.where(inside, v, 0.0)
    mine = odd == high
    mates = jnp.pad(mate_ref[768:816].astype(F32), ((0, 32), (0, 0)))
    rims[0:80] = jnp.where(mine, own_ref[1152:1232].astype(F32), mates)
    for i in range(12):
        row = start + i
        inside = (row >= 0) & (row < 18)
        row = jnp.clip(row, 0, 17)
        at = pl.multiple_of(864 + 16 * row, 16)
        ends = jnp.where(inside, own_ref[pl.ds(at, 16)].astype(F32), 0.0)
        ends = jnp.where(mine, ends, mate_ref[576 + 16 * i : 592 + 16 * i].astype(F32))
        mf[i, pl.ds(134 - 2 * high, 4)] = jnp.where(low, ends[0:4], ends[12:16])
        row = jnp.where(mine, row, i)
        inside = inside | jnp.logical_not(mine)
        v = rims[pl.ds(4 * row + 2 * high, 2)]
        mf[i, pl.ds(132 + 4 * high, 2)] = jnp.where(inside, v, 0.0)
    for q in range(3):
        for i in range(12):
            if not 4 <= i < 8:
                x[q, i, :, 0:128] = hf[i, q : q + 144].astype(BF)
            x[q, i, :, 128:256] = mf[i, q : q + 144].astype(BF)
    for i in range(12):
        m3s[i] = mf[i, 3:147].astype(BF)

    def put_gate(i, gate):
        rf[i, 0:144] = gate[:, 128:] * hf[i + 1, 1:145]
        if 1 <= i < 9:
            ug[i - 1, 0:144] = gate[:, 0:128]

    gates(metric_ref, t, x, gw_ref, state_ref, 144, put_gate)
    for q in range(3):
        for i in range(10):
            r[q, i] = rf[i, q : q + 144].astype(BF)

    def put_new(i, cand):
        u = ug[i, 1:145]
        h = hf[i + 2, 2:146]
        new = (1.0 - u) * h + u * cand
        ob[i, pl.ds(c0, 128)] = new[0:128].astype(BF)
        ow[i, pl.ds(2 - 2 * high, 126)] = one_ref[i].astype(F32)[0:126]
        ow[i, pl.ds(126 * high, 2)] = new[132:134]
        ob[i, pl.ds(pl.multiple_of(128 - c0, 128), 128)] = ow[i].astype(BF)
        pltpu.make_async_copy(ob.at[i], out_ref.at[i], sem.at[i]).start()

    candidates(metric_ref, t, x, m3s, r, cw_ref, 144, put_new)
    for i in range(8):
        pltpu.make_async_copy(ob.at[i], out_ref.at[i], sem.at[i]).wait()


def second_part(t, l, metric, hs, near, far, own, mate, z, k, state, gw, cw, one):
    return pl.pallas_call(
        second_kernel,
        out_shape=jax.ShapeDtypeStruct((8, 256, 128), BF),
        in_specs=[SM, SM, SM] + [VM] * 11,
        out_specs=pl.BlockSpec(memory_space=pl.ANY),
        scratch_shapes=[
            pltpu.VMEM((8, 256, 128), BF),
            pltpu.VMEM((8, 128, 128), F32),
            pltpu.SemaphoreType.DMA((8,)),
            pltpu.VMEM((12, 152, 128), F32),
            pltpu.VMEM((12, 152, 128), F32),
            pltpu.VMEM((3, 12, 144, 256), BF),
            pltpu.VMEM((12, 144, 128), BF),
            pltpu.VMEM((10, 152, 128), F32),
            pltpu.VMEM((3, 10, 144, 128), BF),
            pltpu.VMEM((8, 152, 128), F32),
            pltpu.VMEM((80, 128), F32),
        ],
        compiler_params=pltpu.CompilerParams(vmem_limit_bytes=24 << 20),
        cost_estimate=pl.CostEstimate(flops=5000000000, bytes_accessed=4000000, transcendentals=0),
        name="second_part",
    )(t, l, metric, hs, near, far, own, mate, z, k, state, gw, cw, one)


def swaps(n, first):
    pairs = [(i % n, (i + 1) % n) for i in range(first, n, 2)]
    return pairs + [(j, i) for i, j in pairs]


def body(first, second, hidden, encoder_weight, gates_weight, candidate_weight, row_metric):
    t = lax.axis_index("lat").astype(jnp.int32)[None]
    l = lax.axis_index("lon").astype(jnp.int32)[None]
    count = lax.axis_size("lon")
    slabs = count * lax.axis_size("lat")
    core = [(i, i ^ 1) for i in range(4)]
    chip = [(i, i ^ 2) for i in range(4)]

    a_send, b_send, near_send, far_send = pack(t, l, first, second, hidden)
    with jax.named_scope("rim_far"):
        b = lax.ppermute(b_send, BOTH, swaps(slabs, 1))
    with jax.named_scope("rim_near"):
        a = lax.ppermute(a_send, BOTH, swaps(slabs, 0))
    with jax.named_scope("state_near"):
        near = lax.ppermute(near_send, "lon", swaps(count, 0))
    with jax.named_scope("state_far"):
        far = lax.ppermute(far_send, "lon", swaps(count, 1))
    zi_send, oi, ci, w_wide = inner(t, first, second, encoder_weight)
    with jax.named_scope("inner_chip"):
        zi = lax.ppermute(zi_send, "lat", chip)
    state_one = state_first(t, row_metric, hidden, gates_weight)
    state_two = state_second(t, l, row_metric, hidden, near, far, gates_weight)
    ze_send, own, own_send = edge(t, first, second, a, b, near, far, w_wide, oi, ci, state_one)
    with jax.named_scope("edge_chip"):
        ze = lax.ppermute(ze_send, "lat", chip)
    with jax.named_scope("own_core"):
        mate = lax.ppermute(own_send, "lat", core)
    one, laid = first_part(t, row_metric, hidden, a, b, own, mate, state_one, gates_weight, candidate_weight)
    z = join(zi, ze, one)
    with jax.named_scope("chip_core"):
        k = lax.ppermute(z, "lat", core)
    return second_part(t, l, row_metric, laid, near, far, own, mate, z, k, state_two, gates_weight, candidate_weight, one)


def solution(mesh):
    return jax.shard_map(
        body,
        mesh=mesh,
        in_specs=(
            P(None, BOTH, None),
            P(None, BOTH, None),
            P("lat", "lon", None),
            P(),
            P(),
            P(),
            P(),
        ),
        out_specs=P("lat", "lon", None),
        check_vma=False,
    )
```

```python
import functools

import jax
import jax.numpy as jnp
from jax import lax
from jax.experimental import pallas as pl
from jax.experimental.pallas import tpu as pltpu
from jax.sharding import PartitionSpec as P

RADIUS, WIN = 8, 17
G, S = 16, 5
BF, F32 = jnp.bfloat16, jnp.float32
NT = (((1,), (1,)), ((), ()))
BOTH = ("lon", "lat")
VM = pl.BlockSpec(memory_space=pltpu.VMEM)
SM = pl.BlockSpec(memory_space=pltpu.SMEM)


def mirror(x):
    n = x.shape[0] // 8
    ids = 7 - lax.broadcasted_iota(jnp.int32, (8, 128), 0)
    tiles = [
        jnp.take_along_axis(x[8 * k : 8 * k + 8], ids, axis=0, mode="promise_in_bounds")
        for k in reversed(range(n))
    ]
    return jnp.concatenate(tiles, axis=0)


def pack_kernel(t_ref, l_ref, f_ref, s_ref, h_ref, a_ref, b_ref, near_ref, far_ref, up, down, sb, fb, hb, cb, sem):
    rows = f_ref.shape[0]
    moves = []
    for n, col in enumerate((48, 0)):
        moves.append((s_ref.at[:, col : col + 16], sb.at[n]))
        moves.append((f_ref.at[:, col : col + 16], fb.at[n]))
        moves.append((h_ref.at[6 - 6 * n : 8 - 6 * n], hb.at[n]))
        moves.append((h_ref.at[:, 240 - 240 * n : 256 - 240 * n], cb.at[n]))
    copies = [pltpu.make_async_copy(a, b, sem.at[k]) for k, (a, b) in enumerate(moves)]
    for c in copies:
        c.start()
    for k in (0, 4):
        copies[k].wait()
    for r in range(rows):
        up[10 * r : 10 * r + 10] = sb[0, r].astype(F32)[6:16]
        down[10 * r : 10 * r + 10] = sb[1, r].astype(F32)[0:10]
    for k in (1, 5, 2, 6, 3, 7):
        copies[k].wait()
    for r in range(rows):
        up[320 + 2 * r : 322 + 2 * r] = fb[0, r].astype(F32)[14:16]
        down[320 + 2 * r : 322 + 2 * r] = fb[1, r].astype(F32)[0:2]
    east = jnp.concatenate([cb[0, i].astype(F32)[14:16] for i in range(8)], axis=0)
    west = jnp.concatenate([cb[1, i].astype(F32)[0:2] for i in range(8)], axis=0)
    even = lax.rem(l_ref[0], 2) == 0
    near_ref[...] = jnp.where(even, east, west).astype(BF)
    far_ref[...] = jnp.where(even, west, east).astype(BF)
    even = lax.rem(t_ref[0], 2) == 0

    b_ref[896:912] = jnp.zeros((16, 128), BF)

    def put(n_ref, p_ref):
        n_ref[0:384] = up[...].astype(BF)
        p_ref[0:384] = down[...].astype(BF)
        for i in range(2):
            n_ref[384 + 256 * i : 640 + 256 * i] = hb[0, i]
            p_ref[384 + 256 * i : 640 + 256 * i] = hb[1, i]

    @pl.when(even)
    def _():
        put(a_ref, b_ref)

    @pl.when(jnp.logical_not(even))
    def _():
        put(b_ref, a_ref)


def pack(t, l, f, s, h):
    hbm = pl.BlockSpec(memory_space=pl.ANY)
    return pl.pallas_call(
        pack_kernel,
        out_shape=(pltpu.VMEM((896, 128), BF), pltpu.VMEM((912, 128), BF)) + (pltpu.VMEM((16, 128), BF),) * 2,
        in_specs=[SM, SM, hbm, hbm, hbm],
        out_specs=(VM,) * 4,
        scratch_shapes=[
            pltpu.VMEM((384, 128), F32),
            pltpu.VMEM((384, 128), F32),
            pltpu.VMEM((2, 32, 16, 128), BF),
            pltpu.VMEM((2, 32, 16, 128), BF),
            pltpu.VMEM((2, 2, 256, 128), BF),
            pltpu.VMEM((2, 8, 16, 128), BF),
            pltpu.SemaphoreType.DMA((8,)),
        ],
        name="pack",
    )(t, l, f, s, h)


def correlate_groups(fe, se, w_ref, band, acc, groups):
    rows = fe.shape[0]
    blocks = rows // 8
    width = G * len(groups)
    scale = 128**-0.5
    for n, (fcol, scol) in enumerate(groups):
        for b in range(blocks):
            lo, hi = max(0, 8 * b - 8), min(rows, 8 * b + 16)
            keys = se[8 * b : 8 * b + 8, scol : scol + 32, :].reshape(256, 128)
            query = fe[lo:hi, fcol : fcol + G, :].reshape((hi - lo) * G, 128).astype(BF)
            c = lax.dot_general(query, keys, NT, preferred_element_type=F32)
            c = (c * scale).reshape(hi - lo, G, 256)
            for h in range(2):
                part = pltpu.roll(c[:, :, 128 * h : 128 * h + 128], 0, 2, stride=1, stride_axis=1)
                band[b, lo - 8 * b + 8 : hi - 8 * b + 8, G * n : G * n + G, 128 * h : 128 * h + 128] = part.astype(BF)
    done = set()
    for d in range(-8, 16):
        bs = [b for b in range(blocks) if 0 <= 8 * b + d < rows]
        b0, b1 = bs[0], bs[-1] + 1
        lhs = band[b0:b1, d + 8].reshape((b1 - b0) * width, 256)
        o = 15 - d
        part = jnp.dot(lhs, w_ref[32 * o : 32 * o + 256, :], preferred_element_type=F32)
        part = part.reshape(b1 - b0, width, 128)
        for n, b in enumerate(bs):
            i = 8 * b + d
            if i in done:
                acc[i + 2] += part[n]
            else:
                acc[i + 2] = part[n]
                done.add(i)
    zero = jnp.zeros((2, width, 128), F32)
    acc[0:2] = zero
    acc[rows + 2 : rows + 4] = zero


def widen(enc_ref, wide_ref, enc, wide):
    wide[...] = jnp.zeros(wide.shape, F32)
    enc[0:8] = jnp.zeros((8, 128), F32)
    enc[8:297] = enc_ref[...].astype(F32)
    for a in range(WIN):
        at = 32 * (a + 7) + 15
        wide[at : at + 17] = mirror(enc[17 * a + 1 : 17 * a + 25])[0:17]
    wide_ref[...] = wide[...].astype(BF)


def inner_kernel(t_ref, f_ref, s_ref, enc_ref, z_ref, o_ref, c_ref, w_ref, fe, se, band, acc, enc, wide):
    widen(enc_ref, w_ref, enc, wide)
    for r in range(f_ref.shape[0]):
        fe[r] = f_ref[r].astype(F32)
        se[r] = mirror(s_ref[r].astype(F32)).astype(BF)
    correlate_groups(fe, se, w_ref, band, acc, [(8 + G * g, 32 - G * g) for g in range(3)])
    high = t_ref[0] // 2
    for base, ref in ((14 * (1 - high) + 2, z_ref), (14 * high + 2, o_ref)):
        for r in range(18):
            ref[48 * r : 48 * r + 48] = jnp.maximum(acc[base + r], 0.0).astype(BF)
    base = 8 * (t_ref[0] ^ 1)
    for r in range(12):
        c_ref[48 * r : 48 * r + 48] = jnp.maximum(acc[base + r], 0.0).astype(BF)


def inner(t, f, s, enc):
    return pl.pallas_call(
        inner_kernel,
        out_shape=(jax.ShapeDtypeStruct((864, 128), BF),) * 2 + (jax.ShapeDtypeStruct((576, 128), BF), jax.ShapeDtypeStruct((992, 128), BF)),
        in_specs=[SM] + [VM] * 3,
        out_specs=(VM,) * 4,
        scratch_shapes=[
            pltpu.VMEM((32, 64, 128), F32),
            pltpu.VMEM((32, 64, 128), BF),
            pltpu.VMEM((4, 24, 48, 256), BF),
            pltpu.VMEM((36, 48, 128), F32),
            pltpu.VMEM((304, 128), F32),
            pltpu.VMEM((992, 128), F32),
        ],
        compiler_params=pltpu.CompilerParams(vmem_limit_bytes=24 << 20),
        cost_estimate=pl.CostEstimate(flops=1000000000, bytes_accessed=1000000, transcendentals=0),
        name="inner",
    )(t, f, s, enc)


def edge_kernel(t_ref, f_ref, s_ref, a_ref, b_ref, near_ref, far_ref, w_ref, oi_ref, ci_ref, state_ref, z_ref, o_ref, c_ref, fe, se, hal, band, acc):
    t = t_ref[0]
    odd = lax.rem(t, 2)
    for n, ref in ((1 - odd, a_ref), (odd, b_ref)):
        hal[n, 0:16] = jnp.zeros((16, 128), F32)
        hal[n, 16:400] = ref[0:384].astype(F32)
    fpad = jnp.zeros((8, 128), F32)
    for r in range(f_ref.shape[0]):
        fe[r, 0:8] = fpad
        fe[r, 24:32] = fpad
        fe[r, 8:16] = f_ref[r, 0:16].astype(F32)[0:8]
        fe[r, 16:24] = f_ref[r, 48:64].astype(F32)[8:16]
        fe[r, 6:8] = hal[0, 336 + 2 * r : 338 + 2 * r]
        fe[r, 24:26] = hal[1, 336 + 2 * r : 338 + 2 * r]
        se[r, 32:48] = mirror(s_ref[r, 0:16].astype(F32)).astype(BF)
        se[r, 48:64] = mirror(hal[0, 10 + 10 * r : 26 + 10 * r]).astype(BF)
        se[r, 0:16] = mirror(hal[1, 16 + 10 * r : 32 + 10 * r]).astype(BF)
        se[r, 16:32] = mirror(s_ref[r, 48:64].astype(F32)).astype(BF)
    correlate_groups(fe, se, w_ref, band, acc, [(0, 32), (16, 0)])

    def write(ref, base, count=18):
        rims = []
        for r in range(count):
            m = jnp.maximum(acc[base + r], 0.0)
            ref[16 * r : 16 * r + 16] = m[8:24].astype(BF)
            rims += [m[6:8], m[24:26]]
        if count % 4:
            rims.append(jnp.zeros((8, 128), F32))
        at, n = 16 * count, -(-count // 4) * 16
        ref[at : at + n] = jnp.concatenate(rims, axis=0).astype(BF)

    write(z_ref, 14 * (1 - t // 2) + 2)
    o_ref[0:864] = oi_ref[...]
    write(o_ref.at[864:1232], 14 * (t // 2) + 2)
    c_ref[0:576] = ci_ref[...]
    write(c_ref.at[576:816], 8 * (t ^ 1), 12)
    for ref, at in ((z_ref, 368), (c_ref, 816)):
        ref[at : at + 16] = near_ref[...]
        ref[at + 16 : at + 32] = far_ref[...]


def side_rows(t, a_ref, b_ref, top, bot):
    even = lax.rem(t, 2) == 0

    @pl.when(even)
    def _():
        bot[...] = a_ref[384:896].astype(F32)
        top[...] = jnp.where(t == 2, b_ref[384:896].astype(F32), 0.0)

    @pl.when(jnp.logical_not(even))
    def _():
        top[...] = a_ref[384:896].astype(F32)
        bot[...] = jnp.where(t == 1, b_ref[384:896].astype(F32), 0.0)


def edge(t, f, s, a, b, near, far, w_wide, oi, ci, state):
    return pl.pallas_call(
        edge_kernel,
        out_shape=(jax.ShapeDtypeStruct((400, 128), BF), jax.ShapeDtypeStruct((1232, 128), BF), jax.ShapeDtypeStruct((848, 128), BF)),
        in_specs=[SM] + [VM] * 10,
        out_specs=(VM,) * 3,
        scratch_shapes=[
            pltpu.VMEM((32, 32, 128), F32),
            pltpu.VMEM((32, 64, 128), BF),
            pltpu.VMEM((2, 400, 128), F32),
            pltpu.VMEM((4, 24, 32, 256), BF),
            pltpu.VMEM((36, 32, 128), F32),
        ],
        compiler_params=pltpu.CompilerParams(vmem_limit_bytes=24 << 20),
        cost_estimate=pl.CostEstimate(flops=1000000000, bytes_accessed=1000000, transcendentals=0),
        name="edge",
    )(t, f, s, a, b, near, far, w_wide, oi, ci, state)


def join_kernel(i_ref, e_ref, one_ref, o_ref):
    o_ref[0:864] = i_ref[...]
    o_ref[864:1264] = e_ref[...]


def join(zi, ze, one):
    return pl.pallas_call(
        join_kernel,
        out_shape=jax.ShapeDtypeStruct((1264, 128), BF),
        in_specs=[VM] * 3,
        out_specs=VM,
        compiler_params=pltpu.CompilerParams(vmem_limit_bytes=8 << 20),
        name="join",
    )(zi, ze, one)


def state_rows(t, a_ref, b_ref, h_ref, hs, top, bot):
    side_rows(t, a_ref, b_ref, top, bot)
    hs[0:512] = top[...]
    hs[2560:3072] = bot[...]
    for i in range(8):
        hs[512 + 256 * i : 768 + 256 * i] = h_ref[i].astype(F32)


def gate_products(x, gw_ref, width, i, lanes):
    def part(qs):
        lhs = jnp.concatenate([x[q, i + p : i + p + 2, :, lanes[0]].reshape(2 * width, -1) for q in qs for p in range(3)], axis=1)
        rhs = jnp.concatenate([gw_ref[p, q, lanes[1]] for q in qs for p in range(3)], axis=0)
        return jnp.dot(lhs, rhs, preferred_element_type=F32)

    return part((0, 2)), part((1,))


def gates(metric_ref, t, x, gw_ref, state_ref, width, put):
    for i in range(0, 10, 2):
        known = 2 <= i < 8
        half = slice(128, 256)
        sides, center = gate_products(x, gw_ref, width, i, (half, half) if known else (slice(0, 256), slice(0, 256)))
        for n in range(2):
            cut = slice(width * n, width * n + width)
            gate = center[cut] + sides[cut] * metric_ref[jnp.clip(8 * t + i + n - 1, 0, 31)]
            if known:
                gate = gate + state_ref[i + n - 2]
            put(i + n, 0.5 * jnp.tanh(0.5 * gate) + 0.5)


def state_products(metric_ref, t, x, gw_ref, width, out):
    for i in range(0, 6, 2):
        sides, center = gate_products(x, gw_ref, width, i, (slice(0, 128), slice(0, 128)))
        for n in range(2):
            cut = slice(width * n, width * n + width)
            out[i + n] = center[cut] + sides[cut] * metric_ref[8 * t + i + n + 1]


def state_first_kernel(t_ref, metric_ref, h_ref, gw_ref, out_ref, hs, x):
    t = t_ref[0]
    for i in range(8):
        hs[256 * i : 256 * i + 256] = h_ref[i].astype(F32)
    for q in range(3):
        for i in range(8):
            x[q, i] = hs[pl.ds(256 * i + 126 * (t // 2) + q, 128)].astype(BF)
    state_products(metric_ref, t, x, gw_ref, 128, out_ref)


def state_second_kernel(t_ref, l_ref, metric_ref, h_ref, near_ref, far_ref, gw_ref, out_ref, hs, hf, x):
    t = t_ref[0]
    high = t // 2
    c0 = pl.multiple_of(128 - 128 * high, 128)
    west_even = lax.rem(l_ref[0], 2) == 0
    near, far = near_ref[...].astype(F32), far_ref[...].astype(F32)
    hr = jnp.where(west_even, near, far)
    hl = jnp.where(west_even, far, near)
    for i in range(8):
        hs[256 * i : 256 * i + 256] = h_ref[i].astype(F32)
    for i in range(8):
        outer(hf, hs, i, c0, high, hl[2 * i : 2 * i + 2], hr[2 * i : 2 * i + 2])
    for q in range(3):
        for i in range(8):
            x[q, i] = hf[i, q : q + 144].astype(BF)
    state_products(metric_ref, t, x, gw_ref, 144, out_ref)


def outer(hf, hs, i, c0, high, side_w, side_e):
    low = high == 0
    hf[i, 2:130] = hs[pl.ds(256 * i + c0, 128)]
    hf[i, 0:2] = jnp.where(low, hs[256 * i + 126 : 256 * i + 128], side_w)
    hf[i, 130:132] = jnp.where(low, side_e, hs[256 * i + 128 : 256 * i + 130])
    hf[i, pl.ds(134 - 2 * high, 4)] = hs[pl.ds(256 * i + 252 * high, 4)]
    hf[i, pl.ds(132 + 4 * high, 2)] = jnp.where(low, side_w, side_e)


def state_first(t, metric, h, gw):
    return pl.pallas_call(
        state_first_kernel,
        out_shape=jax.ShapeDtypeStruct((6, 128, 256), F32),
        in_specs=[SM, SM] + [VM] * 2,
        out_specs=VM,
        scratch_shapes=[pltpu.VMEM((2048, 128), F32), pltpu.VMEM((3, 8, 128, 128), BF)],
        compiler_params=pltpu.CompilerParams(vmem_limit_bytes=24 << 20),
        cost_estimate=pl.CostEstimate(flops=10**9, bytes_accessed=2 << 20, transcendentals=0),
        name="state_first",
    )(t, metric, h, gw)


def state_second(t, l, metric, h, near, far, gw):
    return pl.pallas_call(
        state_second_kernel,
        out_shape=jax.ShapeDtypeStruct((6, 144, 256), F32),
        in_specs=[SM, SM, SM] + [VM] * 4,
        out_specs=VM,
        scratch_shapes=[pltpu.VMEM((2048, 128), F32), pltpu.VMEM((8, 152, 128), F32), pltpu.VMEM((3, 8, 144, 128), BF)],
        compiler_params=pltpu.CompilerParams(vmem_limit_bytes=24 << 20),
        cost_estimate=pl.CostEstimate(flops=10**9, bytes_accessed=2 << 20, transcendentals=0),
        name="state_second",
    )(t, l, metric, h, near, far, gw)


def candidates(metric_ref, t, x, m3s, r, cw_ref, width, put):
    zero = jnp.zeros((256, 128), BF)

    def pair(rr, q):
        first = cw_ref[rr, q] if rr < 3 else zero
        second = cw_ref[rr - 1, q] if rr > 0 else zero
        return jnp.concatenate([first, second], axis=1)

    sides_w = jnp.concatenate([pair(rr, q) for q in (0, 2) for rr in range(4)], axis=0)
    center_w = jnp.concatenate([pair(rr, 1) for rr in range(4)], axis=0)

    def taps(q, row):
        mm = m3s[row + 1] if q == 2 else x[q + 1, row + 1, 0:width, 128:256]
        return [r[q, row], mm]

    def stack(qs, i):
        one = [jnp.concatenate(sum([taps(q, i + k + rr) for q in qs for rr in range(4)], []), axis=1) for k in (0, 2)]
        return jnp.concatenate(one, axis=0)

    for i in range(0, 8, 4):
        sides = jnp.dot(stack((0, 2), i), sides_w, preferred_element_type=F32)
        center = jnp.dot(stack((1,), i), center_w, preferred_element_type=F32)
        for n in range(4):
            cut = (slice(width * (n // 2), width * (n // 2) + width), slice(128 * (n % 2), 128 * (n % 2) + 128))
            put(i + n, jnp.tanh(center[cut] + sides[cut] * metric_ref[8 * t + i + n]))


def piece_row(ref, row, inside, count):
    mid = ref[pl.ds(pl.multiple_of(48 * row, 16), 48)].astype(F32)
    ends = ref[pl.ds(pl.multiple_of(48 * count + 16 * row, 16), 16)].astype(F32)
    if inside is not None:
        mid, ends = jnp.where(inside, mid, 0.0), jnp.where(inside, ends, 0.0)
    return mid, ends


def first_kernel(t_ref, metric_ref, h_ref, a_ref, b_ref, own_ref, mate_ref, state_ref, gw_ref, cw_ref, out_ref, hs, mf, x, m3s, rf, r, ug, top, bot, rims):
    t = t_ref[0]
    high = t // 2
    state_rows(t, a_ref, b_ref, h_ref, hs, top, bot)
    start = 8 * t - 2 - 14 * high
    odd = lax.rem(t, 2)
    for s, ref, count in ((odd, own_ref, 18), (1 - odd, mate_ref, 12)):
        rims[0:80] = ref[1152:1232].astype(F32) if count == 18 else jnp.pad(ref[768:816].astype(F32), ((0, 32), (0, 0)))
        for i in range(12):
            row, inside = i, None
            if count == 18:
                row = start + i
                inside = (row >= 0) & (row < 18)
                row = jnp.clip(row, 0, 17)
            mid, ends = piece_row(ref, row, inside, count)
            at = 64 * s + 16 * high
            mf[i, pl.ds(at + 8, 48)] = mid
            mf[i, pl.ds(at, 8)] = ends[0:8]
            mf[i, pl.ds(at + 56, 8)] = ends[8:16]

            @pl.when(s != high)
            def _(i=i, row=row, s=s, inside=inside):
                v = rims[pl.ds(4 * row + 2 * s, 2)]
                mf[i, pl.ds(128 - 114 * high, 2)] = v if inside is None else jnp.where(inside, v, 0.0)

    for q in range(3):
        for i in range(12):
            if not 4 <= i < 8:
                x[q, i, :, 0:128] = hs[pl.ds(256 * i + 126 * high + q, 128)].astype(BF)
            x[q, i, :, 128:256] = mf[i, pl.ds(14 * high + q, 128)].astype(BF)
    for i in range(12):
        m3s[i] = mf[i, pl.ds(14 * high + 3, 128)].astype(BF)

    def put_gate(i, gate):
        rf[i, 0:128] = gate[:, 128:] * hs[pl.ds(256 * (i + 1) + 126 * high + 1, 128)]
        if 1 <= i < 9:
            ug[i - 1, 0:128] = gate[:, 0:128]

    gates(metric_ref, t, x, gw_ref, state_ref, 128, put_gate)
    for q in range(3):
        for i in range(10):
            r[q, i] = rf[i, q : q + 128].astype(BF)

    def put_new(i, cand):
        u = ug[i, 1:129]
        h = hs[pl.ds(256 * (i + 2) + 126 * high + 2, 128)]
        out_ref[i] = ((1.0 - u) * h + u * cand).astype(BF)

    candidates(metric_ref, t, x, m3s, r, cw_ref, 128, put_new)


def first_part(t, metric, h, a, b, own, mate, state, gw, cw):
    return pl.pallas_call(
        first_kernel,
        out_shape=(jax.ShapeDtypeStruct((8, 128, 128), BF), pltpu.VMEM((3072, 128), F32)),
        in_specs=[SM, SM] + [VM] * 8,
        out_specs=(VM, VM),
        scratch_shapes=[
            pltpu.VMEM((12, 152, 128), F32),
            pltpu.VMEM((3, 12, 128, 256), BF),
            pltpu.VMEM((12, 128, 128), BF),
            pltpu.VMEM((10, 136, 128), F32),
            pltpu.VMEM((3, 10, 128, 128), BF),
            pltpu.VMEM((8, 136, 128), F32),
            pltpu.VMEM((512, 128), F32),
            pltpu.VMEM((512, 128), F32),
            pltpu.VMEM((80, 128), F32),
        ],
        compiler_params=pltpu.CompilerParams(vmem_limit_bytes=24 << 20),
        cost_estimate=pl.CostEstimate(flops=10**7, bytes_accessed=10**5, transcendentals=0),
        name="first_part",
    )(t, metric, h, a, b, own, mate, state, gw, cw)


def second_kernel(
    t_ref, l_ref, metric_ref, hs, near_ref, far_ref, own_ref, mate_ref, z_ref, k_ref, state_ref, gw_ref, cw_ref, one_ref, out_ref,
    ob, ow, sem, hf, mf, x, m3s, rf, r, ug, rims,
):
    t = t_ref[0]
    high = t // 2
    c0 = pl.multiple_of(128 - 128 * high, 128)
    west_even = lax.rem(l_ref[0], 2) == 0
    odd = lax.rem(t, 2)
    low = high == 0

    def twelve(own, at):
        mates, others = mate_ref[816 + at : 832 + at].astype(F32), k_ref[1232 + at : 1248 + at].astype(F32)
        others = jnp.where((t == 1) | (t == 2), others, 0.0)
        above = jnp.where(odd == 1, mates, others)[12:16]
        below = jnp.where(odd == 1, others, mates)[0:4]
        return jnp.concatenate([above, own[...].astype(F32), below], axis=0)

    near, far = twelve(near_ref, 0), twelve(far_ref, 16)
    hr = jnp.where(west_even, near, far)
    hl = jnp.where(west_even, far, near)
    for i in range(12):
        outer(hf, hs, i, c0, high, hl[2 * i : 2 * i + 2], hr[2 * i : 2 * i + 2])
    start = 8 * t - 2 - 14 * high
    for s, ref in ((odd, z_ref), (1 - odd, k_ref)):
        rims[0:80] = ref[1152:1232].astype(F32)
        for i in range(12):
            row = start + i
            inside = (row >= 0) & (row < 18)
            row = jnp.clip(row, 0, 17)
            mid = ref[pl.ds(pl.multiple_of(48 * row, 16), 48)].astype(F32)
            ends = ref[pl.ds(pl.multiple_of(864 + 16 * row, 16), 16)].astype(F32)
            mf[i, pl.ds(10 + 64 * s, 48)] = jnp.where(inside, mid, 0.0)
            ends = jnp.where(inside, ends, 0.0)
            mf[i, pl.ds(2 + 64 * s, 8)] = ends[0:8]
            mf[i, pl.ds(58 + 64 * s, 8)] = ends[8:16]
            v = rims[pl.ds(4 * row + 2 * s, 2)]
            mf[i, pl.ds(130 * s, 2)] = jnp.where(inside, v, 0.0)
    mine = odd == high
    mates = jnp.pad(mate_ref[768:816].astype(F32), ((0, 32), (0, 0)))
    rims[0:80] = jnp.where(mine, own_ref[1152:1232].astype(F32), mates)
    for i in range(12):
        row = start + i
        inside = (row >= 0) & (row < 18)
        row = jnp.clip(row, 0, 17)
        at = pl.multiple_of(864 + 16 * row, 16)
        ends = jnp.where(inside, own_ref[pl.ds(at, 16)].astype(F32), 0.0)
        ends = jnp.where(mine, ends, mate_ref[576 + 16 * i : 592 + 16 * i].astype(F32))
        mf[i, pl.ds(134 - 2 * high, 4)] = jnp.where(low, ends[0:4], ends[12:16])
        row = jnp.where(mine, row, i)
        inside = inside | jnp.logical_not(mine)
        v = rims[pl.ds(4 * row + 2 * high, 2)]
        mf[i, pl.ds(132 + 4 * high, 2)] = jnp.where(inside, v, 0.0)
    for q in range(3):
        for i in range(12):
            if not 4 <= i < 8:
                x[q, i, :, 0:128] = hf[i, q : q + 144].astype(BF)
            x[q, i, :, 128:256] = mf[i, q : q + 144].astype(BF)
    for i in range(12):
        m3s[i] = mf[i, 3:147].astype(BF)

    def put_gate(i, gate):
        rf[i, 0:144] = gate[:, 128:] * hf[i + 1, 1:145]
        if 1 <= i < 9:
            ug[i - 1, 0:144] = gate[:, 0:128]

    gates(metric_ref, t, x, gw_ref, state_ref, 144, put_gate)
    for q in range(3):
        for i in range(10):
            r[q, i] = rf[i, q : q + 144].astype(BF)

    def put_new(i, cand):
        u = ug[i, 1:145]
        h = hf[i + 2, 2:146]
        new = (1.0 - u) * h + u * cand
        ob[i, pl.ds(c0, 128)] = new[0:128].astype(BF)
        ow[i, pl.ds(2 - 2 * high, 126)] = one_ref[i].astype(F32)[0:126]
        ow[i, pl.ds(126 * high, 2)] = new[132:134]
        ob[i, pl.ds(pl.multiple_of(128 - c0, 128), 128)] = ow[i].astype(BF)
        pltpu.make_async_copy(ob.at[i], out_ref.at[i], sem.at[i]).start()

    candidates(metric_ref, t, x, m3s, r, cw_ref, 144, put_new)
    for i in range(8):
        pltpu.make_async_copy(ob.at[i], out_ref.at[i], sem.at[i]).wait()


def second_part(t, l, metric, hs, near, far, own, mate, z, k, state, gw, cw, one):
    return pl.pallas_call(
        second_kernel,
        out_shape=jax.ShapeDtypeStruct((8, 256, 128), BF),
        in_specs=[SM, SM, SM] + [VM] * 11,
        out_specs=pl.BlockSpec(memory_space=pl.ANY),
        scratch_shapes=[
            pltpu.VMEM((8, 256, 128), BF),
            pltpu.VMEM((8, 128, 128), F32),
            pltpu.SemaphoreType.DMA((8,)),
            pltpu.VMEM((12, 152, 128), F32),
            pltpu.VMEM((12, 152, 128), F32),
            pltpu.VMEM((3, 12, 144, 256), BF),
            pltpu.VMEM((12, 144, 128), BF),
            pltpu.VMEM((10, 152, 128), F32),
            pltpu.VMEM((3, 10, 144, 128), BF),
            pltpu.VMEM((8, 152, 128), F32),
            pltpu.VMEM((80, 128), F32),
        ],
        compiler_params=pltpu.CompilerParams(vmem_limit_bytes=24 << 20),
        cost_estimate=pl.CostEstimate(flops=5000000000, bytes_accessed=4000000, transcendentals=0),
        name="second_part",
    )(t, l, metric, hs, near, far, own, mate, z, k, state, gw, cw, one)


def swaps(n, first):
    pairs = [(i % n, (i + 1) % n) for i in range(first, n, 2)]
    return pairs + [(j, i) for i, j in pairs]


def body(first, second, hidden, encoder_weight, gates_weight, candidate_weight, row_metric):
    t = lax.axis_index("lat").astype(jnp.int32)[None]
    l = lax.axis_index("lon").astype(jnp.int32)[None]
    count = lax.axis_size("lon")
    slabs = count * lax.axis_size("lat")
    core = [(i, i ^ 1) for i in range(4)]
    chip = [(i, i ^ 2) for i in range(4)]

    a_send, b_send, near_send, far_send = pack(t, l, first, second, hidden)
    with jax.named_scope("rim_far"):
        b = lax.ppermute(b_send, BOTH, swaps(slabs, 1))
    with jax.named_scope("rim_near"):
        a = lax.ppermute(a_send, BOTH, swaps(slabs, 0))
    with jax.named_scope("state_near"):
        near = lax.ppermute(near_send, "lon", swaps(count, 0))
    with jax.named_scope("state_far"):
        far = lax.ppermute(far_send, "lon", swaps(count, 1))
    zi_send, oi, ci, w_wide = inner(t, first, second, encoder_weight)
    with jax.named_scope("inner_chip"):
        zi = lax.ppermute(zi_send, "lat", chip)
    state_one = state_first(t, row_metric, hidden, gates_weight)
    state_two = state_second(t, l, row_metric, hidden, near, far, gates_weight)
    ze_send, own, own_send = edge(t, first, second, a, b, near, far, w_wide, oi, ci, state_one)
    with jax.named_scope("edge_chip"):
        ze = lax.ppermute(ze_send, "lat", chip)
    with jax.named_scope("own_core"):
        mate = lax.ppermute(own_send, "lat", core)
    one, laid = first_part(t, row_metric, hidden, a, b, own, mate, state_one, gates_weight, candidate_weight)
    z = join(zi, ze, one)
    with jax.named_scope("chip_core"):
        k = lax.ppermute(z, "lat", core)
    return second_part(t, l, row_metric, laid, near, far, own, mate, z, k, state_two, gates_weight, candidate_weight, one)


def solution(mesh):
    return jax.shard_map(
        body,
        mesh=mesh,
        in_specs=(
            P(None, BOTH, None),
            P(None, BOTH, None),
            P("lat", "lon", None),
            P(),
            P(),
            P(),
            P(),
        ),
        out_specs=P("lat", "lon", None),
        check_vma=False,
    )
```
